32 devices in a mesh: ep: 32 (over z, y, x, core).
Axes of the slice: x: 2, y: 2, z: 4, core: 2. Of those that a mesh axis runs over, the one named last changes fastest.
Arguments:
- x_in: float32 [6144, 768], P('ep'), may hold values from -6 to 6
- cotangent: float32 [6144, 768], P('ep'), may hold values from -6 to 6
- attn_gain: bfloat16 [2, 768], P(None, 'ep'), may hold values from 0.5 to 1.5
- w_qkv: bfloat16 [2, 768, 2304], P(None, 'ep'), may hold values from -0.21875 to 0.21875
- w_out: bfloat16 [2, 768, 768], P(None, 'ep'), may hold values from -1.75 to 1.75
- moe_gain: bfloat16 [2, 768], P(None, 'ep'), may hold values from 0.5 to 1.5
- w_router: float32 [2, 768, 12], replicated, may hold values from -0.15625 to 0.15625
- w_carry: float32 [12, 12], replicated, may hold values from -1.8 to 1.8
- const_gate: float32 [2, 2, 2, 768], replicated, may hold values from -0.21875 to 0.21875
- const_value: float32 [2, 2, 768], replicated, may hold values from -6 to 6
- exp_gate: bfloat16 [2, 32, 768, 512], P(None, 'ep'), may hold values from -0.21875 to 0.21875
- exp_up: bfloat16 [2, 32, 768, 512], P(None, 'ep'), may hold values from -0.21875 to 0.21875
- exp_down: bfloat16 [2, 32, 512, 768], P(None, 'ep'), may hold values from -0.25 to 0.25
- routes: int32 [2, 6144, 2], P(None, 'ep'), may hold values from 0 to 11, all different within a row
- drop_order: int32 [32, 192], P('ep'), may hold values from 0 to 191, each once within a row
- image_start: int32 [32], P('ep'), may hold values from 0 to 64
Outputs:
- hidden_out: float32 [6144, 768], P('ep')
- input_grad: float32 [6144, 768], P('ep')
- grad_attn_gain: float32 [2, 768], P(None, 'ep')
- grad_qkv: float32 [2, 768, 2304], P(None, 'ep')
- grad_out: float32 [2, 768, 768], P(None, 'ep')
- grad_moe_gain: float32 [2, 768], P(None, 'ep')
- grad_router: float32 [2, 768, 12], replicated
- grad_carry: float32 [12, 12], replicated
- grad_const_gate: float32 [2, 2, 2, 768], replicated
- grad_const_value: float32 [2, 2, 768], replicated
- grad_exp_gate: float32 [2, 32, 768, 512], P(None, 'ep')
- grad_exp_up: float32 [2, 32, 768, 512], P(None, 'ep')
- grad_exp_down: float32 [2, 32, 512, 768], P(None, 'ep')
The draws below stay inside these ranges and needn't reach their ends.
Inputs may be any that keep to these rules, and one draw needn't show every extreme that they name: `routes`: each row of a layer names two different experts. `drop_order`: each row is a permutation of the positions of one sequence; the smaller number takes an expert slot first.
All inputs are finite; a program needn't handle non-finite values.
Results may differ from the reference program's by a relative error of at most 0.022.
Values may be sent and summed in bfloat16 or wider, within the bound.
No kernel may reach another device: no remote copies, remote signals or barrier semaphores. Data moves between devices by JAX's collectives and lax.ppermute only.
A program may use at most 192 MiB of HBM per device.

```python
import jax
import jax.numpy as jnp
from jax import lax

D = 768
H = 12
HD = 64
FF = 2048
E = 8
NR = 12
NC = 2
LAYERS = 2
TOK_DEV = 192
HOLD = 4
SPAN = 128
CAP = 40
COPIES = 1
FF_HOLD = 512
FF_DEV = 512
TOKENS = 6144
SEQS = 32
N_EP = 32


def place_ends(values, rng, least, high):
    longest = values.shape.index(max(values.shape))
    spots = []
    for shift in (0, 1):
        where = [jax.random.randint(jax.random.fold_in(rng, axis), (), 0, length) for axis, length in enumerate(values.shape)]
        where[longest] = (where[longest] + shift) % values.shape[longest]
        spots.append(tuple(where))
    return values.at[spots[0]].set(least).at[spots[1]].set(high)


def raised(result, own_key, source, target, shards_of, factor):
    def block_of(dim):
        return (jnp.arange(result.shape[dim]) // (result.shape[dim] // shards_of)).reshape((-1,) + (1,) * (result.ndim - 1 - dim))

    one_side = jax.random.permutation(own_key, shards_of)[block_of(target)]
    far = (block_of(target) + shards_of // 2) % shards_of
    return jnp.where((block_of(source) == one_side) | (block_of(source) == far), factor * result, result)


def block_levels(key, dims, cuts, smallest, largest):
    def one(dim, parts):
        steps = jax.random.uniform(jax.random.fold_in(jax.random.fold_in(key, 6), dim), (parts,), jnp.float32, smallest / len(cuts), largest / len(cuts))
        return jnp.repeat(jnp.exp(steps), dims[dim] // parts).reshape((-1,) + (1,) * (len(dims) - dim - 1))

    level = one(*cuts[0])
    for cut in cuts[1:]:
        level = level * one(*cut)
    return level


def different_ones(stream_key, rows, number_of, top, lift):
    order = jax.random.permutation(jax.random.fold_in(stream_key, 1), number_of)
    boost = order
    for power in range(3):
        boost = boost * boost // number_of
    boost = boost * lift // number_of
    lots = jax.random.randint(jax.random.fold_in(stream_key, 2), (rows, number_of), 0, 4096) + boost
    sure = jax.random.permutation(jax.random.fold_in(stream_key, 3), rows)[jnp.arange(number_of) % rows]
    lots = jnp.where(jnp.arange(rows)[:, None] == sure[None, :], 1 << 14, lots)
    merit = lots * number_of + jnp.arange(number_of)
    return lax.top_k(merit.astype(jnp.int32), top)[1].astype(jnp.int32)


def normal_values(stream_key, dims, scale, most, split=(), kind=jnp.bfloat16):
    drawn = scale * jax.random.normal(stream_key, dims, jnp.float32)
    if split:
        drawn = drawn * block_levels(stream_key, dims, split, -0.22, 0.18)
    return jnp.clip(drawn, -most, most).astype(kind)


def noise_with(own_key, shape, scale, most, shards, heavy, kind=jnp.bfloat16):
    array = scale * jax.random.normal(own_key, shape, jnp.float32)
    if shards:
        array = array * block_levels(own_key, shape, shards, -0.22, 0.18)
    return jnp.clip(raised(array, jax.random.fold_in(own_key, 3), *heavy), -most, most).astype(kind)


def setup_inputs(seed: int = 0) -> dict:
    splits = jax.random.split(jax.random.key(seed), 17)
    return {
        "x_in": noise_with(splits[0], (TOKENS, D), 1.0, 6.0, ((0, 32),), (0, 1, 32, 2.75), jnp.float32),
        "cotangent": normal_values(splits[1], (TOKENS, D), 1.0, 6.0, ((0, 32),), jnp.float32),
        "attn_gain": jnp.clip(1.0 + 0.1 * jax.random.normal(splits[2], (LAYERS, D), jnp.float32), 0.5, 1.5).astype(jnp.bfloat16),
        "w_qkv": normal_values(splits[3], (LAYERS, D, 3 * D), D ** -0.5, 0.21875, ((1, 32),)),
        "w_out": normal_values(splits[4], (LAYERS, D, D), (D // 64) ** -0.5, 1.75, ((1, 32),)),
        "moe_gain": jnp.clip(1.0 + 0.1 * jax.random.normal(splits[5], (LAYERS, D), jnp.float32), 0.5, 1.5).astype(jnp.bfloat16),
        "w_router": normal_values(splits[6], (LAYERS, D, NR), (2 * D) ** -0.5, 0.15625, (), jnp.float32),
        "w_carry": normal_values(splits[7], (NR, NR), 0.3, 1.8, (), jnp.float32),
        "const_gate": normal_values(splits[8], (LAYERS, NC, 2, D), D ** -0.5, 0.21875, (), jnp.float32),
        "const_value": normal_values(splits[9], (LAYERS, NC, D), 1.0, 6.0, (), jnp.float32),
        "exp_gate": normal_values(splits[10], (LAYERS, N_EP, D, FF_DEV), D ** -0.5, 0.21875, ((1, 32),)),
        "exp_up": normal_values(splits[11], (LAYERS, N_EP, D, FF_DEV), D ** -0.5, 0.21875, ((1, 32),)),
        "exp_down": normal_values(splits[12], (LAYERS, N_EP, FF_DEV, D), (FF // 4) ** -0.5, 0.25, ((1, 32),)),
        "routes": different_ones(splits[13], LAYERS * TOKENS, NR, 2, 1365).reshape((LAYERS, TOKENS, 2)),
        "drop_order": jax.vmap(lambda own: jax.random.permutation(own, TOK_DEV))(jax.random.split(splits[14], SEQS)).reshape((SEQS, TOK_DEV)).astype(jnp.int32),
        "image_start": place_ends(jax.random.randint(splits[15], (SEQS,), 0, TOK_DEV - SPAN + 1), jax.random.fold_in(splits[15], 1), 0, TOK_DEV - SPAN).astype(jnp.int32),
    }


TOP_PRECISION = lax.Precision.HIGHEST
EPSILON = 1e-06

@jax.custom_vjp
def low(v):
    return lax.optimization_barrier(v.astype(jnp.bfloat16)).astype(jnp.float32)

@jax.custom_vjp
def low_back(v):
    return v

def low_keep(v):
    return (low(v), None)

def low_pass(kept, grad):
    return (grad,)

def back_keep(v):
    return (v, None)

def back_low(kept, grad):
    return (low(grad),)
low.defvjp(low_keep, low_pass)
low_back.defvjp(back_keep, back_low)

def norm_rows(values, gain):
    return values * lax.rsqrt(lax.optimization_barrier(jnp.mean(values * values, -1, keepdims=True)) + EPSILON) * gain

def rope_tables(length):
    position = jnp.arange(length).astype(jnp.float32)
    inverse = 10000.0 ** (-jnp.arange(HD // 2).astype(jnp.float32) * 2.0 / HD)
    angles = position[:, None] * inverse[None, :]
    return (jnp.cos(angles)[:, None, :], jnp.sin(angles)[:, None, :])

def rotate(values, cosine_table, sine_table):
    half_width = values.shape[-1] // 2
    first_half = values[..., :half_width]
    second_half = values[..., half_width:]
    return jnp.concatenate([first_half * cosine_table - second_half * sine_table, second_half * cosine_table + first_half * sine_table], -1)

def span_mask(length, span_start):
    query_pos = jnp.arange(length, dtype=jnp.int32)[:, None]
    key_pos = jnp.arange(length, dtype=jnp.int32)[None, :]
    inside_query = (query_pos >= span_start) & (query_pos < span_start + SPAN)
    inside_key = (key_pos >= span_start) & (key_pos < span_start + SPAN)
    return (key_pos <= query_pos) | inside_query & inside_key

def slot_table(routing, priority):
    expert_ids = jnp.arange(E, dtype=jnp.int32)
    wanted = jnp.any(routing[:, :, None] == expert_ids[None, None, :], 1).astype(jnp.int32)
    earlier = (priority[None, :] < priority[:, None]).astype(jnp.int32)
    counts = lax.optimization_barrier(jnp.sum(earlier[:, :, None] * wanted[None, :, :], 1)).astype(jnp.int32)
    rank_of = jnp.take_along_axis(counts, jnp.clip(routing, 0, E - 1), axis=1)
    is_kept = (routing < E) & (rank_of < CAP)
    target = jnp.where(is_kept, routing * CAP + rank_of, -1).astype(jnp.int32)
    return (target, is_kept)

def expert_index(routing, drop_order):
    target, is_kept = jax.vmap(slot_table)(routing.reshape(SEQS, TOK_DEV, 2), drop_order)
    device_ids = jnp.arange(SEQS, dtype=jnp.int32)[:, None, None]
    expert_ids = jnp.maximum(target, 0) // CAP
    rank_of = jnp.maximum(target, 0) % CAP
    place_of = jnp.where(is_kept, expert_ids * (SEQS * CAP) + device_ids * CAP + rank_of, E * SEQS * CAP).astype(jnp.int32)
    token_ids = jnp.broadcast_to(jnp.arange(TOKENS, dtype=jnp.int32).reshape(SEQS, TOK_DEV, 1), place_of.shape)
    row_table = jnp.full((E * SEQS * CAP + 1,), TOKENS, jnp.int32).at[place_of.reshape(-1)].set(token_ids.reshape(-1))
    return (place_of.reshape(TOKENS, 2), row_table[:E * SEQS * CAP])

def mixture(normed, logits, picked, cgate, cvalue, routing):
    chosen = jnp.take_along_axis(logits, routing, axis=1)
    gate_values = jax.nn.softmax(chosen, -1)
    blending = jax.nn.softmax(jnp.einsum('td,cjd->tcj', normed, cgate, precision=TOP_PRECISION), -1)
    constant = blending[:, :, 0:1] * normed[:, None, :] + blending[:, :, 1:2] * cvalue[None, :, :]
    summed = jnp.zeros_like(normed)
    for column in range(2):
        expert_id = routing[:, column][:, None]
        branch = jnp.where(expert_id < E, picked[:, column], 0.0)
        branch = branch + jnp.where(expert_id == E + 1, normed, 0.0)
        for member in range(NC):
            branch = branch + jnp.where(expert_id == E + 2 + member, constant[:, member], 0.0)
        summed = summed + gate_values[:, column][:, None] * branch
    return summed

def attend_one(packed):
    queries, key_rows, values, span_start = packed
    allowed = span_mask(TOK_DEV, span_start)
    scores = jnp.einsum('qhd,khd->hqk', queries, key_rows, precision=TOP_PRECISION) * HD ** (-0.5)
    scores = low_back(jnp.where(allowed[None], scores, -1e+30))
    attention = low(jax.nn.softmax(scores, -1))
    return jnp.einsum('hqk,khd->qhd', attention, values, precision=TOP_PRECISION)

def expert_apply(packed):
    routed_rows, gate_weight, up_weight, down_weight = packed
    spread = low_back(jnp.broadcast_to(routed_rows[None], (gate_weight.shape[0],) + routed_rows.shape))
    gate_pre = low_back(jnp.einsum('srd,sdf->srf', spread, gate_weight, precision=TOP_PRECISION))
    up_pre = low_back(jnp.einsum('srd,sdf->srf', spread, up_weight, precision=TOP_PRECISION))
    hidden = low(jax.nn.silu(gate_pre) * up_pre)
    shares = low(jnp.einsum('srf,sfd->srd', hidden, down_weight, precision=TOP_PRECISION))
    return low_back(lax.optimization_barrier(jnp.sum(shares, 0)))

def reference(x_in, cotangent, attn_gain, w_qkv, w_out, moe_gain, w_router, w_carry, const_gate, const_value, exp_gate, exp_up, exp_down, routes, drop_order, image_start):
    places = []
    tables = []
    for layer_at in range(LAYERS):
        place_of, row_table = expert_index(routes[layer_at], drop_order)
        places.append(place_of)
        tables.append(row_table)
    cosine_table, sine_table = rope_tables(TOK_DEV)

    def forward(stream, attn_scale, qkv_all, out_all, moe_scale, router_all, carry_weight, cgate_all, cvalue_all, gate_all, up_all, down_all):
        previous = None
        for layer_at in range(LAYERS):
            normed = norm_rows(stream, attn_scale[layer_at])
            packed = low_back(jnp.dot(low(normed), qkv_all[layer_at], precision=TOP_PRECISION))
            packed = packed.reshape(SEQS, TOK_DEV, 3, H, HD)
            queries = low(rotate(packed[:, :, 0], cosine_table, sine_table))
            key_rows = low(rotate(packed[:, :, 1], cosine_table, sine_table))
            values = low(packed[:, :, 2])
            attended = lax.map(jax.checkpoint(attend_one), (queries, key_rows, values, image_start))
            attended = attended.reshape(TOKENS, D)
            middle = stream + low_back(jnp.dot(low(low_back(attended)), out_all[layer_at], precision=TOP_PRECISION))
            mixed_in = norm_rows(middle, moe_scale[layer_at])
            logits = jnp.dot(mixed_in, router_all[layer_at], precision=TOP_PRECISION)
            if layer_at > 0:
                logits = logits + jnp.dot(previous, carry_weight, precision=TOP_PRECISION)
            padded = jnp.concatenate([low(mixed_in), jnp.zeros((1, D), jnp.float32)], 0)
            routed_rows = padded[tables[layer_at]].reshape(E, SEQS * CAP, D)
            gate_weight = gate_all[layer_at].reshape(COPIES, HOLD, E, D, FF_DEV).transpose(2, 1, 3, 0, 4)
            gate_weight = gate_weight.reshape(E, HOLD, D, FF_HOLD)
            up_weight = up_all[layer_at].reshape(COPIES, HOLD, E, D, FF_DEV).transpose(2, 1, 3, 0, 4)
            up_weight = up_weight.reshape(E, HOLD, D, FF_HOLD)
            down_weight = down_all[layer_at].reshape(COPIES, HOLD, E, FF_DEV, D).transpose(2, 1, 0, 3, 4)
            down_weight = down_weight.reshape(E, HOLD, FF_HOLD, D)
            outputs = lax.map(jax.checkpoint(expert_apply), (routed_rows, gate_weight, up_weight, down_weight))
            outputs = jnp.concatenate([outputs.reshape(E * SEQS * CAP, D), jnp.zeros((1, D), jnp.float32)], 0)
            picked = outputs[places[layer_at]]
            stream = middle + mixture(mixed_in, logits, picked, cgate_all[layer_at], cvalue_all[layer_at], routes[layer_at])
            previous = logits
        return stream
    floats = (x_in.astype(jnp.float32), attn_gain.astype(jnp.float32), w_qkv.astype(jnp.float32), w_out.astype(jnp.float32), moe_gain.astype(jnp.float32), w_router.astype(jnp.float32), w_carry.astype(jnp.float32), const_gate.astype(jnp.float32), const_value.astype(jnp.float32), exp_gate.astype(jnp.float32), exp_up.astype(jnp.float32), exp_down.astype(jnp.float32))
    hidden_out, pull_back = jax.vjp(forward, *floats)
    gradients = pull_back(cotangent.astype(jnp.float32))
    return (hidden_out, gradients[0], gradients[1], gradients[2], gradients[3], gradients[4], gradients[5], gradients[6], gradients[7], gradients[8], gradients[9], gradients[10], gradients[11])
```

```python
from functools import partial

import jax
import jax.numpy as jnp
import numpy as np
from jax import lax
from jax.experimental import pallas as pl
from jax.experimental.pallas import tpu as pltpu
from jax.sharding import PartitionSpec as P

H = 12
HD = 64
E = 8
NC = 2
LAYERS = 2
SPAN = 128
CAP = 40
SLOTS = E * CAP
ZW = 16

EPSILON = 1e-06
NEGATIVE = -1e30
F32 = jnp.float32
BF16 = jnp.bfloat16
TOP = lax.Precision.HIGHEST
VMEM_LIMIT = 50 * 1024 * 1024


def whole(space=pltpu.VMEM):
    return pl.BlockSpec(memory_space=space)


def shaped(shape, dtype):
    return jax.ShapeDtypeStruct(shape, dtype)


def params():
    return pltpu.CompilerParams(vmem_limit_bytes=VMEM_LIMIT)


def dot(a, b, dims=((1,), (0,)), precision=None):
    return lax.dot_general(a, b, (dims, ((), ())), precision=precision, preferred_element_type=F32)


ROWS_BY_ROWS = ((1,), (1,))
COLS_BY_COLS = ((0,), (0,))


def spread_matrix(order):
    feature = lax.broadcasted_iota(jnp.int32, (order.shape[1], order.shape[1]), 0)
    return (feature == order).astype(F32).astype(BF16)


def reorder(values, places):
    return values if places is None else dot(values, places).astype(BF16)


def restore(values, places):
    if places is None:
        return values
    if values.dtype == BF16:
        return dot(values, places, ROWS_BY_ROWS).astype(BF16)
    high = values.astype(BF16)
    rest = values - high.astype(F32)
    middle = rest.astype(BF16)
    low = (rest - middle.astype(F32)).astype(BF16)
    return dot(high, places, ROWS_BY_ROWS) + (dot(middle, places, ROWS_BY_ROWS) + dot(low, places, ROWS_BY_ROWS))


def through(values, blocks, columns):
    rows = blocks[0].shape[0]
    return sum(dot(values[:, i * rows : (i + 1) * rows], block[:, columns]) for i, block in enumerate(blocks))


def through_back(grads, blocks, columns):
    return jnp.concatenate([dot(grads, block[:, columns], ROWS_BY_ROWS) for block in blocks], 1)


def rope_tables(length):
    position = np.arange(length).astype(np.float32)
    inverse = (10000.0 ** (-np.arange(HD // 2).astype(np.float32) * 2.0 / HD)).astype(np.float32)
    angles = (position[:, None] * inverse[None, :]).astype(np.float32)
    cosine, sine = np.cos(angles), np.sin(angles)
    return (
        np.concatenate([cosine] * 4, 1).astype(np.float32),
        np.concatenate([-sine, sine, -sine, sine], 1).astype(np.float32),
    )


def swap_halves(values):
    lane = lax.broadcasted_iota(jnp.int32, values.shape, 1)
    low = lane % HD < HD // 2
    return jnp.where(low, pltpu.roll(values, 128 - HD // 2, 1), pltpu.roll(values, HD // 2, 1))


def span_mask(length, start):
    query = lax.broadcasted_iota(jnp.int32, (length, length), 0)
    key = lax.broadcasted_iota(jnp.int32, (length, length), 1)
    in_query = (query >= start) & (query < start + SPAN)
    in_key = (key >= start) & (key < start + SPAN)
    return (key <= query) | (in_query & in_key)


def head_masks(length):
    lane = lax.broadcasted_iota(jnp.int32, (length, 2 * HD), 1)
    return (lane < HD, lane >= HD)


def row_mean(values):
    return jnp.mean(values, -1, keepdims=True)


def row_sum(values):
    return jnp.sum(values, -1, keepdims=True)


def slot_matrix(target_row):
    slot = lax.broadcasted_iota(jnp.int32, (SLOTS, target_row.shape[1]), 0)
    return slot == target_row


def pick_matrix(target_col):
    slot = lax.broadcasted_iota(jnp.int32, (target_col.shape[0], SLOTS), 1)
    return slot == target_col


def gate_pair(logits, first, second):
    lane = lax.broadcasted_iota(jnp.int32, logits.shape, 1)
    one = row_sum(jnp.where(lane == first, logits, 0.0))
    two = row_sum(jnp.where(lane == second, logits, 0.0))
    return soft_pair(one, two)


def soft_pair(one, two):
    top = jnp.maximum(one, two)
    one, two = jnp.exp(one - top), jnp.exp(two - top)
    total = one + two
    return one / total, two / total


def blend_pairs(logits):
    base = ZW - 2 * NC
    return [
        soft_pair(logits[:, base + 2 * c : base + 2 * c + 1], logits[:, base + 2 * c + 1 : base + 2 * c + 2])
        for c in range(NC)
    ]


def chosen_weight(gates, routes, expert):
    return sum(jnp.where(route == expert, gate, 0.0) for gate, route in zip(gates, routes))


def mix_weights(gates, routes, blends):
    of_u = chosen_weight(gates, routes, E + 1)
    of_const = []
    for c in range(NC):
        weight = chosen_weight(gates, routes, E + 2 + c)
        of_u = of_u + weight * blends[c][0]
        of_const.append(weight * blends[c][1])
    return of_u, of_const


def prep_kernel(routes_row, routes_col, order_row, order_col, cot, target_row, target_col, cot_slots):
    tokens = order_row.shape[1]
    earlier = jnp.where(order_row[...] < order_col[...], 1.0, 0.0).astype(BF16)
    later = jnp.where(order_col[...] < order_row[...], 1.0, 0.0).astype(BF16)
    lane = lax.broadcasted_iota(jnp.int32, (tokens, 128), 1)
    sub = lax.broadcasted_iota(jnp.int32, (16, tokens), 0)
    for layer in range(LAYERS):
        cols = [routes_col[:, 2 * layer + k : 2 * layer + k + 1] for k in range(2)]
        rows = [routes_row[2 * layer + k : 2 * layer + k + 1, :] for k in range(2)]
        wanted = jnp.where((lane == cols[0]) | (lane == cols[1]), 1.0, 0.0).astype(BF16)
        counts = dot(earlier, wanted)
        wanted_t = jnp.where((sub == rows[0]) | (sub == rows[1]), 1.0, 0.0).astype(BF16)
        counts_t = dot(wanted_t, later)
        for k in range(2):
            rank = row_sum(jnp.where(lane == cols[k], counts, 0.0)).astype(jnp.int32)
            kept = (cols[k] < E) & (rank < CAP)
            target_col[:, 2 * layer + k : 2 * layer + k + 1] = jnp.where(kept, cols[k] * CAP + rank, -1)
            rank_t = jnp.sum(jnp.where(sub == rows[k], counts_t, 0.0), 0, keepdims=True).astype(jnp.int32)
            kept_t = (rows[k] < E) & (rank_t < CAP)
            target_row[2 * layer + k : 2 * layer + k + 1, :] = jnp.where(kept_t, rows[k] * CAP + rank_t, -1)
    last = 2 * (LAYERS - 1)
    spread = slot_matrix(target_row[last : last + 1, :]) | slot_matrix(target_row[last + 1 : last + 2, :])
    rows = dot(spread.astype(F32).astype(BF16), cot[...].astype(BF16)).astype(BF16)
    for holder in range(cot_slots.shape[0]):
        cot_slots[holder] = rows


def attend(x, attn_gain, blocks, places, cosine, signed_sine, start, q, k, v, stat, o, packed, attended):
    tokens, width = x.shape
    scale = HD**-0.5
    normed = x * lax.rsqrt(row_mean(x * x) + EPSILON) * attn_gain
    packed[...] = through(reorder(normed.astype(BF16), places), blocks, slice(0, 3 * width))
    allowed = span_mask(tokens, start)
    masks = head_masks(tokens)
    lane = lax.broadcasted_iota(jnp.int32, (tokens, 128), 1)
    kept = jnp.zeros((tokens, 128), F32)
    for pair in range(H // 2):
        at = slice(128 * pair, 128 * pair + 128)
        turned = []
        for part in range(2):
            raw = packed[:, part * width + 128 * pair : part * width + 128 * pair + 128]
            turned.append((raw * cosine + swap_halves(raw) * signed_sine).astype(BF16))
        queries, keys = turned
        values = packed[:, 2 * width + 128 * pair : 2 * width + 128 * pair + 128].astype(BF16)
        q[:, at], k[:, at], v[:, at] = queries, keys, values
        total = jnp.zeros((tokens, 128), F32)
        for side in range(2):
            mine = masks[side]
            scores = dot(jnp.where(mine, queries, 0), keys, ROWS_BY_ROWS) * scale
            scores = jnp.where(allowed, scores, NEGATIVE)
            top = jnp.max(scores, -1, keepdims=True)
            weights = jnp.exp(scores - top)
            inverse = 1.0 / row_sum(weights)
            kept = jnp.where(lane == 2 * pair + side, top, kept)
            kept = jnp.where(lane == 64 + 2 * pair + side, inverse, kept)
            total = total + dot((weights * inverse).astype(BF16), jnp.where(mine, values, 0))
        attended[:, at] = total.astype(BF16)
    stat[...] = kept
    o[...] = attended[...]
    return x + through(reorder(attended[...], places), blocks, slice(3 * width, 4 * width))


def mix_in(y, moe_gain, mix_rows, target_row, z_extra):
    u = y * lax.rsqrt(row_mean(y * y) + EPSILON) * moe_gain
    logits = dot(u, mix_rows, ROWS_BY_ROWS, TOP)
    if z_extra is not None:
        logits = logits + z_extra
    spread = slot_matrix(target_row[0:1]) | slot_matrix(target_row[1:2])
    return u, logits, dot(spread.astype(F32).astype(BF16), u.astype(BF16)).astype(BF16)


def forward_first(
    start, x, near, far, mix_rows, target_row, order, cosine, signed_sine,
    q, k, v, stat, o, y, z, slots, gains, packed, attended,
):
    width = x.shape[1]
    places = spread_matrix(order[...])
    columns = slice(4 * width, 4 * width + 128)
    stored = jnp.concatenate([near[:, columns], far[:, columns]], 0)
    gain_rows = dot(stored, places, ((0,), (1,)))[0:8, :]
    gains[...] = gain_rows
    middle = attend(
        x[...], gain_rows[0:1], (near, far), places, cosine[...], signed_sine[...], start[0], q, k, v, stat, o, packed,
        attended,
    )
    y[...] = middle
    u, logits, rows = mix_in(middle, gain_rows[1:2], mix_rows[...], target_row[0:2, :], None)
    z[...] = logits
    for holder in range(slots.shape[0]):
        slots[holder] = rows


def gather_shares(returned, target_col, layer):
    both = [
        pick_matrix(target_col[:, 2 * layer + k : 2 * layer + k + 1]).astype(F32).astype(BF16) for k in range(2)
    ]
    totals = [0.0, 0.0]
    for holder in range(returned.shape[0]):
        share = returned[holder]
        for k in range(2):
            totals[k] = totals[k] + dot(both[k], share)
    return totals


def mixed_stream(y, u, logits, routes, const_value, picks):
    gates = gate_pair(logits, *routes)
    of_u, of_const = mix_weights(gates, routes, blend_pairs(logits))
    stream = y + of_u * u
    for c in range(NC):
        stream = stream + of_const[c] * const_value[c : c + 1, :]
    return stream + gates[0] * picks[0] + gates[1] * picks[1]


def forward_second(
    start, returned, y0, z0, gains, const_value0, routes_col, target_col, weights, mix_rows, carry, target_row, cosine,
    signed_sine,
    picks0, x1, q, k, v, stat, o, y, z, slots, gate_slots, packed, attended,
):
    picks = gather_shares(returned, target_col, 0)
    picks0[0], picks0[1] = picks
    y_first, logits_first = y0[...], z0[...]
    u_first = y_first * lax.rsqrt(row_mean(y_first * y_first) + EPSILON) * gains[1:2, :]
    routes = [routes_col[:, k : k + 1] for k in range(2)]
    stream = mixed_stream(y_first, u_first, logits_first, routes, const_value0[...], picks)
    x1[...] = stream
    middle = attend(
        stream, gains[2:3, :], (weights,), None, cosine[...], signed_sine[...], start[0], q, k, v, stat, o, packed, attended
    )
    y[...] = middle
    z_extra = dot(logits_first, carry[...], precision=TOP)
    u, logits, rows = mix_in(middle, gains[3:4, :], mix_rows[...], target_row[2:4, :], z_extra)
    z[...] = logits
    for holder in range(slots.shape[0]):
        slots[holder] = rows
    gates = gate_pair(logits, routes_col[:, 2:3], routes_col[:, 3:4])
    gate_row = 0.0
    for k in range(2):
        mine = pick_matrix(target_col[:, 2 + k : 3 + k])
        gate_row = gate_row + jnp.sum(jnp.where(mine, gates[k], 0.0), 0, keepdims=True)
    gate_slots[...] = jnp.broadcast_to(gate_row, gate_slots.shape)


def final_kernel(returned, y, z, gains, const_value, routes_col, target_col, out):
    picks = gather_shares(returned, target_col, 1)
    middle, logits = y[...], z[...]
    u = middle * lax.rsqrt(row_mean(middle * middle) + EPSILON) * gains[3:4, :]
    routes = [routes_col[:, 2 + k : 3 + k] for k in range(2)]
    out[...] = mixed_stream(middle, u, logits, routes, const_value[...], picks)


def experts_forward(rows, gate_w, up_w, down_w, gate_pre, up_pre, part):
    a = dot(rows[...], gate_w[...])
    b = dot(rows[...], up_w[...])
    gate_pre[...] = a
    up_pre[...] = b
    hidden = (a / (1.0 + jnp.exp(-a)) * b).astype(BF16)
    part[...] = dot(hidden, down_w[...]).astype(BF16)


def expert_back(a, b, df, gate_w, up_w, down_w, hidden, da, db, du):
    dh = dot(df, down_w[...], ROWS_BY_ROWS)
    sig = 1.0 / (1.0 + jnp.exp(-a))
    act = a * sig
    hidden_low = (act * b).astype(BF16)
    hidden[...] = hidden_low
    da_low = (dh * b * sig * (1.0 + a * (1.0 - sig))).astype(BF16)
    db_low = (dh * act).astype(BF16)
    da[...] = da_low
    db[...] = db_low
    du[...] = (dot(da_low, gate_w[...], ROWS_BY_ROWS) + dot(db_low, up_w[...], ROWS_BY_ROWS)).astype(BF16)
    return hidden_low


def experts_backward(df, gate_pre, up_pre, gate_w, up_w, down_w, hidden, da, db, du):
    expert_back(gate_pre[...], up_pre[...], df[...], gate_w, up_w, down_w, hidden, da, db, du)


def experts_both(rows, cot, gate_w, up_w, down_w, part, hidden, da, db, du, dgate):
    a = dot(rows[...], gate_w[...])
    b = dot(rows[...], up_w[...])
    hidden_low = expert_back(a, b, cot[...], gate_w, up_w, down_w, hidden, da, db, du)
    share = dot(hidden_low, down_w[...]).astype(BF16)
    part[...] = share
    inner = row_sum(share.astype(F32) * cot[...].astype(F32))
    dgate[0] = jnp.transpose(jnp.broadcast_to(inner, (inner.shape[0], 128)))[0:8, :]


def expert_grads(scaled, rows, hidden, da, db, df, scale, dgate, dup, ddown):
    step = pl.program_id(0)

    @pl.when(step == 0)
    def _():
        dgate[...] = jnp.zeros_like(dgate)
        dup[...] = jnp.zeros_like(dup)
        ddown[...] = jnp.zeros_like(ddown)

    row_block, hidden_block = rows[...], hidden[...]
    if scaled:
        row_block = (row_block.astype(F32) * scale[...]).astype(BF16)
        hidden_block = (hidden_block.astype(F32) * scale[...]).astype(BF16)
    dgate[0, 0] += dot(row_block, da[...], COLS_BY_COLS)
    dup[0, 0] += dot(row_block, db[...], COLS_BY_COLS)
    ddown[0, 0] += dot(hidden_block, df[...], COLS_BY_COLS)


def mixture_back(layer, grad, dgates, dlogits_extra, y, z, moe_gain, routes_col, const_value, small, at):
    middle, logits = y[...], z[...]
    u = middle * lax.rsqrt(row_mean(middle * middle) + EPSILON) * moe_gain
    routes = [routes_col[:, 2 * layer + r : 2 * layer + r + 1] for r in range(2)]
    gates = gate_pair(logits, *routes)
    blends = blend_pairs(logits)
    by_u = row_sum(grad * u)
    by_const = [row_sum(grad * const_value[c : c + 1, :]) for c in range(NC)]
    dgates = list(dgates)
    for r in range(2):
        dgates[r] = dgates[r] + jnp.where(routes[r] == E + 1, by_u, 0.0)
        for c in range(NC):
            value = blends[c][0] * by_u + blends[c][1] * by_const[c]
            dgates[r] = dgates[r] + jnp.where(routes[r] == E + 2 + c, value, 0.0)
    mean = gates[0] * dgates[0] + gates[1] * dgates[1]
    lane = lax.broadcasted_iota(jnp.int32, logits.shape, 1)
    dlogits = jnp.zeros_like(logits)
    for r in range(2):
        dlogits = jnp.where(lane == routes[r], gates[r] * (dgates[r] - mean), dlogits)
    base = ZW - 2 * NC
    for c in range(NC):
        weight = chosen_weight(gates, routes, E + 2 + c)
        first, second = weight * by_u, weight * by_const[c]
        mean = blends[c][0] * first + blends[c][1] * second
        dlogits = jnp.where(lane == base + 2 * c, blends[c][0] * (first - mean), dlogits)
        dlogits = jnp.where(lane == base + 2 * c + 1, blends[c][1] * (second - mean), dlogits)
        used = jnp.sum(weight * blends[c][1] * grad, 0, keepdims=True)
        small[at + ZW + c : at + ZW + c + 1, :] = used
    if dlogits_extra is not None:
        dlogits = dlogits + dlogits_extra
    small[at : at + ZW, :] = dot(dlogits, u, COLS_BY_COLS, TOP)
    return dlogits


def backward_layer(
    layer, start, grad, dlogits, dexpert, y, x, z, q, k, v, stat, routes_col, mix_rows, attn_gain, moe_gain, blocks, places,
    cosine, signed_sine,
    dx_out, normed_out, dpacked, dy_out, dgains,
):
    tokens, width = x.shape
    scale = HD**-0.5
    middle, logits = y[...], z[...]
    inv_y = lax.rsqrt(row_mean(middle * middle) + EPSILON)
    unit = middle * inv_y
    routes = [routes_col[:, 2 * layer + r : 2 * layer + r + 1] for r in range(2)]
    of_u, _ = mix_weights(gate_pair(logits, *routes), routes, blend_pairs(logits))
    du = of_u * grad + dexpert + dot(dlogits, mix_rows[...], precision=TOP)
    dunit = du * moe_gain
    dmiddle = grad + inv_y * dunit - unit * (inv_y * row_mean(dunit * unit))
    dgains[...] = jnp.zeros_like(dgains)
    dgains[1:2, :] = jnp.sum(du * unit, 0, keepdims=True)
    dy_low = dmiddle.astype(BF16)
    dy_out[...] = dy_low
    dattended = restore(through_back(dy_low, blocks, slice(3 * width, 4 * width)).astype(BF16), places)
    allowed = span_mask(tokens, start)
    masks = head_masks(tokens)
    for pair in range(H // 2):
        at = slice(128 * pair, 128 * pair + 128)
        queries, keys, values, dattn = q[:, at], k[:, at], v[:, at], dattended[:, at]
        dq = jnp.zeros((tokens, 128), F32)
        dk = jnp.zeros((tokens, 128), F32)
        dv = jnp.zeros((tokens, 128), F32)
        for side in range(2):
            mine = masks[side]
            head = 2 * pair + side
            my_queries = jnp.where(mine, queries, 0)
            my_dattn = jnp.where(mine, dattn, 0)
            scores = dot(my_queries, keys, ROWS_BY_ROWS) * scale
            scores = jnp.where(allowed, scores, NEGATIVE)
            weights = jnp.exp(scores - stat[:, head : head + 1]) * stat[:, 64 + head : 65 + head]
            dweights = dot(my_dattn, values, ROWS_BY_ROWS)
            dscores = (weights * (dweights - row_sum(weights * dweights))).astype(BF16)
            dv = dv + dot(weights.astype(BF16), my_dattn, COLS_BY_COLS)
            dq = dq + dot(dscores, jnp.where(mine, keys, 0))
            dk = dk + dot(dscores, my_queries, COLS_BY_COLS)
        dq, dk = dq * scale, dk * scale
        dpacked[:, at] = (dq * cosine - swap_halves(dq) * signed_sine).astype(BF16)
        dpacked[:, width + 128 * pair : width + 128 * pair + 128] = (
            dk * cosine - swap_halves(dk) * signed_sine
        ).astype(BF16)
        dpacked[:, 2 * width + 128 * pair : 2 * width + 128 * pair + 128] = dv.astype(BF16)
    dnormed = restore(through_back(dpacked[...], blocks, slice(0, 3 * width)), places)
    stream = x[...]
    inv_x = lax.rsqrt(row_mean(stream * stream) + EPSILON)
    unit = stream * inv_x
    normed_out[...] = (unit * attn_gain).astype(BF16)
    dgains[0:1, :] = jnp.sum(dnormed * unit, 0, keepdims=True)
    dunit = dnormed * attn_gain
    dx = dmiddle + inv_x * dunit - unit * (inv_x * row_mean(dunit * unit))
    dx_out[...] = dx
    return dx


def backward_second(
    start, dout, shares, dgate, y, x, z, q, k, v, stat, routes_col, target_col, mix_rows, const_value, gains, weights, cosine,
    signed_sine, carry, z0, target_row,
    dx_out, normed_out, dpacked, dy_out, dgains, small, dz0, slots,
):
    small[...] = jnp.zeros_like(small)
    grad = dout[...]
    totals = gather_shares(shares, target_col, 1)
    gates = gate_pair(z[...], routes_col[:, 2:3], routes_col[:, 3:4])
    dexpert = gates[0] * totals[0] + gates[1] * totals[1]
    slot_row = jnp.sum(dgate[...], 0, keepdims=True)
    dgates = [row_sum(jnp.where(pick_matrix(target_col[:, 2 + r : 3 + r]), slot_row, 0.0)) for r in range(2)]
    dlogits = mixture_back(1, grad, dgates, None, y, z, gains[3:4, :], routes_col, const_value, small, 0)
    before = z0[...]
    dz0[...] = dot(dlogits, carry[...], ROWS_BY_ROWS, TOP)
    small[24 : 24 + ZW, 0:ZW] = dot(before, dlogits, COLS_BY_COLS, TOP)
    dx = backward_layer(
        1, start[0], grad, dlogits, dexpert, y, x, z, q, k, v, stat, routes_col, mix_rows, gains[2:3, :], gains[3:4, :],
        (weights,), None, cosine[...], signed_sine[...],
        dx_out, normed_out, dpacked, dy_out, dgains,
    )
    gates = gate_pair(before, routes_col[:, 0:1], routes_col[:, 1:2])
    rows = 0.0
    for r in range(2):
        spread = slot_matrix(target_row[r : r + 1, :]).astype(F32).astype(BF16)
        rows = rows + dot(spread, (gates[r] * dx).astype(BF16))
    rows = rows.astype(BF16)
    for holder in range(slots.shape[0]):
        slots[holder] = rows


def mixture_first(dout, picks, dz0, y, z, gains, routes_col, const_value, small1, dlogits_out, small):
    small[0:24, :] = jnp.zeros((24, small.shape[1]), F32)
    small[24:, :] = small1[...]
    grad = dout[...]
    dgates = [row_sum(grad * picks[r]) for r in range(2)]
    dlogits_out[...] = mixture_back(
        0, grad, dgates, dz0[...], y, z, gains[1:2, :], routes_col, const_value, small, 0
    )


def backward_first(
    start, dout, dlogits, shares, y, x, z, q, k, v, stat, routes_col, target_col, mix_rows, gains, near, far, order, cosine,
    signed_sine,
    dx_out, normed_out, dpacked, dy_out, dgains,
):
    totals = gather_shares(shares, target_col, 0)
    backward_layer(
        0, start[0], dout[...], dlogits[...], totals[0] + totals[1], y, x, z, q, k, v, stat, routes_col, mix_rows,
        gains[0:1, :], gains[1:2, :], (near, far), spread_matrix(order[...]), cosine[...], signed_sine[...],
        dx_out, normed_out, dpacked, dy_out, dgains,
    )


def projection_grads(normed, dpacked, o, dy, dgains, order, out):
    width = normed.shape[1]
    places = spread_matrix(order[...])
    out[:, : 3 * width] = dot(reorder(normed[...], places), dpacked[...], COLS_BY_COLS).astype(BF16)
    out[:, 3 * width : 4 * width] = dot(reorder(o[...], places), dy[...], COLS_BY_COLS).astype(BF16)
    padded = jnp.concatenate([dgains[...], jnp.zeros((120, width), F32)], 0).astype(BF16)
    out[:, 4 * width :] = dot(places, padded, ((0,), (1,))).astype(BF16)


def rotated(shift, devices):
    return [(i, (i + shift) % devices) for i in range(devices)]


def flipped(bits, devices):
    return [(i, i ^ bits) for i in range(devices)]


def feature_order(width):
    devices = lax.axis_size("ep")
    levels = devices // 8
    rows = width // devices
    me = lax.axis_index("ep")
    place = jnp.arange(width, dtype=jnp.int32)
    inside, block = place % rows, place // rows
    level = (block % levels + me // 8) % levels
    chip = ((block // levels) % 4) ^ ((me // 2) % 4)
    core = (block // (4 * levels)) ^ (me % 2)
    return (((level * 4 + chip) * 2 + core) * rows + inside).reshape(1, width)


def gather_near(block):
    devices = lax.axis_size("ep")
    parts = [block] + [lax.ppermute(block, "ep", rotated(-8 * d, devices)) for d in range(1, devices // 8)]
    column = jnp.concatenate(parts, 0)
    parts = [column] + [lax.ppermute(column, "ep", flipped(2 * d, devices)) for d in range(1, 4)]
    near = jnp.concatenate(parts, 0)
    return near, lax.ppermute(near, "ep", flipped(1, devices))


def scatter_sum(packet):
    devices = lax.axis_size("ep")
    half = packet.shape[0] // 2
    far = lax.ppermute(packet[half:], "ep", flipped(1, devices))
    total = packet[:half].astype(F32) + far.astype(F32)
    quarter = half // 4
    low = total.astype(BF16)
    chips = [
        lax.ppermute(low[d * quarter : (d + 1) * quarter], "ep", flipped(2 * d, devices)) for d in range(1, 4)
    ]
    total = total[:quarter] + sum(part.astype(F32) for part in chips)
    levels = devices // 8
    rows = quarter // levels
    low = total.astype(BF16)
    planes = [
        lax.ppermute(low[d * rows : (d + 1) * rows], "ep", rotated(8 * d, devices)) for d in range(1, levels)
    ]
    return total[:rows] + sum(part.astype(F32) for part in planes)


def exchange(slots):
    return lax.all_to_all(slots, "ep", split_axis=0, concat_axis=0, tiled=True)


def by_blocks(rows_per_step, width):
    return pl.BlockSpec((rows_per_step, width), lambda i: (i, 0))


def shards(
    x_in,
    cotangent,
    attn_gain,
    w_qkv,
    w_out,
    moe_gain,
    w_router,
    w_carry,
    const_gate,
    const_value,
    exp_gate,
    exp_up,
    exp_down,
    routes,
    drop_order,
    image_start,
):
    devices = lax.axis_size("ep")
    holders = devices // E
    tokens, width = x_in.shape
    inner = exp_gate.shape[-1]
    total_rows = devices * CAP
    block = SLOTS
    steps = total_rows // block
    cosine, signed_sine = (jnp.asarray(t) for t in rope_tables(tokens))

    def beside(layer, extra):
        return jnp.concatenate([w_qkv[layer], w_out[layer]] + extra, 1)

    gain_columns = jnp.stack([attn_gain[0], moe_gain[0], attn_gain[1], moe_gain[1]], 1)
    gain_columns = jnp.pad(gain_columns, ((0, 0), (0, 124)))
    near, far = gather_near(beside(0, [gain_columns]))
    order = feature_order(width)
    straight = jnp.arange(width, dtype=jnp.int32).reshape(1, width)
    mix_rows = [
        jnp.concatenate([w_router[layer].T, const_gate[layer].reshape(2 * NC, width)], 0) for layer in range(LAYERS)
    ]
    carry = jnp.pad(w_carry, ((0, ZW - w_carry.shape[0]), (0, ZW - w_carry.shape[1])))

    routes_row = routes.transpose(0, 2, 1).reshape(2 * LAYERS, tokens)
    routes_col = routes.transpose(1, 0, 2).reshape(tokens, 2 * LAYERS)

    slots_shape = shaped((holders, SLOTS, width), BF16)
    flat = shaped((tokens, width), F32)
    flat_low = shaped((tokens, width), BF16)
    logits_shape = shaped((tokens, ZW), F32)
    stat_shape = shaped((tokens, 128), F32)
    scratch = [pltpu.VMEM((tokens, 3 * width), F32), pltpu.VMEM((tokens, width), BF16)]

    target_row, target_col, cot_slots = pl.pallas_call(
        prep_kernel,
        out_shape=(shaped((2 * LAYERS, tokens), jnp.int32), shaped((tokens, 2 * LAYERS), jnp.int32), slots_shape),
        compiler_params=params(),
        name="prep",
    )(routes_row, routes_col, drop_order, drop_order.reshape(tokens, 1), cotangent)

    def send(slots):
        return exchange(slots.reshape(devices, CAP, slots.shape[-1]))

    cot_rows = send(cot_slots)
    saved = [None] * LAYERS
    q, k, v, stat, o, y, z, slots, gains = pl.pallas_call(
        forward_first,
        in_specs=[whole(pltpu.SMEM)] + [whole()] * 8,
        out_shape=(
            flat_low, flat_low, flat_low, stat_shape, flat_low, flat, logits_shape, slots_shape, shaped((8, width), F32)
        ),
        scratch_shapes=scratch,
        compiler_params=params(),
        name="forward_first",
    )(image_start, x_in, near, far, mix_rows[0], target_row, order, cosine, signed_sine)
    saved[0] = (y, x_in, z, q, k, v, stat)
    attended0 = o
    slots, cot_rows = lax.optimization_barrier((slots, cot_rows))
    cot_rows = cot_rows.reshape(total_rows, width)

    later, slots = lax.optimization_barrier((beside(1, []), slots))
    weights1 = lax.all_gather(later, "ep", axis=0, tiled=True)

    def weight_specs(layer):
        return [
            pl.BlockSpec((None, None, width, inner), lambda i: (layer, 0, 0, 0)),
            pl.BlockSpec((None, None, width, inner), lambda i: (layer, 0, 0, 0)),
            pl.BlockSpec((None, None, inner, width), lambda i: (layer, 0, 0, 0)),
        ]

    rows0 = send(slots).reshape(total_rows, width)
    gate_pre, up_pre, part = pl.pallas_call(
        experts_forward,
        grid=(steps,),
        in_specs=[by_blocks(block, width)] + weight_specs(0),
        out_specs=(by_blocks(block, inner), by_blocks(block, inner), by_blocks(block, width)),
        out_shape=(
            shaped((total_rows, inner), F32), shaped((total_rows, inner), F32), shaped((total_rows, width), BF16)
        ),
        compiler_params=params(),
        name="experts_forward",
    )(rows0, exp_gate, exp_up, exp_down)

    returned = send(part).reshape(holders, SLOTS, width)
    picks0, x1, q, k, v, stat, o, y, z, slots, gate_slots = pl.pallas_call(
        forward_second,
        in_specs=[whole(pltpu.SMEM)] + [whole()] * 13,
        out_shape=(
            shaped((2, tokens, width), F32), flat, flat_low, flat_low, flat_low, stat_shape, flat_low, flat, logits_shape,
            slots_shape, shaped((holders, SLOTS), F32),
        ),
        scratch_shapes=scratch,
        compiler_params=params(),
        name="forward_second",
    )(
        image_start, returned, saved[0][0], saved[0][2], gains, const_value[0], routes_col, target_col, weights1,
        mix_rows[1], carry, target_row, cosine, signed_sine,
    )
    saved[1] = (y, x1, z, q, k, v, stat)
    attended1 = o

    rows1 = send(slots).reshape(total_rows, width)
    gate_rows = exchange(gate_slots.reshape(devices, CAP)).reshape(total_rows, 1)
    low_inner = shaped((total_rows, inner), BF16)
    low_rows = shaped((total_rows, width), BF16)
    part1, hidden1, da1, db1, du1, dgate1 = pl.pallas_call(
        experts_both,
        grid=(steps,),
        in_specs=[by_blocks(block, width)] * 2 + weight_specs(1),
        out_specs=(
            by_blocks(block, width), by_blocks(block, inner), by_blocks(block, inner), by_blocks(block, inner),
            by_blocks(block, width), pl.BlockSpec((1, 8, block), lambda i: (i, 0, 0)),
        ),
        out_shape=(low_rows, low_inner, low_inner, low_inner, low_rows, shaped((steps, 8, block), F32)),
        compiler_params=params(),
        name="experts_both",
    )(rows1, cot_rows, exp_gate, exp_up, exp_down)

    dgate_back = exchange(dgate1[:, 0, :].reshape(devices, CAP)).reshape(holders, SLOTS)
    shares1 = send(du1).reshape(holders, SLOTS, width)
    back_shapes = (flat, flat_low, shaped((tokens, 3 * width), BF16), flat_low, shaped((8, width), F32))
    dx1, normed1, dpacked1, dy1, dgains1, small1, dz0, df_slots = pl.pallas_call(
        backward_second,
        in_specs=[whole(pltpu.SMEM)] + [whole()] * 21,
        out_shape=back_shapes + (shaped((40, width), F32), logits_shape, slots_shape),
        compiler_params=params(),
        name="backward_second",
    )(
        image_start, cotangent, shares1, dgate_back, *saved[1], routes_col, target_col, mix_rows[1], const_value[1], gains,
        weights1, cosine, signed_sine, carry, saved[0][2], target_row,
    )

    def packet(normed, dpacked, attended, dy, dgains, rows_order):
        return pl.pallas_call(
            projection_grads,
            out_shape=shaped((width, 4 * width + 128), BF16),
            compiler_params=params(),
            cost_estimate=pl.CostEstimate(
                flops=8 * tokens * width * width, bytes_accessed=8 * 1024 * 1024, transcendentals=0
            ),
            name="projection_grads",
        )(normed, dpacked, attended, dy, dgains, rows_order)

    packet1 = packet(normed1, dpacked1, attended1, dy1, dgains1, straight)
    reduced1 = lax.psum_scatter(packet1, "ep", scatter_dimension=0, tiled=True).astype(F32)
    dlogits0, small = pl.pallas_call(
        mixture_first,
        out_shape=(logits_shape, shaped((64, width), F32)),
        compiler_params=params(),
        name="mixture_first",
    )(dx1, picks0, dz0, saved[0][0], saved[0][2], gains, routes_col, const_value[0], small1)

    df0 = send(df_slots).reshape(total_rows, width)
    hidden0, da0, db0, du0 = pl.pallas_call(
        experts_backward,
        grid=(steps,),
        in_specs=[by_blocks(block, width), by_blocks(block, inner), by_blocks(block, inner)] + weight_specs(0),
        out_specs=(
            by_blocks(block, inner), by_blocks(block, inner), by_blocks(block, inner), by_blocks(block, width)
        ),
        out_shape=(low_inner, low_inner, low_inner, low_rows),
        compiler_params=params(),
        name="experts_backward",
    )(df0, gate_pre, up_pre, exp_gate, exp_up, exp_down)
    shares0 = send(du0).reshape(holders, SLOTS, width)

    def weight_grads(layer, rows, hidden, da, db, df, scale, earlier):
        operands = [rows, hidden, da, db, df]
        in_specs = [by_blocks(block, t.shape[1]) for t in operands]
        scaled = scale is not None
        operands.append(scale if scaled else jnp.ones((8, 1), F32))
        in_specs.append(by_blocks(block, 1) if scaled else pl.BlockSpec((8, 1), lambda i: (0, 0)))
        kernel = partial(expert_grads, scaled)
        aliases = {}
        if earlier is not None:
            body = kernel

            def kernel(*refs):
                body(*refs[:6], *refs[9:])

            operands += list(earlier)
            in_specs += [pl.BlockSpec(memory_space=pl.ANY)] * 3
            aliases = {6: 0, 7: 1, 8: 2}
        return pl.pallas_call(
            kernel,
            grid=(steps,),
            in_specs=in_specs,
            out_specs=(
                pl.BlockSpec((1, 1, width, inner), lambda i: (layer, 0, 0, 0)),
                pl.BlockSpec((1, 1, width, inner), lambda i: (layer, 0, 0, 0)),
                pl.BlockSpec((1, 1, inner, width), lambda i: (layer, 0, 0, 0)),
            ),
            out_shape=(
                shaped((LAYERS, 1, width, inner), F32), shaped((LAYERS, 1, width, inner), F32),
                shaped((LAYERS, 1, inner, width), F32),
            ),
            input_output_aliases=aliases,
            compiler_params=params(),
            cost_estimate=pl.CostEstimate(
                flops=6 * total_rows * width * inner, bytes_accessed=16 * 1024 * 1024, transcendentals=0
            ),
            name="expert_grads",
        )(*operands)

    expert_parts = weight_grads(1, rows1, hidden1, da1, db1, cot_rows, gate_rows, None)
    small_parts = exchange(small.reshape(devices, small.size // devices))
    small_parts = jnp.broadcast_to(jnp.sum(small_parts, 0, keepdims=True), small_parts.shape)

    shares0, expert_parts, small_parts = lax.optimization_barrier((shares0, expert_parts, small_parts))
    part1, small_parts, shares0 = lax.optimization_barrier((part1, small_parts, shares0))
    grad_x, normed0, dpacked0, dy0, dgains0 = pl.pallas_call(
        backward_first,
        in_specs=[whole(pltpu.SMEM)] + [whole()] * 19,
        out_shape=back_shapes,
        compiler_params=params(),
        name="backward_first",
    )(
        image_start, dx1, dlogits0, shares0, *saved[0], routes_col, target_col, mix_rows[0], gains, near, far, order,
        cosine, signed_sine,
    )
    reduced0 = scatter_sum(packet(normed0, dpacked0, attended0, dy0, dgains0, order))
    expert_parts = weight_grads(0, rows0, hidden0, da0, db0, df0, None, expert_parts)
    hidden_out = pl.pallas_call(
        final_kernel,
        out_shape=flat,
        compiler_params=params(),
        name="final",
    )(
        send(part1).reshape(holders, SLOTS, width), saved[1][0], saved[1][2], gains, const_value[1], routes_col, target_col
    )

    small = exchange(small_parts).reshape(small.shape)
    both = jnp.stack([small[0:24], small[24:48]])
    routers = w_router.shape[-1]
    reduced = jnp.stack([reduced0, reduced1])
    return (
        hidden_out,
        grad_x,
        reduced[:, :, 4 * width],
        reduced[:, :, : 3 * width],
        reduced[:, :, 3 * width : 4 * width],
        reduced[:, :, 4 * width + 1],
        both[:, :routers].transpose(0, 2, 1),
        small[48 : 48 + routers, :routers],
        both[:, routers:ZW].reshape(LAYERS, NC, 2, width),
        both[:, ZW : ZW + NC],
        *expert_parts,
    )


def solution(mesh):
    in_specs = (
        P("ep", None),
        P("ep", None),
        P(None, "ep"),
        P(None, "ep", None),
        P(None, "ep", None),
        P(None, "ep"),
        P(),
        P(),
        P(),
        P(),
        P(None, "ep", None, None),
        P(None, "ep", None, None),
        P(None, "ep", None, None),
        P(None, "ep", None),
        P("ep", None),
        P("ep"),
    )
    out_specs = (
        P("ep", None),
        P("ep", None),
        P(None, "ep"),
        P(None, "ep", None),
        P(None, "ep", None),
        P(None, "ep"),
        P(),
        P(),
        P(),
        P(),
        P(None, "ep", None, None),
        P(None, "ep", None, None),
        P(None, "ep", None, None),
    )
    return jax.shard_map(shards, mesh=mesh, in_specs=in_specs, out_specs=out_specs, check_vma=False)
```

```python
from functools import partial

import jax
import jax.numpy as jnp
import numpy as np
from jax import lax
from jax.experimental import pallas as pl
from jax.experimental.pallas import tpu as pltpu
from jax.sharding import PartitionSpec as P

H = 12
HD = 64
E = 8
NC = 2
LAYERS = 2
SPAN = 128
CAP = 40
SLOTS = E * CAP
ZW = 16

EPSILON = 1e-06
NEGATIVE = -1e30
F32 = jnp.float32
BF16 = jnp.bfloat16
TOP = lax.Precision.HIGHEST
VMEM_LIMIT = 61 * 1024 * 1024


def whole(space=pltpu.VMEM):
    return pl.BlockSpec(memory_space=space)


def shaped(shape, dtype):
    return pltpu.HBM(shape, dtype)


def params():
    return pltpu.CompilerParams(vmem_limit_bytes=VMEM_LIMIT)


def cost(microseconds):
    return pl.CostEstimate(
        flops=int(microseconds * 1e9), bytes_accessed=int(microseconds * 3e6), transcendentals=0
    )


class Lazy:
    def __init__(self, copies, local):
        self.copies, self.local = copies, local
        self.shape, self.dtype = local.shape, local.dtype
        for copy in copies:
            copy.start()

    def __getitem__(self, index):
        for copy in self.copies:
            copy.wait()
        self.copies = []
        return self.local[index]


class Kept:
    def __init__(self, local, copy):
        self.local, self.copy, self.sent = local, copy, False
        self.shape, self.dtype = local.shape, local.dtype

    def __getitem__(self, index):
        return self.local[index]

    def __setitem__(self, index, value):
        self.local[index] = value

    def flush(self):
        if not self.sent:
            self.copy.start()
        self.sent = True


def staged(kernel, name, microseconds, outs, start, args, pieces=(), scratch=()):
    n_args, n_outs, n_pieces = len(args), len(outs), len(pieces)
    fixed = [pltpu.VMEM(t.shape, t.dtype) for t in args] + [pltpu.VMEM(t.shape, t.dtype) for t in outs]
    if pieces:
        rows, columns = pieces[0].shape
        fixed.append(pltpu.VMEM((rows * n_pieces, columns), pieces[0].dtype))
    fixed.append(pltpu.SemaphoreType.DMA((n_args + n_outs + n_pieces,)))

    def body(start_ref, *refs):
        arg_refs, refs = refs[:n_args], refs[n_args:]
        piece_refs, refs = refs[:n_pieces], refs[n_pieces:]
        out_refs, refs = refs[:n_outs], refs[n_outs:]
        local, rest = refs[: len(fixed)], refs[len(fixed) :]
        sems = local[-1]
        lazies = [
            Lazy([pltpu.make_async_copy(ref, local[i], sems.at[i])], local[i]) for i, ref in enumerate(arg_refs)
        ]
        kept = [
            Kept(local[n_args + i], pltpu.make_async_copy(local[n_args + i], ref, sems.at[n_args + i]))
            for i, ref in enumerate(out_refs)
        ]
        weights = []
        if pieces:
            target, first = local[-2], n_args + n_outs
            copies = [
                pltpu.make_async_copy(ref, target.at[pl.ds(i * rows, rows)], sems.at[first + i])
                for i, ref in enumerate(piece_refs)
            ]
            weights = [Lazy(copies, target)]
        kernel(start_ref, *lazies, *weights, *kept, *rest)
        for out in kept:
            out.flush()
        for out in kept:
            out.copy.wait()

    return pl.pallas_call(
        body,
        in_specs=[whole(pltpu.SMEM)] + [whole(pl.ANY)] * (n_args + n_pieces),
        out_specs=tuple(whole(pl.ANY) for _ in outs),
        out_shape=tuple(outs),
        scratch_shapes=fixed + list(scratch),
        compiler_params=params(),
        cost_estimate=cost(microseconds),
        name=name,
    )(start, *args, *pieces)


def dot(a, b, dims=((1,), (0,)), precision=None):
    return lax.dot_general(a, b, (dims, ((), ())), precision=precision, preferred_element_type=F32)


ROWS_BY_ROWS = ((1,), (1,))
COLS_BY_COLS = ((0,), (0,))


def spread_matrix(order):
    feature = lax.broadcasted_iota(jnp.int32, (order.shape[1], order.shape[1]), 0)
    return (feature == order).astype(F32).astype(BF16)


def gather_matrix(order_col):
    feature = lax.broadcasted_iota(jnp.int32, (order_col.shape[0], order_col.shape[0]), 1)
    return (feature == order_col).astype(F32).astype(BF16)


def reorder(values, places):
    return dot(values, places).astype(BF16)


def restore(values, back):
    if values.dtype == BF16:
        return dot(values, back).astype(BF16)
    high = values.astype(BF16)
    low = (values - high.astype(F32)).astype(BF16)
    return dot(high, back) + dot(low, back)


def rope_tables(length):
    position = np.arange(length).astype(np.float32)
    inverse = (10000.0 ** (-np.arange(HD // 2).astype(np.float32) * 2.0 / HD)).astype(np.float32)
    angles = (position[:, None] * inverse[None, :]).astype(np.float32)
    cosine, sine = np.cos(angles), np.sin(angles)
    return (
        np.concatenate([cosine] * 4, 1).astype(np.float32),
        np.concatenate([-sine, sine, -sine, sine], 1).astype(np.float32),
    )


def swap_halves(values):
    lane = lax.broadcasted_iota(jnp.int32, values.shape, 1)
    low = lane % HD < HD // 2
    return jnp.where(low, pltpu.roll(values, 128 - HD // 2, 1), pltpu.roll(values, HD // 2, 1))


def span_mask(length, start):
    query = lax.broadcasted_iota(jnp.int32, (length, length), 0)
    key = lax.broadcasted_iota(jnp.int32, (length, length), 1)
    in_query = (query >= start) & (query < start + SPAN)
    in_key = (key >= start) & (key < start + SPAN)
    return (key <= query) | (in_query & in_key)


def head_masks(length):
    lane = lax.broadcasted_iota(jnp.int32, (length, 2 * HD), 1)
    return (lane < HD, lane >= HD)


def row_mean(values):
    return jnp.mean(values, -1, keepdims=True)


def row_sum(values):
    return jnp.sum(values, -1, keepdims=True)


def slot_matrix(target_row):
    slot = lax.broadcasted_iota(jnp.int32, (SLOTS, target_row.shape[1]), 0)
    return slot == target_row


def pick_matrix(target_col):
    slot = lax.broadcasted_iota(jnp.int32, (target_col.shape[0], SLOTS), 1)
    return slot == target_col


def gate_pair(logits, first, second):
    lane = lax.broadcasted_iota(jnp.int32, logits.shape, 1)
    one = row_sum(jnp.where(lane == first, logits, 0.0))
    two = row_sum(jnp.where(lane == second, logits, 0.0))
    return soft_pair(one, two)


def soft_pair(one, two):
    top = jnp.maximum(one, two)
    one, two = jnp.exp(one - top), jnp.exp(two - top)
    total = one + two
    return one / total, two / total


def blend_pairs(logits):
    base = ZW - 2 * NC
    return [
        soft_pair(logits[:, base + 2 * c : base + 2 * c + 1], logits[:, base + 2 * c + 1 : base + 2 * c + 2])
        for c in range(NC)
    ]


def chosen_weight(gates, routes, expert):
    return sum(jnp.where(route == expert, gate, 0.0) for gate, route in zip(gates, routes))


def mix_weights(gates, routes, blends):
    of_u = chosen_weight(gates, routes, E + 1)
    of_const = []
    for c in range(NC):
        weight = chosen_weight(gates, routes, E + 2 + c)
        of_u = of_u + weight * blends[c][0]
        of_const.append(weight * blends[c][1])
    return of_u, of_const


def prep_kernel(routes_row, routes_col, order_row, order_col, cot, target_row, target_col, cot_low):
    tokens = order_row.shape[1]
    earlier = jnp.where(order_row[...] < order_col[...], 1.0, 0.0).astype(BF16)
    later = jnp.where(order_col[...] < order_row[...], 1.0, 0.0).astype(BF16)
    lane = lax.broadcasted_iota(jnp.int32, (tokens, 128), 1)
    sub = lax.broadcasted_iota(jnp.int32, (16, tokens), 0)
    for layer in range(LAYERS):
        cols = [routes_col[:, 2 * layer + k : 2 * layer + k + 1] for k in range(2)]
        rows = [routes_row[2 * layer + k : 2 * layer + k + 1, :] for k in range(2)]
        wanted = jnp.where((lane == cols[0]) | (lane == cols[1]), 1.0, 0.0).astype(BF16)
        counts = dot(earlier, wanted)
        wanted_t = jnp.where((sub == rows[0]) | (sub == rows[1]), 1.0, 0.0).astype(BF16)
        counts_t = dot(wanted_t, later)
        for k in range(2):
            rank = row_sum(jnp.where(lane == cols[k], counts, 0.0)).astype(jnp.int32)
            kept = (cols[k] < E) & (rank < CAP)
            target_col[:, 2 * layer + k : 2 * layer + k + 1] = jnp.where(kept, cols[k] * CAP + rank, -1)
            rank_t = jnp.sum(jnp.where(sub == rows[k], counts_t, 0.0), 0, keepdims=True).astype(jnp.int32)
            kept_t = (rows[k] < E) & (rank_t < CAP)
            target_row[2 * layer + k : 2 * layer + k + 1, :] = jnp.where(kept_t, rows[k] * CAP + rank_t, -1)
    width = cot.shape[1]
    cot_low[:, :width] = cot[...].astype(BF16)
    marks = jnp.zeros((tokens, 128), F32)
    for k in range(2):
        last = 2 * (LAYERS - 1) + k
        target = target_col[:, last : last + 1]
        high = (target + 16) // 16 * 16 - 16
        marks = jnp.where(lane == 2 * k, high.astype(F32), marks)
        marks = jnp.where(lane == 2 * k + 1, (target - high).astype(F32), marks)
    cot_low[:, width:] = marks.astype(BF16)


def marked_slots(marks):
    taken = None
    for k in range(2):
        target = (marks[:, 2 * k : 2 * k + 1] + marks[:, 2 * k + 1 : 2 * k + 2]).astype(jnp.int32)
        mine = pick_matrix(target)
        taken = mine if taken is None else taken | mine
    return taken.astype(F32).astype(BF16)


def spread_kernel(place, *refs):
    sources, out = refs[:-1], refs[-1]
    width = out.shape[3]
    for level, source in enumerate(sources):
        taken = marked_slots(source[:, width:].astype(F32))
        rows = dot(taken, source[:, :width], COLS_BY_COLS)
        for expert in range(E):
            out[jnp.bitwise_xor(expert, place[0]), level] = rows[expert * CAP : (expert + 1) * CAP].astype(BF16)


def combine_kernel(shares, *refs):
    sources, outs = refs[: len(refs) // 2], refs[len(refs) // 2 :]
    for level, (source, out) in enumerate(zip(sources, outs)):
        rows = shares[:, level].astype(F32).reshape(SLOTS, shares.shape[3]).astype(BF16)
        out[...] = dot(marked_slots(source[...].astype(F32)), rows).astype(BF16)


def attend(x, attn_gain, weights, places, cosine, signed_sine, start, q, k, v, stat, o, packed, attended):
    tokens, width = x.shape
    scale = HD**-0.5
    normed = x * lax.rsqrt(row_mean(x * x) + EPSILON) * attn_gain
    packed[...] = dot(reorder(normed.astype(BF16), places), weights[:, : 3 * width])
    allowed = span_mask(tokens, start)
    masks = head_masks(tokens)
    lane = lax.broadcasted_iota(jnp.int32, (tokens, 128), 1)
    kept = jnp.zeros((tokens, 128), F32)
    for pair in range(H // 2):
        at = slice(128 * pair, 128 * pair + 128)
        turned = []
        for part in range(2):
            raw = packed[:, part * width + 128 * pair : part * width + 128 * pair + 128]
            turned.append((raw * cosine + swap_halves(raw) * signed_sine).astype(BF16))
        queries, keys = turned
        values = packed[:, 2 * width + 128 * pair : 2 * width + 128 * pair + 128].astype(BF16)
        q[:, at], k[:, at], v[:, at] = queries, keys, values
        total = jnp.zeros((tokens, 128), F32)
        for side in range(2):
            mine = masks[side]
            scores = dot(jnp.where(mine, queries, 0), keys, ROWS_BY_ROWS) * scale
            scores = jnp.where(allowed, scores, NEGATIVE)
            top = jnp.max(scores, -1, keepdims=True)
            probs = jnp.exp(scores - top)
            inverse = 1.0 / row_sum(probs)
            kept = jnp.where(lane == 2 * pair + side, top, kept)
            kept = jnp.where(lane == 64 + 2 * pair + side, inverse, kept)
            total = total + dot((probs * inverse).astype(BF16), jnp.where(mine, values, 0))
        attended[:, at] = total.astype(BF16)
    stat[...] = kept
    o[...] = attended[...]
    for out in (q, k, v, stat, o):
        out.flush()
    return x + dot(reorder(attended[...], places), weights[:, 3 * width : 4 * width])


def mix_in(y, moe_gain, mix_rows, target_row, z_extra):
    u = y * lax.rsqrt(row_mean(y * y) + EPSILON) * moe_gain
    logits = dot(u, mix_rows, ROWS_BY_ROWS, TOP)
    if z_extra is not None:
        logits = logits + z_extra
    spread = slot_matrix(target_row[0:1]) | slot_matrix(target_row[1:2])
    return u, logits, dot(spread.astype(F32).astype(BF16), u.astype(BF16)).astype(BF16)


def forward_first(
    start, x, target_row, order, cosine, signed_sine, mix_rows, weights, q, k, v, stat, o, y, z, slots, gains, packed, attended
):
    width = x.shape[1]
    places = spread_matrix(order[...])
    gain_rows = dot(weights[:, 4 * width :], places, ((0,), (1,)))[0:8, :]
    gains[...] = gain_rows
    gains.flush()
    middle = attend(
        x[...], gain_rows[0:1], weights, places, cosine[...], signed_sine[...], start[0], q, k, v, stat, o, packed, attended
    )
    y[...] = middle
    y.flush()
    u, logits, rows = mix_in(middle, gain_rows[1:2], mix_rows[...], target_row[0:2, :], None)
    z[...] = logits
    for holder in range(slots.shape[0]):
        slots[holder] = rows


def in_two(column, lane):
    high = column.astype(BF16).astype(F32)
    return jnp.where(lane == 0, high, jnp.where(lane == 1, column - high, 0.0)).astype(BF16)


def gather_shares(returned, target_col, layer):
    both = [
        pick_matrix(target_col[:, 2 * layer + k : 2 * layer + k + 1]).astype(F32).astype(BF16) for k in range(2)
    ]
    totals = [0.0, 0.0]
    for holder in range(returned.shape[0]):
        share = returned[holder]
        for k in range(2):
            totals[k] = totals[k] + dot(both[k], share)
    return totals


def mixed_stream(y, u, logits, routes, const_value, picks):
    gates = gate_pair(logits, *routes)
    of_u, of_const = mix_weights(gates, routes, blend_pairs(logits))
    stream = y + of_u * u
    for c in range(NC):
        stream = stream + of_const[c] * const_value[c : c + 1, :]
    return stream if picks is None else stream + gates[0] * picks[0] + gates[1] * picks[1]


def forward_second(
    start, returned, y0, z0, gains, const_value0, routes_col, target_col, order, cosine, signed_sine, mix_rows, carry,
    target_row, weights,
    picks0, x1, q, k, v, stat, o, y, z, slots, gate_slots, packed, attended,
):
    y_first, logits_first = y0[...], z0[...]
    u_first = y_first * lax.rsqrt(row_mean(y_first * y_first) + EPSILON) * gains[1:2, :]
    routes = [routes_col[:, k : k + 1] for k in range(2)]
    picks = gather_shares(returned, target_col, 0)
    picks0[0], picks0[1] = picks
    picks0.flush()
    stream = mixed_stream(y_first, u_first, logits_first, routes, const_value0[...], picks)
    x1[...] = stream
    x1.flush()
    places = spread_matrix(order[...])
    middle = attend(
        stream, gains[2:3, :], weights, places, cosine[...], signed_sine[...], start[0], q, k, v, stat, o, packed, attended
    )
    y[...] = middle
    y.flush()
    z_extra = dot(logits_first, carry[...], precision=TOP)
    u, logits, rows = mix_in(middle, gains[3:4, :], mix_rows[...], target_row[2:4, :], z_extra)
    z[...] = logits
    for holder in range(slots.shape[0]):
        slots[holder] = rows
    slots.flush()
    gates = gate_pair(logits, routes_col[:, 2:3], routes_col[:, 3:4])
    lane = lax.broadcasted_iota(jnp.int32, (x1.shape[0], 128), 1)
    of_slots = 0.0
    for r in range(2):
        spread = slot_matrix(target_row[2 + r : 3 + r, :]).astype(F32).astype(BF16)
        of_slots = of_slots + dot(spread, in_two(gates[r], lane))
    for holder in range(gate_slots.shape[0]):
        gate_slots[holder] = of_slots.astype(BF16)


def final_kernel(y, z, gains, const_value, routes_col, *refs):
    parts, out = refs[:-1], refs[-1]
    middle, logits = y[...], z[...]
    u = middle * lax.rsqrt(row_mean(middle * middle) + EPSILON) * gains[3:4, :]
    routes = [routes_col[:, 2 + k : 3 + k] for k in range(2)]
    stream = middle + sum(part[...].astype(F32) for part in parts)
    out[...] = mixed_stream(stream, u, logits, routes, const_value[...], None)


def experts_forward(rows, gate_w, up_w, down_w, gate_pre, up_pre, part):
    a = dot(rows[...], gate_w[...])
    b = dot(rows[...], up_w[...])
    gate_pre[...] = a
    up_pre[...] = b
    hidden = (a / (1.0 + jnp.exp(-a)) * b).astype(BF16)
    part[...] = dot(hidden, down_w[...]).astype(BF16)


def expert_back(a, b, df, gate_w, up_w, down_w, hidden, da, db):
    dh = dot(df, down_w[...], ROWS_BY_ROWS)
    sig = 1.0 / (1.0 + jnp.exp(-a))
    act = a * sig
    hidden_low = (act * b).astype(BF16)
    hidden[...] = hidden_low
    da_low = (dh * b * sig * (1.0 + a * (1.0 - sig))).astype(BF16)
    db_low = (dh * act).astype(BF16)
    da[...] = da_low
    db[...] = db_low
    du = dot(da_low, gate_w[...], ROWS_BY_ROWS) + dot(db_low, up_w[...], ROWS_BY_ROWS)
    return hidden_low, du.astype(BF16)


def experts_backward(df, gate_pre, up_pre, gate_w, up_w, down_w, hidden, da, db, du):
    du[...] = expert_back(gate_pre[...], up_pre[...], df[...], gate_w, up_w, down_w, hidden, da, db)[1]


def experts_both(rows, cot, gate_w, up_w, down_w, hidden, da, db, du):
    width = rows.shape[1]
    a = dot(rows[...], gate_w[...])
    b = dot(rows[...], up_w[...])
    hidden_low, du_low = expert_back(a, b, cot[...], gate_w, up_w, down_w, hidden, da, db)
    share = dot(hidden_low, down_w[...]).astype(BF16)
    du[:, :width] = du_low
    inner = row_sum(share.astype(F32) * cot[...].astype(F32))
    du[:, width:] = in_two(inner, lax.broadcasted_iota(jnp.int32, (inner.shape[0], 128), 1))


def expert_grads(rows, hidden, da, db, df, dgate, dup, ddown):
    @pl.when(pl.program_id(0) == 0)
    def _():
        dgate[...] = jnp.zeros_like(dgate)
        dup[...] = jnp.zeros_like(dup)
        ddown[...] = jnp.zeros_like(ddown)

    dgate[0, 0] += dot(rows, da[...], COLS_BY_COLS)
    dup[0, 0] += dot(rows, db[...], COLS_BY_COLS)
    ddown[0, 0] += dot(hidden, df[...], COLS_BY_COLS)


def expert_grads_second(level, rows, hidden, da, db, df, gates, down_w, dgate, dup, ddown, shares):
    gate = row_sum(gates[...].astype(F32))
    low = hidden[...]
    share = dot(low, down_w[...]) * gate
    for place in range(E):
        shares[place, 0] = share[place * CAP : (place + 1) * CAP].astype(BF16)
    scaled = (rows[...].astype(F32) * gate).astype(BF16)
    expert_grads(scaled, (low.astype(F32) * gate).astype(BF16), da, db, df, dgate, dup, ddown)


def expert_grads_first(rows, hidden, da, db, df, *refs):
    expert_grads(rows[...], hidden[...], da, db, df, *refs[3:])


def mixture_back(layer, grad, dgates, dlogits_extra, y, z, moe_gain, routes_col, const_value, small, at):
    middle, logits = y[...], z[...]
    u = middle * lax.rsqrt(row_mean(middle * middle) + EPSILON) * moe_gain
    routes = [routes_col[:, 2 * layer + r : 2 * layer + r + 1] for r in range(2)]
    gates = gate_pair(logits, *routes)
    blends = blend_pairs(logits)
    by_u = row_sum(grad * u)
    by_const = [row_sum(grad * const_value[c : c + 1, :]) for c in range(NC)]
    dgates = list(dgates)
    for r in range(2):
        dgates[r] = dgates[r] + jnp.where(routes[r] == E + 1, by_u, 0.0)
        for c in range(NC):
            value = blends[c][0] * by_u + blends[c][1] * by_const[c]
            dgates[r] = dgates[r] + jnp.where(routes[r] == E + 2 + c, value, 0.0)
    mean = gates[0] * dgates[0] + gates[1] * dgates[1]
    lane = lax.broadcasted_iota(jnp.int32, logits.shape, 1)
    dlogits = jnp.zeros_like(logits)
    for r in range(2):
        dlogits = jnp.where(lane == routes[r], gates[r] * (dgates[r] - mean), dlogits)
    base = ZW - 2 * NC
    for c in range(NC):
        weight = chosen_weight(gates, routes, E + 2 + c)
        first, second = weight * by_u, weight * by_const[c]
        mean = blends[c][0] * first + blends[c][1] * second
        dlogits = jnp.where(lane == base + 2 * c, blends[c][0] * (first - mean), dlogits)
        dlogits = jnp.where(lane == base + 2 * c + 1, blends[c][1] * (second - mean), dlogits)
        used = jnp.sum(weight * blends[c][1] * grad, 0, keepdims=True)
        small[at + ZW + c : at + ZW + c + 1, :] = used
    if dlogits_extra is not None:
        dlogits = dlogits + dlogits_extra
    small[at : at + ZW, :] = dot(dlogits, u, COLS_BY_COLS, TOP)
    return dlogits


def backward_layer(
    layer, start, grad, dlogits, dexpert, y, x, z, q, k, v, stat, routes_col, mix_rows, attn_gain, moe_gain, weights, back,
    cosine, signed_sine,
    dx_out, normed_out, dpacked, dy_out, dgains,
):
    tokens, width = x.shape
    scale = HD**-0.5
    middle, logits = y[...], z[...]
    inv_y = lax.rsqrt(row_mean(middle * middle) + EPSILON)
    unit = middle * inv_y
    routes = [routes_col[:, 2 * layer + r : 2 * layer + r + 1] for r in range(2)]
    of_u, _ = mix_weights(gate_pair(logits, *routes), routes, blend_pairs(logits))
    du = of_u * grad + dexpert + dot(dlogits, mix_rows[...], precision=TOP)
    dunit = du * moe_gain
    dmiddle = grad + inv_y * dunit - unit * (inv_y * row_mean(dunit * unit))
    dgains[...] = jnp.zeros_like(dgains)
    dgains[1:2, :] = jnp.sum(du * unit, 0, keepdims=True)
    dy_low = dmiddle.astype(BF16)
    dy_out[...] = dy_low
    dy_out.flush()
    dattended = restore(dot(dy_low, weights[:, 3 * width : 4 * width], ROWS_BY_ROWS).astype(BF16), back)
    allowed = span_mask(tokens, start)
    masks = head_masks(tokens)
    for pair in range(H // 2):
        at = slice(128 * pair, 128 * pair + 128)
        queries, keys, values, dattn = q[:, at], k[:, at], v[:, at], dattended[:, at]
        dq = jnp.zeros((tokens, 128), F32)
        dk = jnp.zeros((tokens, 128), F32)
        dv = jnp.zeros((tokens, 128), F32)
        for side in range(2):
            mine = masks[side]
            head = 2 * pair + side
            my_queries = jnp.where(mine, queries, 0)
            my_dattn = jnp.where(mine, dattn, 0)
            scores = dot(my_queries, keys, ROWS_BY_ROWS) * scale
            scores = jnp.where(allowed, scores, NEGATIVE)
            probs = jnp.exp(scores - stat[:, head : head + 1]) * stat[:, 64 + head : 65 + head]
            dprobs = dot(my_dattn, values, ROWS_BY_ROWS)
            dscores = (probs * (dprobs - row_sum(probs * dprobs))).astype(BF16)
            dv = dv + dot(probs.astype(BF16), my_dattn, COLS_BY_COLS)
            dq = dq + dot(dscores, jnp.where(mine, keys, 0))
            dk = dk + dot(dscores, my_queries, COLS_BY_COLS)
        dq, dk = dq * scale, dk * scale
        dpacked[:, at] = (dq * cosine - swap_halves(dq) * signed_sine).astype(BF16)
        dpacked[:, width + 128 * pair : width + 128 * pair + 128] = (
            dk * cosine - swap_halves(dk) * signed_sine
        ).astype(BF16)
        dpacked[:, 2 * width + 128 * pair : 2 * width + 128 * pair + 128] = dv.astype(BF16)
    dpacked.flush()
    dnormed = restore(dot(dpacked[...], weights[:, : 3 * width], ROWS_BY_ROWS), back)
    stream = x[...]
    inv_x = lax.rsqrt(row_mean(stream * stream) + EPSILON)
    unit = stream * inv_x
    normed_out[...] = (unit * attn_gain).astype(BF16)
    normed_out.flush()
    dgains[0:1, :] = jnp.sum(dnormed * unit, 0, keepdims=True)
    dunit = dnormed * attn_gain
    dx = dmiddle + inv_x * dunit - unit * (inv_x * row_mean(dunit * unit))
    dx_out[...] = dx
    dx_out.flush()
    return dx


def backward_second(
    start, dout, y, z, gains, routes_col, target_col, const_value, shares, mix_rows, carry, z0, order_col, stat, q, k, v,
    cosine, signed_sine, x, target_row, weights,
    dx_out, normed_out, dpacked, dy_out, dgains, small, dz0, slots,
):
    small[...] = jnp.zeros_like(small)
    grad = dout[...]
    totals = gather_shares(shares, target_col, 1)
    gates = gate_pair(z[...], routes_col[:, 2:3], routes_col[:, 3:4])
    width = x.shape[1]
    dexpert = gates[0] * totals[0][:, :width] + gates[1] * totals[1][:, :width]
    dgates = [row_sum(totals[r][:, width:]) for r in range(2)]
    dlogits = mixture_back(1, grad, dgates, None, y, z, gains[3:4, :], routes_col, const_value, small, 0)
    before = z0[...]
    dz0[...] = dot(dlogits, carry[...], ROWS_BY_ROWS, TOP)
    small[24 : 24 + ZW, 0:ZW] = dot(before, dlogits, COLS_BY_COLS, TOP)
    small.flush()
    dz0.flush()
    dx = backward_layer(
        1, start[0], grad, dlogits, dexpert, y, x, z, q, k, v, stat, routes_col, mix_rows, gains[2:3, :], gains[3:4, :],
        weights, gather_matrix(order_col[...]), cosine[...], signed_sine[...],
        dx_out, normed_out, dpacked, dy_out, dgains,
    )
    gates = gate_pair(before, routes_col[:, 0:1], routes_col[:, 1:2])
    rows = 0.0
    for r in range(2):
        spread = slot_matrix(target_row[r : r + 1, :]).astype(F32).astype(BF16)
        rows = rows + dot(spread, (gates[r] * dx).astype(BF16))
    rows = rows.astype(BF16)
    for holder in range(slots.shape[0]):
        slots[holder] = rows


def mixture_first(start, dout, y, z, gains, routes_col, const_value, picks, dz0, small1, dlogits_out, small):
    small[0:24, :] = jnp.zeros((24, small.shape[1]), F32)
    small[24:, :] = small1[...]
    grad = dout[...]
    dgates = [row_sum(grad * picks[r]) for r in range(2)]
    dlogits_out[...] = mixture_back(
        0, grad, dgates, dz0[...], y, z, gains[1:2, :], routes_col, const_value, small, 0
    )


def backward_first(
    start, dout, y, z, gains, routes_col, target_col, dlogits, mix_rows, shares, order_col, order, stat, q, k, v, cosine,
    signed_sine, x, o, weights,
    dx_out, *rest,
):
    grads, (normed, dpacked, dy, dgains) = rest[:8], rest[8:]
    totals = gather_shares(shares, target_col, 0)
    backward_layer(
        0, start[0], dout[...], dlogits[...], totals[0] + totals[1], y, x, z, q, k, v, stat, routes_col, mix_rows,
        gains[0:1, :], gains[1:2, :], weights, gather_matrix(order_col[...]), cosine[...], signed_sine[...],
        dx_out, Local(normed), Local(dpacked), Local(dy), dgains,
    )
    packet(normed, dpacked, o, dy, order, dgains, None, grads)


class Local:
    def __init__(self, local):
        self.local = local

    def __getitem__(self, index):
        return self.local[index]

    def __setitem__(self, index, value):
        self.local[index] = value

    def flush(self):
        pass


def projection_grads(start, normed, dpacked, o, dy, order, dgains, extra, *outs):
    packet(normed, dpacked, o, dy, order, dgains, extra, outs)


def packet(normed, dpacked, o, dy, order, dgains, extra, outs):
    width = normed.shape[1]
    places = spread_matrix(order[...])
    rows = width // len(outs)

    def store(first, part):
        low = part.astype(BF16)
        for i, out in enumerate(outs):
            out[:, first : first + part.shape[1]] = low[i * rows : (i + 1) * rows]

    sums = [dgains[...]] + ([] if extra is None else [extra[...]])
    sums.append(jnp.zeros((128 - sum(t.shape[0] for t in sums), width), F32))
    store(4 * width, dot(places, jnp.concatenate(sums, 0).astype(BF16), ((0,), (1,))))
    store(3 * width, dot(reorder(o[...], places), dy[...], COLS_BY_COLS))
    features = reorder(normed[...], places)
    for part in range(3):
        columns = slice(part * width, (part + 1) * width)
        store(part * width, dot(features, dpacked[:, columns], COLS_BY_COLS))


def rotated(shift, devices):
    return [(i, (i + shift) % devices) for i in range(devices)]


def flipped(bits, devices):
    return [(i, i ^ bits) for i in range(devices)]


def feature_order(width):
    devices = lax.axis_size("ep")
    levels = devices // 8
    rows = width // devices
    me = lax.axis_index("ep")
    place = jnp.arange(width, dtype=jnp.int32)
    inside, block = place % rows, place // rows
    level = (block % levels + me // 8) % levels
    chip = ((block // levels) % 4) ^ ((me // 2) % 4)
    core = (block // (4 * levels)) ^ (me % 2)
    return (((level * 4 + chip) * 2 + core) * rows + inside).reshape(1, width)


def plane_parts(block):
    devices = lax.axis_size("ep")
    return [block] + [lax.ppermute(block, "ep", rotated(-8 * d, devices)) for d in range(1, devices // 8)]


def gather_planes(block):
    return jnp.concatenate(plane_parts(block), 0)


def gather_plane(column, chips):
    return [lax.ppermute(column, "ep", flipped(2 * d, lax.axis_size("ep"))) for d in chips]


def gather_chip(near):
    return near + [lax.ppermute(piece, "ep", flipped(1, lax.axis_size("ep"))) for piece in near]


def sum_chips(pieces):
    devices = lax.axis_size("ep")
    totals = [None] * 4
    for d in (1, 2, 3, 0):
        far = lax.ppermute(pieces[4 + d], "ep", flipped(1, devices))
        totals[d] = pieces[d].astype(F32) + far.astype(F32)
    return totals[0], [total.astype(BF16) for total in totals[1:]]


def sum_plane(total, low):
    devices = lax.axis_size("ep")
    return total, [lax.ppermute(low[d - 1], "ep", flipped(2 * d, devices)) for d in range(1, 4)]


def sum_planes(total, chips):
    devices = lax.axis_size("ep")
    total = total + sum(part.astype(F32) for part in chips)
    levels = devices // 8
    rows = total.shape[0] // levels
    low = total.astype(BF16)
    planes = [
        lax.ppermute(low[d * rows : (d + 1) * rows], "ep", rotated(8 * d, devices)) for d in range(1, levels)
    ]
    return total[:rows] + sum(part.astype(F32) for part in planes)


def exchange(slots):
    return lax.all_to_all(slots, "ep", split_axis=0, concat_axis=0, tiled=True)


def by_blocks(rows_per_step, width):
    return pl.BlockSpec((rows_per_step, width), lambda i: (i, 0))


def shards(
    x_in,
    cotangent,
    attn_gain,
    w_qkv,
    w_out,
    moe_gain,
    w_router,
    w_carry,
    const_gate,
    const_value,
    exp_gate,
    exp_up,
    exp_down,
    routes,
    drop_order,
    image_start,
):
    devices = lax.axis_size("ep")
    holders = devices // E
    tokens, width = x_in.shape
    inner = exp_gate.shape[-1]
    total_rows = devices * CAP
    block = SLOTS
    steps = total_rows // block
    cosine, signed_sine = (jnp.asarray(t) for t in rope_tables(tokens))

    def beside(layer, extra):
        return jnp.concatenate([w_qkv[layer], w_out[layer]] + extra, 1)

    gain_columns = jnp.stack([attn_gain[0], moe_gain[0], attn_gain[1], moe_gain[1]], 1)
    gain_columns = jnp.pad(gain_columns, ((0, 0), (0, 124)))
    order = feature_order(width)
    order_col = order.reshape(width, 1)
    mix_rows = [
        jnp.concatenate([w_router[layer].T, const_gate[layer].reshape(2 * NC, width)], 0) for layer in range(LAYERS)
    ]
    carry = jnp.pad(w_carry, ((0, ZW - w_carry.shape[0]), (0, ZW - w_carry.shape[1])))

    routes_row = routes.transpose(0, 2, 1).reshape(2 * LAYERS, tokens)
    routes_col = routes.transpose(1, 0, 2).reshape(tokens, 2 * LAYERS)

    slots_shape = shaped((holders, SLOTS, width), BF16)
    flat = shaped((tokens, width), F32)
    flat_low = shaped((tokens, width), BF16)
    logits_shape = shaped((tokens, ZW), F32)
    stat_shape = shaped((tokens, 128), F32)
    scratch = [pltpu.VMEM((tokens, 3 * width), F32), pltpu.VMEM((tokens, width), BF16)]

    target_row, target_col, cot_low = pl.pallas_call(
        prep_kernel,
        out_shape=(
            shaped((2 * LAYERS, tokens), jnp.int32), shaped((tokens, 2 * LAYERS), jnp.int32),
            shaped((tokens, width + 128), BF16),
        ),
        compiler_params=params(),
        cost_estimate=cost(3),
        name="prep",
    )(routes_row, routes_col, drop_order, drop_order.reshape(tokens, 1), cotangent)

    def send(slots):
        return exchange(slots.reshape(devices, CAP, slots.shape[-1]))

    def in_plane(rows):
        groups = [list(range(E * i, E * i + E)) for i in range(holders)]
        back = lax.all_to_all(
            rows.reshape(E, holders * CAP, width), "ep", split_axis=0, concat_axis=0, tiled=True, axis_index_groups=groups
        )
        return back.reshape(rows.shape)

    column0, cot_low = lax.optimization_barrier((gather_planes(beside(0, [gain_columns])), cot_low))
    near0 = [column0] + gather_plane(column0, (1, 2, 3))
    cot_column = plane_parts(cot_low)
    near0, later = lax.optimization_barrier((near0, beside(1, [jnp.zeros_like(gain_columns)])))
    pieces0, cot_column = lax.optimization_barrier((gather_chip(near0), cot_column))
    column1 = plane_parts(later)
    q, k, v, stat, o, y, z, slots, gains = staged(
        forward_first, "forward_first", 10,
        (flat_low, flat_low, flat_low, stat_shape, flat_low, flat, logits_shape, slots_shape, shaped((8, width), F32)),
        image_start, (x_in, target_row, order, cosine, signed_sine, mix_rows[0]), pieces0, scratch,
    )
    y0, z0, attention0 = y, z, (stat, q, k, v)
    attended0 = o
    column1, slots = lax.optimization_barrier((column1, slots))
    column1 = jnp.concatenate(column1, 0)
    near1 = gather_plane(column1, (1, 2))

    def weight_specs(layer):
        return [
            pl.BlockSpec((None, None, width, inner), lambda i: (layer, 0, 0, 0)),
            pl.BlockSpec((None, None, width, inner), lambda i: (layer, 0, 0, 0)),
            pl.BlockSpec((None, None, inner, width), lambda i: (layer, 0, 0, 0)),
        ]

    rows0, near1, column1 = lax.optimization_barrier((send(slots).reshape(total_rows, width), near1, column1))
    pieces1 = gather_chip([column1] + near1 + gather_plane(column1, (3,)))
    gate_pre, up_pre, part = pl.pallas_call(
        experts_forward,
        grid=(steps,),
        in_specs=[by_blocks(block, width)] + weight_specs(0),
        out_specs=(by_blocks(block, inner), by_blocks(block, inner), by_blocks(block, width)),
        out_shape=(
            shaped((total_rows, inner), F32), shaped((total_rows, inner), F32), shaped((total_rows, width), BF16)
        ),
        compiler_params=params(),
        cost_estimate=cost(7),
        name="experts_forward",
    )(rows0, exp_gate, exp_up, exp_down)

    marks, part = lax.optimization_barrier((cot_column, part))
    place = (lax.axis_index("ep") % E).astype(jnp.int32)
    cot_slots = pl.pallas_call(
        spread_kernel,
        in_specs=[whole(pltpu.SMEM)] + [whole()] * holders,
        out_shape=shaped((E, holders, CAP, width), BF16),
        compiler_params=params(),
        cost_estimate=cost(4),
        name="spread",
    )(place.reshape(1), *marks)
    cot_back = jnp.stack(
        [cot_slots[0]] + [lax.ppermute(cot_slots[d], "ep", flipped(d, devices)) for d in range(1, E)]
    ).reshape(devices, CAP, width)
    block_of = jnp.arange(devices)
    level = (block_of // E + holders - lax.axis_index("ep") // E) % holders
    cot_rows = jnp.take(cot_back, jnp.bitwise_xor(block_of % E, place) * holders + level, axis=0)
    returned = send(part).reshape(holders, SLOTS, width)
    picks0, x1, q, k, v, stat, o, y1, z1, slots, gate_slots = staged(
        forward_second, "forward_second", 11,
        (
            shaped((2, tokens, width), F32), flat, flat_low, flat_low, flat_low, stat_shape, flat_low, flat, logits_shape,
            slots_shape, shaped((holders, SLOTS, 128), BF16),
        ),
        image_start,
        (
            returned, y0, z0, gains, const_value[0], routes_col, target_col, order, cosine, signed_sine, mix_rows[1], carry,
            target_row,
        ),
        pieces1, scratch,
    )
    attention1, attended1 = (stat, q, k, v), o

    cot_rows = cot_rows.reshape(total_rows, width)
    rows1, cot_rows = lax.optimization_barrier((send(slots).reshape(total_rows, width), cot_rows))
    low_inner = shaped((total_rows, inner), BF16)
    low_rows = shaped((total_rows, width), BF16)
    hidden1, da1, db1, du1 = pl.pallas_call(
        experts_both,
        grid=(steps,),
        in_specs=[by_blocks(block, width)] * 2 + weight_specs(1),
        out_specs=(
            by_blocks(block, inner), by_blocks(block, inner), by_blocks(block, inner), by_blocks(block, width + 128)
        ),
        out_shape=(low_inner, low_inner, low_inner, shaped((total_rows, width + 128), BF16)),
        compiler_params=params(),
        cost_estimate=cost(11),
        name="experts_both",
    )(rows1, cot_rows, exp_gate, exp_up, exp_down)

    shares1 = send(du1).reshape(holders, SLOTS, width + 128)
    gate_slots, shares1 = lax.optimization_barrier((gate_slots, shares1))
    gate_rows = send(gate_slots)
    packed_low = shaped((tokens, 3 * width), BF16)
    gains_shape = shaped((8, width), F32)
    dx1, normed1, dpacked1, dy1, dgains1, small1, dz0, df_slots = staged(
        backward_second, "backward_second", 16,
        (flat, flat_low, packed_low, flat_low, gains_shape, shaped((40, width), F32), logits_shape, slots_shape),
        image_start,
        (
            cotangent, y1, z1, gains, routes_col, target_col, const_value[1], shares1, mix_rows[1], carry, z0, order_col,
            *attention1, cosine, signed_sine, x1, target_row,
        ),
        pieces1,
    )
    piece = shaped((width // 8, 4 * width + 128), BF16)
    dlogits0, small = staged(
        mixture_first, "mixture_first", 4, (logits_shape, shaped((64, width), F32)),
        image_start, (dx1, y0, z0, gains, routes_col, const_value[0], picks0, dz0, small1),
    )
    grads1 = staged(
        projection_grads, "projection_grads", 6, (piece,) * 8,
        image_start, (normed1, dpacked1, attended1, dy1, order, dgains1, small),
    )
    total1, chips1 = sum_plane(*sum_chips(grads1))

    df_slots, gate_rows = lax.optimization_barrier((df_slots, gate_rows))
    df0 = send(df_slots).reshape(total_rows, width)
    hidden0, da0, db0, du0 = pl.pallas_call(
        experts_backward,
        grid=(steps,),
        in_specs=[by_blocks(block, width), by_blocks(block, inner), by_blocks(block, inner)] + weight_specs(0),
        out_specs=(
            by_blocks(block, inner), by_blocks(block, inner), by_blocks(block, inner), by_blocks(block, width)
        ),
        out_shape=(low_inner, low_inner, low_inner, low_rows),
        compiler_params=params(),
        cost_estimate=cost(9),
        name="experts_backward",
    )(df0, gate_pre, up_pre, exp_gate, exp_up, exp_down)
    shares0 = send(du0).reshape(holders, SLOTS, width)

    grad_shapes = (
        shaped((LAYERS, 1, width, inner), F32), shaped((LAYERS, 1, width, inner), F32),
        shaped((LAYERS, 1, inner, width), F32),
    )
    operands = (rows1, hidden1, da1, db1, cot_rows, gate_rows.reshape(total_rows, 128))
    *expert_parts, gated = pl.pallas_call(
        expert_grads_second,
        grid_spec=pltpu.PrefetchScalarGridSpec(
            num_scalar_prefetch=1,
            grid=(steps,),
            in_specs=[pl.BlockSpec((block, t.shape[1]), lambda i, level: (i, 0)) for t in operands]
            + [pl.BlockSpec((None, None, inner, width), lambda i, level: (1, 0, 0, 0))],
            out_specs=(
                pl.BlockSpec((1, 1, width, inner), lambda i, level: (1, 0, 0, 0)),
                pl.BlockSpec((1, 1, width, inner), lambda i, level: (1, 0, 0, 0)),
                pl.BlockSpec((1, 1, inner, width), lambda i, level: (1, 0, 0, 0)),
                pl.BlockSpec((E, 1, CAP, width), lambda i, level: (0, lax.rem(i + steps - level[0], steps), 0, 0)),
            ),
        ),
        out_shape=grad_shapes + (shaped((E, holders, CAP, width), BF16),),
        compiler_params=params(),
        cost_estimate=cost(9),
        name="expert_grads_second",
    )((lax.axis_index("ep") // E).astype(jnp.int32).reshape(1), *operands, exp_down)
    chips1, expert_parts = lax.optimization_barrier((chips1, expert_parts))
    reduced1 = sum_planes(total1, chips1)
    gated, shares0 = lax.optimization_barrier((gated, shares0))
    gated = in_plane(gated)
    grad_x, *grads0 = staged(
        backward_first, "backward_first", 1, (flat,) + (piece,) * 8,
        image_start,
        (
            dx1, y0, z0, gains, routes_col, target_col, dlogits0, mix_rows[0], shares0, order_col, order, *attention0, cosine,
            signed_sine, x_in, attended0,
        ),
        pieces0,
        [
            pltpu.VMEM((tokens, width), BF16), pltpu.VMEM((tokens, 3 * width), BF16), pltpu.VMEM((tokens, width), BF16),
            pltpu.VMEM((8, width), F32),
        ],
    )
    grads0, gated = lax.optimization_barrier((grads0, gated))
    (total0, low0), gated, mine, hidden0 = lax.optimization_barrier(
        (sum_chips(grads0), gated, reduced1[:, 4 * width :], hidden0)
    )
    total0, chips0 = sum_plane(total0, low0)
    operands = (rows0, hidden0, da0, db0, df0)
    expert_parts = pl.pallas_call(
        expert_grads_first,
        grid=(steps,),
        in_specs=[by_blocks(block, t.shape[1]) for t in operands] + [whole(pl.ANY)] * 3,
        out_specs=(
            pl.BlockSpec((1, 1, width, inner), lambda i: (0, 0, 0, 0)),
            pl.BlockSpec((1, 1, width, inner), lambda i: (0, 0, 0, 0)),
            pl.BlockSpec((1, 1, inner, width), lambda i: (0, 0, 0, 0)),
        ),
        out_shape=grad_shapes,
        input_output_aliases={5: 0, 6: 1, 7: 2},
        compiler_params=params(),
        cost_estimate=cost(9),
        name="expert_grads_first",
    )(*operands, *expert_parts)
    small = exchange(jnp.broadcast_to(mine[None], (devices,) + mine.shape))
    chips0, expert_parts, small = lax.optimization_barrier((chips0, expert_parts, small))
    reduced0 = sum_planes(total0, chips0)
    small = small.reshape(width, 128)[:, 8:72]

    mark_specs = [pl.BlockSpec((tokens, 128), lambda i: (0, width // 128)) for _ in cot_column]
    parts = pl.pallas_call(
        combine_kernel,
        grid=(1,),
        in_specs=[pl.BlockSpec((E, holders, CAP, width), lambda i: (0, 0, 0, 0))] + mark_specs,
        out_specs=tuple(pl.BlockSpec((tokens, width), lambda i: (0, 0)) for _ in cot_column),
        out_shape=(flat_low,) * holders,
        compiler_params=params(),
        cost_estimate=cost(5),
        name="combine",
    )(gated, *cot_column)
    parts = [parts[0]] + [lax.ppermute(parts[d], "ep", rotated(8 * d, devices)) for d in range(1, holders)]
    hidden_out = pl.pallas_call(
        final_kernel,
        out_shape=flat,
        compiler_params=params(),
        cost_estimate=cost(4),
        name="final",
    )(y1, z1, gains, const_value[1], routes_col, *parts)

    routers = w_router.shape[-1]
    across = small.T
    both = jnp.stack([across[0:24], across[24:48]])
    reduced = jnp.stack([reduced0, reduced1])
    return (
        hidden_out,
        grad_x,
        reduced[:, :, 4 * width],
        reduced[:, :, : 3 * width],
        reduced[:, :, 3 * width : 4 * width],
        reduced[:, :, 4 * width + 1],
        jnp.stack([small[:, :routers], small[:, 24 : 24 + routers]]),
        across[48 : 48 + routers, :routers],
        both[:, routers:ZW].reshape(LAYERS, NC, 2, width),
        both[:, ZW : ZW + NC],
        *expert_parts,
    )


def solution(mesh):
    in_specs = (
        P("ep", None),
        P("ep", None),
        P(None, "ep"),
        P(None, "ep", None),
        P(None, "ep", None),
        P(None, "ep"),
        P(),
        P(),
        P(),
        P(),
        P(None, "ep", None, None),
        P(None, "ep", None, None),
        P(None, "ep", None, None),
        P(None, "ep", None),
        P("ep", None),
        P("ep"),
    )
    out_specs = (
        P("ep", None),
        P("ep", None),
        P(None, "ep"),
        P(None, "ep", None),
        P(None, "ep", None),
        P(None, "ep"),
        P(),
        P(),
        P(),
        P(),
        P(None, "ep", None, None),
        P(None, "ep", None, None),
        P(None, "ep", None, None),
    )
    return jax.shard_map(shards, mesh=mesh, in_specs=in_specs, out_specs=out_specs, check_vma=False)
```

```python
from functools import partial

import jax
import jax.numpy as jnp
import numpy as np
from jax import lax
from jax.experimental import pallas as pl
from jax.experimental.pallas import tpu as pltpu
from jax.sharding import PartitionSpec as P

H = 12
HD = 64
E = 8
NC = 2
LAYERS = 2
SPAN = 128
CAP = 40
SLOTS = E * CAP
ZW = 16

EPSILON = 1e-06
NEGATIVE = -1e30
F32 = jnp.float32
BF16 = jnp.bfloat16
TOP = lax.Precision.HIGHEST
VMEM_LIMIT = 61 * 1024 * 1024


def whole(space=pltpu.VMEM):
    return pl.BlockSpec(memory_space=space)


def shaped(shape, dtype):
    return pltpu.HBM(shape, dtype)


def params(limit=VMEM_LIMIT):
    return pltpu.CompilerParams(vmem_limit_bytes=limit)


def far(*arrays):
    return [pltpu.with_memory_space_constraint(t, pltpu.HBM) for t in arrays]


def cost(microseconds):
    return pl.CostEstimate(
        flops=int(microseconds * 1e9), bytes_accessed=int(microseconds * 3e6), transcendentals=0
    )


class Lazy:
    def __init__(self, copies, local):
        self.copies, self.local = copies, local
        self.shape, self.dtype = local.shape, local.dtype
        for copy in copies:
            copy.start()

    def finish(self):
        for copy in self.copies:
            copy.wait()
        self.copies = []

    def __getitem__(self, index):
        self.finish()
        return self.local[index]


class Kept:
    def __init__(self, local, copy):
        self.local, self.copy, self.sent = local, copy, False
        self.shape, self.dtype = local.shape, local.dtype

    def __getitem__(self, index):
        return self.local[index]

    def __setitem__(self, index, value):
        self.local[index] = value

    def flush(self):
        if not self.sent:
            self.copy.start()
        self.sent = True


def staged(kernel, name, microseconds, outs, start, args, pieces=(), scratch=()):
    n_args, n_outs, n_pieces = len(args), len(outs), len(pieces)
    fixed = [pltpu.VMEM(t.shape, t.dtype) for t in args] + [pltpu.VMEM(t.shape, t.dtype) for t in outs]
    if pieces:
        rows, columns = pieces[0].shape
        fixed.append(pltpu.VMEM((rows * n_pieces, columns), pieces[0].dtype))
    fixed.append(pltpu.SemaphoreType.DMA((n_args + n_outs + n_pieces,)))

    def body(start_ref, *refs):
        arg_refs, refs = refs[:n_args], refs[n_args:]
        piece_refs, refs = refs[:n_pieces], refs[n_pieces:]
        out_refs, refs = refs[:n_outs], refs[n_outs:]
        local, rest = refs[: len(fixed)], refs[len(fixed) :]
        sems = local[-1]
        lazies = [
            Lazy([pltpu.make_async_copy(ref, local[i], sems.at[i])], local[i]) for i, ref in enumerate(arg_refs)
        ]
        kept = [
            Kept(local[n_args + i], pltpu.make_async_copy(local[n_args + i], ref, sems.at[n_args + i]))
            for i, ref in enumerate(out_refs)
        ]
        weights = []
        if pieces:
            target, first = local[-2], n_args + n_outs
            copies = [
                pltpu.make_async_copy(ref, target.at[pl.ds(i * rows, rows)], sems.at[first + i])
                for i, ref in enumerate(piece_refs)
            ]
            weights = [Lazy(copies, target)]
        kernel(start_ref, *lazies, *weights, *kept, *rest)
        for lazy in lazies + weights:
            lazy.finish()
        for out in kept:
            out.flush()
        for out in kept:
            out.copy.wait()

    return pl.pallas_call(
        body,
        in_specs=[whole(pltpu.SMEM)] + [whole(pl.ANY)] * (n_args + n_pieces),
        out_specs=tuple(whole(pl.ANY) for _ in outs),
        out_shape=tuple(outs),
        scratch_shapes=fixed + list(scratch),
        compiler_params=params(44 * 1024 * 1024),
        cost_estimate=cost(microseconds),
        name=name,
    )(start, *[t if t.ndim == 3 and t.dtype == BF16 else far(t)[0] for t in args], *far(*pieces))


def dot(a, b, dims=((1,), (0,)), precision=None):
    return lax.dot_general(a, b, (dims, ((), ())), precision=precision, preferred_element_type=F32)


ROWS_BY_ROWS = ((1,), (1,))
COLS_BY_COLS = ((0,), (0,))


def spread_matrix(order):
    feature = lax.broadcasted_iota(jnp.int32, (order.shape[1], order.shape[1]), 0)
    return (feature == order).astype(F32).astype(BF16)


def gather_matrix(order_col):
    feature = lax.broadcasted_iota(jnp.int32, (order_col.shape[0], order_col.shape[0]), 1)
    return (feature == order_col).astype(F32).astype(BF16)


def reorder(values, places):
    return dot(values, places).astype(BF16)


def restore(values, back):
    if values.dtype == BF16:
        return dot(values, back).astype(BF16)
    high = values.astype(BF16)
    low = (values - high.astype(F32)).astype(BF16)
    rows = values.shape[0]
    both = dot(jnp.concatenate([high, low], 0), back)
    return both[:rows] + both[rows:]


def rope_tables(length):
    position = np.arange(length).astype(np.float32)
    inverse = (10000.0 ** (-np.arange(HD // 2).astype(np.float32) * 2.0 / HD)).astype(np.float32)
    angles = (position[:, None] * inverse[None, :]).astype(np.float32)
    cosine, sine = np.cos(angles), np.sin(angles)
    return (
        np.concatenate([cosine] * 4, 1).astype(np.float32),
        np.concatenate([-sine, sine, -sine, sine], 1).astype(np.float32),
    )


def swap_halves(values):
    lane = lax.broadcasted_iota(jnp.int32, values.shape, 1)
    low = lane % HD < HD // 2
    return jnp.where(low, pltpu.roll(values, 128 - HD // 2, 1), pltpu.roll(values, HD // 2, 1))


def span_mask(length, start):
    query = lax.broadcasted_iota(jnp.int32, (length, length), 0)
    key = lax.broadcasted_iota(jnp.int32, (length, length), 1)
    in_query = (query >= start) & (query < start + SPAN)
    in_key = (key >= start) & (key < start + SPAN)
    return (key <= query) | (in_query & in_key)


def head_masks(length):
    lane = lax.broadcasted_iota(jnp.int32, (length, 2 * HD), 1)
    return (lane < HD, lane >= HD)


def row_mean(values):
    return jnp.mean(values, -1, keepdims=True)


def row_sum(values):
    return jnp.sum(values, -1, keepdims=True)


def slot_matrix(target_row):
    slot = lax.broadcasted_iota(jnp.int32, (SLOTS, target_row.shape[1]), 0)
    return slot == target_row


def pick_matrix(target_col):
    slot = lax.broadcasted_iota(jnp.int32, (target_col.shape[0], SLOTS), 1)
    return slot == target_col


def gate_pair(logits, first, second):
    lane = lax.broadcasted_iota(jnp.int32, logits.shape, 1)
    one = row_sum(jnp.where(lane == first, logits, 0.0))
    two = row_sum(jnp.where(lane == second, logits, 0.0))
    return soft_pair(one, two)


def soft_pair(one, two):
    top = jnp.maximum(one, two)
    one, two = jnp.exp(one - top), jnp.exp(two - top)
    total = one + two
    return one / total, two / total


def blend_pairs(logits):
    base = ZW - 2 * NC
    return [
        soft_pair(logits[:, base + 2 * c : base + 2 * c + 1], logits[:, base + 2 * c + 1 : base + 2 * c + 2])
        for c in range(NC)
    ]


def chosen_weight(gates, routes, expert):
    return sum(jnp.where(route == expert, gate, 0.0) for gate, route in zip(gates, routes))


def mix_weights(gates, routes, blends):
    of_u = chosen_weight(gates, routes, E + 1)
    of_const = []
    for c in range(NC):
        weight = chosen_weight(gates, routes, E + 2 + c)
        of_u = of_u + weight * blends[c][0]
        of_const.append(weight * blends[c][1])
    return of_u, of_const


def prep_kernel(routes_row, routes_col, order_row, order_col, cot, target_row, target_col, cot_low):
    tokens = order_row.shape[1]
    earlier = jnp.where(order_row[...] < order_col[...], 1.0, 0.0).astype(BF16)
    later = jnp.where(order_col[...] < order_row[...], 1.0, 0.0).astype(BF16)
    lane = lax.broadcasted_iota(jnp.int32, (tokens, 128), 1)
    sub = lax.broadcasted_iota(jnp.int32, (16, tokens), 0)
    for layer in range(LAYERS):
        cols = [routes_col[:, 2 * layer + k : 2 * layer + k + 1] for k in range(2)]
        rows = [routes_row[2 * layer + k : 2 * layer + k + 1, :] for k in range(2)]
        wanted = jnp.where((lane == cols[0]) | (lane == cols[1]), 1.0, 0.0).astype(BF16)
        counts = dot(earlier, wanted)
        wanted_t = jnp.where((sub == rows[0]) | (sub == rows[1]), 1.0, 0.0).astype(BF16)
        counts_t = dot(wanted_t, later)
        for k in range(2):
            rank = row_sum(jnp.where(lane == cols[k], counts, 0.0)).astype(jnp.int32)
            kept = (cols[k] < E) & (rank < CAP)
            target_col[:, 2 * layer + k : 2 * layer + k + 1] = jnp.where(kept, cols[k] * CAP + rank, -1)
            rank_t = jnp.sum(jnp.where(sub == rows[k], counts_t, 0.0), 0, keepdims=True).astype(jnp.int32)
            kept_t = (rows[k] < E) & (rank_t < CAP)
            target_row[2 * layer + k : 2 * layer + k + 1, :] = jnp.where(kept_t, rows[k] * CAP + rank_t, -1)
    width = cot.shape[1]
    rows = cot[...].astype(BF16)
    marks = jnp.zeros((tokens, 128), F32)
    for k in range(2):
        last = 2 * (LAYERS - 1) + k
        target = target_col[:, last : last + 1]
        high = (target + 16) // 16 * 16 - 16
        marks = jnp.where(lane == 2 * k, high.astype(F32), marks)
        marks = jnp.where(lane == 2 * k + 1, (target - high).astype(F32), marks)
    for holder in range(cot_low.shape[0]):
        cot_low[holder, :, :width] = rows
        cot_low[holder, :, width:] = marks.astype(BF16)


def marked_slots(marks):
    taken = None
    for k in range(2):
        target = (marks[:, 2 * k : 2 * k + 1] + marks[:, 2 * k + 1 : 2 * k + 2]).astype(jnp.int32)
        mine = pick_matrix(target)
        taken = mine if taken is None else taken | mine
    return taken.astype(F32).astype(BF16)


def spread_kernel(place, *refs):
    sources, out = refs
    width = out.shape[3]
    for level in range(sources.shape[0]):
        source = sources.at[level]
        taken = marked_slots(source[:, width:].astype(F32))
        rows = dot(taken, source[:, :width], COLS_BY_COLS)
        for expert in range(E):
            out[jnp.bitwise_xor(expert, place[0]), level] = rows[expert * CAP : (expert + 1) * CAP].astype(BF16)


def combine_kernel(shares, *refs):
    sources, out = refs
    for level in range(sources.shape[0]):
        rows = shares[:, level].astype(F32).reshape(SLOTS, shares.shape[3]).astype(BF16)
        out[level] = dot(marked_slots(sources[level].astype(F32)), rows).astype(BF16)


def attend(x, attn_gain, weights, places, cosine, signed_sine, start, q, k, v, stat, o, packed, attended):
    tokens, width = x.shape
    scale = HD**-0.5
    normed = x * lax.rsqrt(row_mean(x * x) + EPSILON) * attn_gain
    packed[...] = dot(reorder(normed.astype(BF16), places), weights[:, : 3 * width])
    allowed = span_mask(tokens, start)
    masks = head_masks(tokens)
    lane = lax.broadcasted_iota(jnp.int32, (tokens, 128), 1)
    kept = jnp.zeros((tokens, 128), F32)
    for pair in range(H // 2):
        at = slice(128 * pair, 128 * pair + 128)
        turned = []
        for part in range(2):
            raw = packed[:, part * width + 128 * pair : part * width + 128 * pair + 128]
            turned.append((raw * cosine + swap_halves(raw) * signed_sine).astype(BF16))
        queries, keys = turned
        values = packed[:, 2 * width + 128 * pair : 2 * width + 128 * pair + 128].astype(BF16)
        q[:, at], k[:, at], v[:, at] = queries, keys, values
        total = jnp.zeros((tokens, 128), F32)
        for side in range(2):
            mine = masks[side]
            scores = dot(jnp.where(mine, queries, 0), keys, ROWS_BY_ROWS) * scale
            scores = jnp.where(allowed, scores, NEGATIVE)
            top = jnp.max(scores, -1, keepdims=True)
            probs = jnp.exp(scores - top)
            inverse = 1.0 / row_sum(probs)
            kept = jnp.where(lane == 2 * pair + side, top, kept)
            kept = jnp.where(lane == 64 + 2 * pair + side, inverse, kept)
            total = total + dot((probs * inverse).astype(BF16), jnp.where(mine, values, 0))
        attended[:, at] = total.astype(BF16)
    stat[...] = kept
    o[...] = attended[...]
    for out in (q, k, v, stat, o):
        out.flush()
    return x + dot(reorder(attended[...], places), weights[:, 3 * width : 4 * width])


def mix_in(y, moe_gain, mix_rows, target_row, z_extra):
    u = y * lax.rsqrt(row_mean(y * y) + EPSILON) * moe_gain
    logits = dot(u, mix_rows, ROWS_BY_ROWS, TOP)
    if z_extra is not None:
        logits = logits + z_extra
    spread = slot_matrix(target_row[0:1]) | slot_matrix(target_row[1:2])
    return u, logits, dot(spread.astype(F32).astype(BF16), u.astype(BF16)).astype(BF16)


def forward_first(
    start, x, target_row, order, cosine, signed_sine, mix_rows, weights, q, k, v, stat, o, y, z, slots, gains, packed, attended
):
    width = x.shape[1]
    places = spread_matrix(order[...])
    gain_rows = dot(weights[:, 4 * width :], places, ((0,), (1,)))[0:8, :]
    gains[...] = gain_rows
    gains.flush()
    middle = attend(
        x[...], gain_rows[0:1], weights, places, cosine[...], signed_sine[...], start[0], q, k, v, stat, o, packed, attended
    )
    y[...] = middle
    y.flush()
    u, logits, rows = mix_in(middle, gain_rows[1:2], mix_rows[...], target_row[0:2, :], None)
    z[...] = logits
    for holder in range(slots.shape[0]):
        slots[holder] = rows


def in_two(column, lane):
    high = column.astype(BF16).astype(F32)
    return jnp.where(lane == 0, high, jnp.where(lane == 1, column - high, 0.0)).astype(BF16)


def gather_shares(returned, target_col, layer):
    tokens = target_col.shape[0]
    both = jnp.concatenate(
        [pick_matrix(target_col[:, 2 * layer + k : 2 * layer + k + 1]).astype(F32) for k in range(2)], 0
    ).astype(BF16)
    total = sum(dot(both, returned[holder]) for holder in range(returned.shape[0]))
    return [total[:tokens], total[tokens:]]


def gather_sum(returned, target_col, layer):
    picked = [pick_matrix(target_col[:, 2 * layer + k : 2 * layer + k + 1]) for k in range(2)]
    picked = (picked[0] | picked[1]).astype(F32).astype(BF16)
    return sum(dot(picked, returned[holder]) for holder in range(returned.shape[0]))


def mixed_stream(y, u, logits, routes, const_value, picks):
    gates = gate_pair(logits, *routes)
    of_u, of_const = mix_weights(gates, routes, blend_pairs(logits))
    stream = y + of_u * u
    for c in range(NC):
        stream = stream + of_const[c] * const_value[c : c + 1, :]
    return stream if picks is None else stream + gates[0] * picks[0] + gates[1] * picks[1]


def forward_second(
    start, returned, y0, z0, gains, const_value0, routes_col, target_col, order, cosine, signed_sine, mix_rows, carry,
    target_row, weights,
    picks0, x1, q, k, v, stat, o, y, z, slots, gate_slots, packed, attended,
):
    y_first, logits_first = y0[...], z0[...]
    u_first = y_first * lax.rsqrt(row_mean(y_first * y_first) + EPSILON) * gains[1:2, :]
    routes = [routes_col[:, k : k + 1] for k in range(2)]
    picks = gather_shares(returned, target_col, 0)
    picks0[0], picks0[1] = picks
    picks0.flush()
    stream = mixed_stream(y_first, u_first, logits_first, routes, const_value0[...], picks)
    x1[...] = stream
    x1.flush()
    places = spread_matrix(order[...])
    middle = attend(
        stream, gains[2:3, :], weights, places, cosine[...], signed_sine[...], start[0], q, k, v, stat, o, packed, attended
    )
    y[...] = middle
    y.flush()
    z_extra = dot(logits_first, carry[...], precision=TOP)
    u, logits, rows = mix_in(middle, gains[3:4, :], mix_rows[...], target_row[2:4, :], z_extra)
    z[...] = logits
    for holder in range(slots.shape[0]):
        slots[holder] = rows
    slots.flush()
    gates = gate_pair(logits, routes_col[:, 2:3], routes_col[:, 3:4])
    lane = lax.broadcasted_iota(jnp.int32, (x1.shape[0], 128), 1)
    of_slots = 0.0
    for r in range(2):
        spread = slot_matrix(target_row[2 + r : 3 + r, :]).astype(F32).astype(BF16)
        of_slots = of_slots + dot(spread, in_two(gates[r], lane))
    for holder in range(gate_slots.shape[0]):
        gate_slots[holder] = of_slots.astype(BF16)


def final_kernel(y, z, gains, const_value, routes_col, parts, out):
    middle, logits = y[...], z[...]
    u = middle * lax.rsqrt(row_mean(middle * middle) + EPSILON) * gains[3:4, :]
    routes = [routes_col[:, 2 + k : 3 + k] for k in range(2)]
    stream = middle + sum(parts[level].astype(F32) for level in range(parts.shape[0]))
    out[...] = mixed_stream(stream, u, logits, routes, const_value[...], None)


def experts_forward(rows, gate_w, up_w, down_w, gate_pre, up_pre, part):
    a = dot(rows[...], gate_w[...])
    b = dot(rows[...], up_w[...])
    gate_pre[...] = a
    up_pre[...] = b
    hidden = (a / (1.0 + jnp.exp(-a)) * b).astype(BF16)
    part[...] = dot(hidden, down_w[...]).astype(BF16)


def expert_back(a, b, df, gate_w, up_w, down_w, hidden, da, db):
    dh = dot(df, down_w[...], ROWS_BY_ROWS)
    sig = 1.0 / (1.0 + jnp.exp(-a))
    act = a * sig
    hidden_low = (act * b).astype(BF16)
    hidden[...] = hidden_low
    da_low = (dh * b * sig * (1.0 + a * (1.0 - sig))).astype(BF16)
    db_low = (dh * act).astype(BF16)
    da[...] = da_low
    db[...] = db_low
    du = dot(da_low, gate_w[...], ROWS_BY_ROWS) + dot(db_low, up_w[...], ROWS_BY_ROWS)
    return hidden_low, du.astype(BF16)


def experts_backward(df, gate_pre, up_pre, gate_w, up_w, down_w, hidden, da, db, du):
    du[...] = expert_back(gate_pre[...], up_pre[...], df[...], gate_w, up_w, down_w, hidden, da, db)[1]


def in_order(pieces, place):
    for bit in (1, 2, 4):
        flip = jnp.bitwise_and(place, bit) != 0
        pieces = [jnp.where(flip, pieces[i ^ bit], pieces[i]) for i in range(E)]
    return pieces


def experts_both(place, rows, *refs):
    pieces, (gate_w, up_w, down_w, hidden, da, db, du, cot) = refs[:E], refs[E:]
    width = rows.shape[1]
    pieces = in_order([piece[...].reshape(CAP, width).astype(F32) for piece in pieces], place[0])
    cot[...] = jnp.concatenate(pieces, 0).astype(BF16)
    a = dot(rows[...], gate_w[...])
    b = dot(rows[...], up_w[...])
    hidden_low, du_low = expert_back(a, b, cot[...], gate_w, up_w, down_w, hidden, da, db)
    share = dot(hidden_low, down_w[...]).astype(BF16)
    du[:, :width] = du_low
    inner = row_sum(share.astype(F32) * cot[...].astype(F32))
    du[:, width:] = in_two(inner, lax.broadcasted_iota(jnp.int32, (inner.shape[0], 128), 1))


def expert_grads(rows, hidden, da, db, df, dgate, dup, ddown):
    @pl.when(pl.program_id(0) == 0)
    def _():
        dgate[...] = jnp.zeros_like(dgate)
        dup[...] = jnp.zeros_like(dup)
        ddown[...] = jnp.zeros_like(ddown)

    dgate[0, 0] += dot(rows, da[...], COLS_BY_COLS)
    dup[0, 0] += dot(rows, db[...], COLS_BY_COLS)
    ddown[0, 0] += dot(hidden, df[...], COLS_BY_COLS)


def expert_grads_second(rows, hidden, da, db, df, gates, down_w, dgate, dup, ddown, shares):
    gate = row_sum(gates[...].astype(F32))
    low = hidden[...]
    share = dot(low, down_w[...]) * gate
    for place in range(E):
        shares[place, 0] = share[place * CAP : (place + 1) * CAP].astype(BF16)
    scaled = (rows[...].astype(F32) * gate).astype(BF16)
    expert_grads(scaled, (low.astype(F32) * gate).astype(BF16), da, db, df, dgate, dup, ddown)


def expert_grads_first(rows, hidden, da, db, df, *refs):
    expert_grads(rows[...], hidden[...], da, db, df, *refs[3:])


def mixture_back(layer, grad, dgates, dlogits_extra, y, z, moe_gain, routes_col, const_value):
    middle, logits = y[...], z[...]
    u = middle * lax.rsqrt(row_mean(middle * middle) + EPSILON) * moe_gain
    routes = [routes_col[:, 2 * layer + r : 2 * layer + r + 1] for r in range(2)]
    gates = gate_pair(logits, *routes)
    blends = blend_pairs(logits)
    by_u = row_sum(grad * u)
    by_const = [row_sum(grad * const_value[c : c + 1, :]) for c in range(NC)]
    dgates = list(dgates)
    for r in range(2):
        dgates[r] = dgates[r] + jnp.where(routes[r] == E + 1, by_u, 0.0)
        for c in range(NC):
            value = blends[c][0] * by_u + blends[c][1] * by_const[c]
            dgates[r] = dgates[r] + jnp.where(routes[r] == E + 2 + c, value, 0.0)
    mean = gates[0] * dgates[0] + gates[1] * dgates[1]
    lane = lax.broadcasted_iota(jnp.int32, logits.shape, 1)
    dlogits = jnp.zeros_like(logits)
    for r in range(2):
        dlogits = jnp.where(lane == routes[r], gates[r] * (dgates[r] - mean), dlogits)
    base = ZW - 2 * NC
    for c in range(NC):
        weight = chosen_weight(gates, routes, E + 2 + c)
        first, second = weight * by_u, weight * by_const[c]
        mean = blends[c][0] * first + blends[c][1] * second
        dlogits = jnp.where(lane == base + 2 * c, blends[c][0] * (first - mean), dlogits)
        dlogits = jnp.where(lane == base + 2 * c + 1, blends[c][1] * (second - mean), dlogits)
    return dlogits if dlogits_extra is None else dlogits + dlogits_extra


def mixture_grads(layer, grad, dlogits, y, z, moe_gain, routes_col, small, at):
    middle, logits = y[...], z[...]
    u = middle * lax.rsqrt(row_mean(middle * middle) + EPSILON) * moe_gain
    routes = [routes_col[:, 2 * layer + r : 2 * layer + r + 1] for r in range(2)]
    _, of_const = mix_weights(gate_pair(logits, *routes), routes, blend_pairs(logits))
    for c in range(NC):
        small[at + ZW + c : at + ZW + c + 1, :] = jnp.sum(of_const[c] * grad, 0, keepdims=True)
    small[at : at + ZW, :] = dot(dlogits, u, COLS_BY_COLS, TOP)


def backward_layer(
    layer, start, grad, dlogits, dexpert, y, x, z, q, k, v, stat, routes_col, mix_rows, attn_gain, moe_gain, weights, back,
    cosine, signed_sine,
    dx_out, normed_out, dpacked, dy_out, dgains,
):
    tokens, width = x.shape
    scale = HD**-0.5
    middle, logits = y[...], z[...]
    inv_y = lax.rsqrt(row_mean(middle * middle) + EPSILON)
    unit = middle * inv_y
    routes = [routes_col[:, 2 * layer + r : 2 * layer + r + 1] for r in range(2)]
    of_u, _ = mix_weights(gate_pair(logits, *routes), routes, blend_pairs(logits))
    du = of_u * grad + dexpert + dot(dlogits, mix_rows[...], precision=TOP)
    dunit = du * moe_gain
    dmiddle = grad + inv_y * dunit - unit * (inv_y * row_mean(dunit * unit))
    dgains[...] = jnp.zeros_like(dgains)
    dgains[1:2, :] = jnp.sum(du * unit, 0, keepdims=True)
    dy_low = dmiddle.astype(BF16)
    dy_out[...] = dy_low
    dy_out.flush()
    dattended = restore(dot(dy_low, weights[:, 3 * width : 4 * width], ROWS_BY_ROWS).astype(BF16), back)
    allowed = span_mask(tokens, start)
    masks = head_masks(tokens)
    for pair in range(H // 2):
        at = slice(128 * pair, 128 * pair + 128)
        queries, keys, values, dattn = q[:, at], k[:, at], v[:, at], dattended[:, at]
        dq = jnp.zeros((tokens, 128), F32)
        dk = jnp.zeros((tokens, 128), F32)
        dv = jnp.zeros((tokens, 128), F32)
        for side in range(2):
            mine = masks[side]
            head = 2 * pair + side
            my_queries = jnp.where(mine, queries, 0)
            my_dattn = jnp.where(mine, dattn, 0)
            scores = dot(my_queries, keys, ROWS_BY_ROWS) * scale
            scores = jnp.where(allowed, scores, NEGATIVE)
            probs = jnp.exp(scores - stat[:, head : head + 1]) * stat[:, 64 + head : 65 + head]
            dprobs = dot(my_dattn, values, ROWS_BY_ROWS)
            dscores = (probs * (dprobs - row_sum(probs * dprobs))).astype(BF16)
            dv = dv + dot(probs.astype(BF16), my_dattn, COLS_BY_COLS)
            dq = dq + dot(dscores, jnp.where(mine, keys, 0))
            dk = dk + dot(dscores, my_queries, COLS_BY_COLS)
        dq, dk = dq * scale, dk * scale
        dpacked[:, at] = (dq * cosine - swap_halves(dq) * signed_sine).astype(BF16)
        dpacked[:, width + 128 * pair : width + 128 * pair + 128] = (
            dk * cosine - swap_halves(dk) * signed_sine
        ).astype(BF16)
        dpacked[:, 2 * width + 128 * pair : 2 * width + 128 * pair + 128] = dv.astype(BF16)
    dpacked.flush()
    dnormed = restore(dot(dpacked[...], weights[:, : 3 * width], ROWS_BY_ROWS), back)
    stream = x[...]
    inv_x = lax.rsqrt(row_mean(stream * stream) + EPSILON)
    unit = stream * inv_x
    normed_out[...] = (unit * attn_gain).astype(BF16)
    normed_out.flush()
    dgains[0:1, :] = jnp.sum(dnormed * unit, 0, keepdims=True)
    dunit = dnormed * attn_gain
    dx = dmiddle + inv_x * dunit - unit * (inv_x * row_mean(dunit * unit))
    dx_out[...] = dx
    dx_out.flush()
    return dx


def backward_second(
    start, dout, y, z, gains, routes_col, target_col, const_value, shares, mix_rows, carry, z0, order_col, stat, q, k, v,
    cosine, signed_sine, x, target_row, weights,
    dx_out, normed_out, dpacked, dy_out, dgains, dlogits_out, dz0, slots,
):
    grad = dout[...]
    totals = gather_shares(shares, target_col, 1)
    gates = gate_pair(z[...], routes_col[:, 2:3], routes_col[:, 3:4])
    width = x.shape[1]
    dexpert = gates[0] * totals[0][:, :width] + gates[1] * totals[1][:, :width]
    dgates = [row_sum(totals[r][:, width:]) for r in range(2)]
    dlogits = mixture_back(1, grad, dgates, None, y, z, gains[3:4, :], routes_col, const_value)
    dlogits_out[...] = dlogits
    dz0[...] = dot(dlogits, carry[...], ROWS_BY_ROWS, TOP)
    dlogits_out.flush()
    dz0.flush()
    dx = backward_layer(
        1, start[0], grad, dlogits, dexpert, y, x, z, q, k, v, stat, routes_col, mix_rows, gains[2:3, :], gains[3:4, :],
        weights, gather_matrix(order_col[...]), cosine[...], signed_sine[...],
        dx_out, normed_out, dpacked, dy_out, dgains,
    )
    gates = gate_pair(z0[...], routes_col[:, 0:1], routes_col[:, 1:2])
    rows = 0.0
    for r in range(2):
        spread = slot_matrix(target_row[r : r + 1, :]).astype(F32).astype(BF16)
        rows = rows + dot(spread, (gates[r] * dx).astype(BF16))
    rows = rows.astype(BF16)
    for holder in range(slots.shape[0]):
        slots[holder] = rows


def mixture_first(
    start, dout, y, z, gains, routes_col, const_value, picks, dz0, cotangent, y1, z1, dlogits1, dlogits_out, small
):
    small[...] = jnp.zeros_like(small)
    grad = dout[...]
    dgates = [row_sum(grad * picks[r]) for r in range(2)]
    dlogits = mixture_back(0, grad, dgates, dz0[...], y, z, gains[1:2, :], routes_col, const_value)
    dlogits_out[...] = dlogits
    mixture_grads(0, grad, dlogits, y, z, gains[1:2, :], routes_col, small, 0)
    mixture_grads(1, cotangent[...], dlogits1[...], y1, z1, gains[3:4, :], routes_col, small, 24)
    small[48 : 48 + ZW, 0:ZW] = dot(z[...], dlogits1[...], COLS_BY_COLS, TOP)


def backward_first(
    start, dout, y, z, gains, routes_col, target_col, dlogits, mix_rows, shares, order_col, order, stat, q, k, v, cosine,
    signed_sine, x, o, weights,
    dx_out, *rest,
):
    grads, (normed, dpacked, dy, dgains) = rest[:8], rest[8:]
    backward_layer(
        0, start[0], dout[...], dlogits[...], gather_sum(shares, target_col, 0), y, x, z, q, k, v, stat, routes_col, mix_rows,
        gains[0:1, :], gains[1:2, :], weights, gather_matrix(order_col[...]), cosine[...], signed_sine[...],
        dx_out, Local(normed), Local(dpacked), Local(dy), dgains,
    )
    packet(normed, dpacked, o, dy, order, dgains, None, grads)


class Local:
    def __init__(self, local):
        self.local = local

    def __getitem__(self, index):
        return self.local[index]

    def __setitem__(self, index, value):
        self.local[index] = value

    def flush(self):
        pass


def projection_grads(start, normed, dpacked, o, dy, order, dgains, extra, *outs):
    packet(normed, dpacked, o, dy, order, dgains, extra, outs)


def packet(normed, dpacked, o, dy, order, dgains, extra, outs):
    width = normed.shape[1]
    places = spread_matrix(order[...])
    rows = width // len(outs)

    def store(first, part):
        low = part.astype(BF16)
        for i, out in enumerate(outs):
            out[:, first : first + part.shape[1]] = low[i * rows : (i + 1) * rows]

    sums = [dgains[...]] + ([] if extra is None else [extra[...]])
    sums.append(jnp.zeros((128 - sum(t.shape[0] for t in sums), width), F32))
    store(4 * width, dot(places, jnp.concatenate(sums, 0).astype(BF16), ((0,), (1,))))
    store(3 * width, dot(reorder(o[...], places), dy[...], COLS_BY_COLS))
    features = reorder(normed[...], places)
    for part in range(3):
        columns = slice(part * width, (part + 1) * width)
        store(part * width, dot(features, dpacked[:, columns], COLS_BY_COLS))


def rotated(shift, devices):
    return [(i, (i + shift) % devices) for i in range(devices)]


def flipped(bits, devices):
    return [(i, i ^ bits) for i in range(devices)]


def feature_order(width):
    devices = lax.axis_size("ep")
    levels = devices // 8
    rows = width // devices
    me = lax.axis_index("ep")
    place = jnp.arange(width, dtype=jnp.int32)
    inside, block = place % rows, place // rows
    level = (block % levels + me // 8) % levels
    chip = ((block // levels) % 4) ^ ((me // 2) % 4)
    core = (block // (4 * levels)) ^ (me % 2)
    return (((level * 4 + chip) * 2 + core) * rows + inside).reshape(1, width)


def plane_parts(block):
    devices = lax.axis_size("ep")
    return [block] + [lax.ppermute(block, "ep", rotated(-8 * d, devices)) for d in range(1, devices // 8)]


def gather_planes(block):
    return jnp.concatenate(plane_parts(block), 0)


def gather_plane(column, chips):
    return [lax.ppermute(column, "ep", flipped(2 * d, lax.axis_size("ep"))) for d in chips]


def gather_chip(near):
    return near + [lax.ppermute(piece, "ep", flipped(1, lax.axis_size("ep"))) for piece in near]


def sum_chips(pieces):
    devices = lax.axis_size("ep")
    totals = [None] * 4
    for d in (1, 2, 3, 0):
        far = lax.ppermute(pieces[4 + d], "ep", flipped(1, devices))
        totals[d] = pieces[d].astype(F32) + far.astype(F32)
    return totals[0], [total.astype(BF16) for total in totals[1:]]


def sum_plane(low, chips):
    return [lax.ppermute(part, "ep", flipped(2 * d, lax.axis_size("ep"))) for part, d in zip(low, chips)]


def sum_planes(total, chips):
    devices = lax.axis_size("ep")
    total = total + sum(part.astype(F32) for part in chips)
    levels = devices // 8
    rows = total.shape[0] // levels
    low = total.astype(BF16)
    planes = [
        lax.ppermute(low[d * rows : (d + 1) * rows], "ep", rotated(8 * d, devices)) for d in range(1, levels)
    ]
    return total[:rows] + sum(part.astype(F32) for part in planes)


def exchange(slots):
    return lax.all_to_all(slots, "ep", split_axis=0, concat_axis=0, tiled=True)


def by_blocks(rows_per_step, width):
    return pl.BlockSpec((rows_per_step, width), lambda i: (i, 0))


def shards(
    x_in,
    cotangent,
    attn_gain,
    w_qkv,
    w_out,
    moe_gain,
    w_router,
    w_carry,
    const_gate,
    const_value,
    exp_gate,
    exp_up,
    exp_down,
    routes,
    drop_order,
    image_start,
):
    devices = lax.axis_size("ep")
    holders = devices // E
    tokens, width = x_in.shape
    inner = exp_gate.shape[-1]
    total_rows = devices * CAP
    block = SLOTS
    steps = total_rows // block
    cosine, signed_sine = (jnp.asarray(t) for t in rope_tables(tokens))

    def beside(layer, extra):
        return jnp.concatenate([w_qkv[layer], w_out[layer]] + extra, 1)

    gain_columns = jnp.stack([attn_gain[0], moe_gain[0], attn_gain[1], moe_gain[1]], 1)
    gain_columns = jnp.pad(gain_columns, ((0, 0), (0, 124)))
    order = feature_order(width)
    order_col = order.reshape(width, 1)
    mix_rows = [
        jnp.concatenate([w_router[layer].T, const_gate[layer].reshape(2 * NC, width)], 0) for layer in range(LAYERS)
    ]
    carry = jnp.pad(w_carry, ((0, ZW - w_carry.shape[0]), (0, ZW - w_carry.shape[1])))

    routes_row = routes.transpose(0, 2, 1).reshape(2 * LAYERS, tokens)
    routes_col = routes.transpose(1, 0, 2).reshape(tokens, 2 * LAYERS)

    slots_shape = shaped((holders, SLOTS, width), BF16)
    flat = shaped((tokens, width), F32)
    flat_low = shaped((tokens, width), BF16)
    logits_shape = shaped((tokens, ZW), F32)
    stat_shape = shaped((tokens, 128), F32)
    scratch = [pltpu.VMEM((tokens, 3 * width), F32), pltpu.VMEM((tokens, width), BF16)]

    target_row, target_col, cot_low = pl.pallas_call(
        prep_kernel,
        out_shape=(
            shaped((2 * LAYERS, tokens), jnp.int32), shaped((tokens, 2 * LAYERS), jnp.int32),
            shaped((holders, tokens, width + 128), BF16),
        ),
        compiler_params=params(),
        cost_estimate=cost(3),
        name="prep",
    )(routes_row, routes_col, drop_order, drop_order.reshape(tokens, 1), cotangent)

    def send(slots):
        return exchange(slots.reshape(devices, CAP, slots.shape[-1]))

    def across_planes(rows):
        groups = [list(range(i, devices, E)) for i in range(E)]
        return lax.all_to_all(rows, "ep", split_axis=0, concat_axis=0, tiled=True, axis_index_groups=groups)

    def in_plane(rows):
        groups = [list(range(E * i, E * i + E)) for i in range(holders)]
        back = lax.all_to_all(
            rows.reshape(E, holders * CAP, width), "ep", split_axis=0, concat_axis=0, tiled=True, axis_index_groups=groups
        )
        return back.reshape(rows.shape)

    column0, cot_low, later = lax.optimization_barrier(
        (gather_planes(beside(0, [gain_columns])), cot_low, beside(1, [jnp.zeros_like(gain_columns)]))
    )
    near0 = [column0] + gather_plane(column0, (1, 2, 3))
    cot_column = across_planes(cot_low)
    pieces0, cot_column = lax.optimization_barrier((gather_chip(near0), cot_column))
    column1 = plane_parts(later)
    q, k, v, stat, o, y, z, slots, gains = staged(
        forward_first, "forward_first", 10,
        (flat_low, flat_low, flat_low, stat_shape, flat_low, flat, logits_shape, slots_shape, shaped((8, width), F32)),
        image_start, (x_in, target_row, order, cosine, signed_sine, mix_rows[0]), pieces0, scratch,
    )
    y0, z0, attention0 = y, z, (stat, q, k, v)
    attended0 = o
    column1, slots = lax.optimization_barrier((column1, slots))
    column1 = jnp.concatenate(column1, 0)
    near1 = gather_plane(column1, (1, 2))

    def weight_specs(layer):
        return [
            pl.BlockSpec((None, None, width, inner), lambda i: (layer, 0, 0, 0)),
            pl.BlockSpec((None, None, width, inner), lambda i: (layer, 0, 0, 0)),
            pl.BlockSpec((None, None, inner, width), lambda i: (layer, 0, 0, 0)),
        ]

    rows0, near1, column1 = lax.optimization_barrier((send(slots).reshape(total_rows, width), near1, column1))
    pieces1 = gather_chip([column1] + near1 + gather_plane(column1, (3,)))
    gate_pre, up_pre, part = pl.pallas_call(
        experts_forward,
        grid=(steps,),
        in_specs=[by_blocks(block, width)] + weight_specs(0),
        out_specs=(by_blocks(block, inner), by_blocks(block, inner), by_blocks(block, width)),
        out_shape=(
            shaped((total_rows, inner), F32), shaped((total_rows, inner), F32), shaped((total_rows, width), BF16)
        ),
        compiler_params=params(24 * 1024 * 1024),
        cost_estimate=cost(7),
        name="experts_forward",
    )(rows0, *far(exp_gate, exp_up, exp_down))

    marks, part = lax.optimization_barrier((cot_column, part))
    place = (lax.axis_index("ep") % E).astype(jnp.int32)
    cot_slots = pl.pallas_call(
        spread_kernel,
        in_specs=[whole(pltpu.SMEM), whole()],
        out_shape=shaped((E, holders, CAP, width), BF16),
        compiler_params=params(),
        cost_estimate=cost(4),
        name="spread",
    )(place.reshape(1), marks)
    returned, cot_slots = lax.optimization_barrier((send(part).reshape(holders, SLOTS, width), cot_slots))
    picks0, x1, q, k, v, stat, o, y1, z1, slots, gate_slots = staged(
        forward_second, "forward_second", 11,
        (
            shaped((2, tokens, width), F32), flat, flat_low, flat_low, flat_low, stat_shape, flat_low, flat, logits_shape,
            slots_shape, shaped((holders, SLOTS, 128), BF16),
        ),
        image_start,
        (
            returned, y0, z0, gains, const_value[0], routes_col, target_col, order, cosine, signed_sine, mix_rows[1], carry,
            target_row,
        ),
        pieces1, scratch,
    )
    attention1, attended1 = (stat, q, k, v), o

    cot_back = [lax.ppermute(cot_slots[d], "ep", flipped(d, devices)) for d in range(1, E)]
    rows1, cot_back = lax.optimization_barrier((send(slots).reshape(total_rows, width), cot_back))
    low_inner = shaped((total_rows, inner), BF16)
    low_rows = shaped((total_rows, width), BF16)
    hidden1, da1, db1, du1, cot_rows = pl.pallas_call(
        experts_both,
        grid=(steps,),
        in_specs=[whole(pltpu.SMEM), by_blocks(block, width), pl.BlockSpec((1, 1, CAP, width), lambda i: (0, i, 0, 0))]
        + [pl.BlockSpec((1, CAP, width), lambda i: (i, 0, 0))] * (E - 1)
        + weight_specs(1),
        out_specs=(
            by_blocks(block, inner), by_blocks(block, inner), by_blocks(block, inner), by_blocks(block, width + 128),
            by_blocks(block, width),
        ),
        out_shape=(low_inner, low_inner, low_inner, shaped((total_rows, width + 128), BF16), low_rows),
        compiler_params=params(24 * 1024 * 1024),
        cost_estimate=cost(11),
        name="experts_both",
    )(place.reshape(1), rows1, *far(cot_slots, *cot_back, exp_gate, exp_up, exp_down))

    shares1 = send(du1).reshape(holders, SLOTS, width + 128)
    gate_slots, shares1 = lax.optimization_barrier((gate_slots, shares1))
    gate_rows = send(gate_slots)
    packed_low = shaped((tokens, 3 * width), BF16)
    gains_shape = shaped((8, width), F32)
    dx1, normed1, dpacked1, dy1, dgains1, dlogits1, dz0, df_slots = staged(
        backward_second, "backward_second", 16,
        (flat, flat_low, packed_low, flat_low, gains_shape, logits_shape, logits_shape, slots_shape),
        image_start,
        (
            cotangent, y1, z1, gains, routes_col, target_col, const_value[1], shares1, mix_rows[1], carry, z0, order_col,
            *attention1, cosine, signed_sine, x1, target_row,
        ),
        pieces1,
    )
    piece = shaped((width // 8, 4 * width + 128), BF16)
    dlogits0, small = staged(
        mixture_first, "mixture_first", 0.5, (logits_shape, shaped((64, width), F32)),
        image_start, (dx1, y0, z0, gains, routes_col, const_value[0], picks0, dz0, cotangent, y1, z1, dlogits1),
    )
    grads1 = staged(
        projection_grads, "projection_grads", 0.5, (piece,) * 8,
        image_start, (normed1, dpacked1, attended1, dy1, order, dgains1, small),
    )
    total1, low1 = sum_chips(grads1)
    chips1 = sum_plane(low1[:2], (1, 2))

    df_slots, gate_rows = lax.optimization_barrier((df_slots, gate_rows))
    df0 = send(df_slots).reshape(total_rows, width)
    df0, chips1, low1 = lax.optimization_barrier((df0, chips1, low1))
    chips1 += sum_plane(low1[2:], (3,))
    hidden0, da0, db0, du0 = pl.pallas_call(
        experts_backward,
        grid=(steps,),
        in_specs=[by_blocks(block, width), by_blocks(block, inner), by_blocks(block, inner)] + weight_specs(0),
        out_specs=(
            by_blocks(block, inner), by_blocks(block, inner), by_blocks(block, inner), by_blocks(block, width)
        ),
        out_shape=(low_inner, low_inner, low_inner, low_rows),
        compiler_params=params(24 * 1024 * 1024),
        cost_estimate=cost(9),
        name="experts_backward",
    )(df0, *far(gate_pre, up_pre, exp_gate, exp_up, exp_down))
    shares0 = send(du0).reshape(holders, SLOTS, width)

    grad_shapes = (
        shaped((LAYERS, 1, width, inner), F32), shaped((LAYERS, 1, width, inner), F32),
        shaped((LAYERS, 1, inner, width), F32),
    )
    operands = (rows1, hidden1, da1, db1, cot_rows, gate_rows.reshape(total_rows, 128))
    *expert_parts, gated = pl.pallas_call(
        expert_grads_second,
        grid_spec=pl.GridSpec(
            grid=(steps,),
            in_specs=[by_blocks(block, t.shape[1]) for t in operands] + weight_specs(1)[2:],
            out_specs=(
                pl.BlockSpec((1, 1, width, inner), lambda i: (1, 0, 0, 0)),
                pl.BlockSpec((1, 1, width, inner), lambda i: (1, 0, 0, 0)),
                pl.BlockSpec((1, 1, inner, width), lambda i: (1, 0, 0, 0)),
                pl.BlockSpec((E, 1, CAP, width), lambda i: (0, i, 0, 0)),
            ),
        ),
        out_shape=grad_shapes + (shaped((E, holders, CAP, width), BF16),),
        compiler_params=params(),
        cost_estimate=cost(9),
        name="expert_grads_second",
    )(*operands, exp_down)
    chips1, expert_parts = lax.optimization_barrier((chips1, expert_parts))
    reduced1 = sum_planes(total1, chips1)
    gated, shares0 = lax.optimization_barrier((gated, shares0))
    gated = in_plane(gated)
    grad_x, *grads0 = staged(
        backward_first, "backward_first", 1, (flat,) + (piece,) * 8,
        image_start,
        (
            dx1, y0, z0, gains, routes_col, target_col, dlogits0, mix_rows[0], shares0, order_col, order, *attention0, cosine,
            signed_sine, x_in, attended0,
        ),
        pieces0,
        [
            pltpu.VMEM((tokens, width), BF16), pltpu.VMEM((tokens, 3 * width), BF16), pltpu.VMEM((tokens, width), BF16),
            pltpu.VMEM((8, width), F32),
        ],
    )
    grads0, gated = lax.optimization_barrier((grads0, gated))
    (total0, low0), gated, mine, hidden0 = lax.optimization_barrier(
        (sum_chips(grads0), gated, reduced1[:, 4 * width :], hidden0)
    )
    chips0 = sum_plane(low0, (1, 2, 3))
    parts = pl.pallas_call(
        combine_kernel,
        grid=(1,),
        in_specs=[
            pl.BlockSpec((E, holders, CAP, width), lambda i: (0, 0, 0, 0)),
            pl.BlockSpec((holders, tokens, 128), lambda i: (0, 0, width // 128)),
        ],
        out_specs=pl.BlockSpec((holders, tokens, width), lambda i: (0, 0, 0)),
        out_shape=shaped((holders, tokens, width), BF16),
        compiler_params=params(),
        cost_estimate=cost(5),
        name="combine",
    )(gated, cot_column)
    parts, hidden0 = lax.optimization_barrier((parts, hidden0))
    operands = (rows0, hidden0, da0, db0, df0)
    expert_parts = pl.pallas_call(
        expert_grads_first,
        grid=(steps,),
        in_specs=[by_blocks(block, t.shape[1]) for t in operands] + [whole(pl.ANY)] * 3,
        out_specs=(
            pl.BlockSpec((1, 1, width, inner), lambda i: (0, 0, 0, 0)),
            pl.BlockSpec((1, 1, width, inner), lambda i: (0, 0, 0, 0)),
            pl.BlockSpec((1, 1, inner, width), lambda i: (0, 0, 0, 0)),
        ),
        out_shape=grad_shapes,
        input_output_aliases={5: 0, 6: 1, 7: 2},
        compiler_params=params(),
        cost_estimate=cost(9),
        name="expert_grads_first",
    )(*operands, *expert_parts)
    parts = across_planes(parts)
    mine, parts, chips0 = lax.optimization_barrier((mine, parts, chips0))
    reduced0 = sum_planes(total0, chips0)
    small = exchange(jnp.broadcast_to(mine[None], (devices,) + mine.shape)).reshape(width, 128)[:, 8:72]
    hidden_out = pl.pallas_call(
        final_kernel,
        out_shape=flat,
        compiler_params=params(),
        cost_estimate=cost(4),
        name="final",
    )(y1, z1, gains, const_value[1], routes_col, parts)

    routers = w_router.shape[-1]
    across = small.T
    both = jnp.stack([across[0:24], across[24:48]])
    reduced = jnp.stack([reduced0, reduced1])
    return (
        hidden_out,
        grad_x,
        reduced[:, :, 4 * width],
        reduced[:, :, : 3 * width],
        reduced[:, :, 3 * width : 4 * width],
        reduced[:, :, 4 * width + 1],
        jnp.stack([small[:, :routers], small[:, 24 : 24 + routers]]),
        across[48 : 48 + routers, :routers],
        both[:, routers:ZW].reshape(LAYERS, NC, 2, width),
        both[:, ZW : ZW + NC],
        *expert_parts,
    )


def solution(mesh):
    in_specs = (
        P("ep", None),
        P("ep", None),
        P(None, "ep"),
        P(None, "ep", None),
        P(None, "ep", None),
        P(None, "ep"),
        P(),
        P(),
        P(),
        P(),
        P(None, "ep", None, None),
        P(None, "ep", None, None),
        P(None, "ep", None, None),
        P(None, "ep", None),
        P("ep", None),
        P("ep"),
    )
    out_specs = (
        P("ep", None),
        P("ep", None),
        P(None, "ep"),
        P(None, "ep", None),
        P(None, "ep", None),
        P(None, "ep"),
        P(),
        P(),
        P(),
        P(),
        P(None, "ep", None, None),
        P(None, "ep", None, None),
        P(None, "ep", None, None),
    )
    return jax.shard_map(shards, mesh=mesh, in_specs=in_specs, out_specs=out_specs, check_vma=False)
```

```python
from functools import partial

import jax
import jax.numpy as jnp
import numpy as np
from jax import lax
from jax.experimental import pallas as pl
from jax.experimental.pallas import tpu as pltpu
from jax.sharding import PartitionSpec as P

H = 12
HD = 64
E = 8
NC = 2
LAYERS = 2
SPAN = 128
CAP = 40
SLOTS = E * CAP
ZW = 16

EPSILON = 1e-06
NEGATIVE = -1e30
F32 = jnp.float32
BF16 = jnp.bfloat16
TOP = lax.Precision.HIGHEST
VMEM_LIMIT = 61 * 1024 * 1024


def whole(space=pltpu.VMEM):
    return pl.BlockSpec(memory_space=space)


def shaped(shape, dtype):
    return pltpu.HBM(shape, dtype)


def params(limit=VMEM_LIMIT):
    return pltpu.CompilerParams(vmem_limit_bytes=limit)


def far(*arrays):
    return [pltpu.with_memory_space_constraint(t, pltpu.HBM) for t in arrays]


def cost(microseconds):
    return pl.CostEstimate(
        flops=int(microseconds * 1e9), bytes_accessed=int(microseconds * 3e6), transcendentals=0
    )


class Lazy:
    def __init__(self, copies, local):
        self.copies, self.local = copies, local
        self.shape, self.dtype = local.shape, local.dtype
        for copy in copies:
            copy.start()

    def finish(self):
        for copy in self.copies:
            copy.wait()
        self.copies = []

    def __getitem__(self, index):
        self.finish()
        return self.local[index]


class Kept:
    def __init__(self, local, copy):
        self.local, self.copy, self.sent = local, copy, False
        self.shape, self.dtype = local.shape, local.dtype

    def __getitem__(self, index):
        return self.local[index]

    def __setitem__(self, index, value):
        self.local[index] = value

    def flush(self):
        if not self.sent:
            self.copy.start()
        self.sent = True


def staged(kernel, name, microseconds, outs, start, args, pieces=(), scratch=()):
    n_args, n_outs, n_pieces = len(args), len(outs), len(pieces)
    fixed = [pltpu.VMEM(t.shape, t.dtype) for t in args] + [pltpu.VMEM(t.shape, t.dtype) for t in outs]
    if pieces:
        rows, columns = pieces[0].shape
        fixed.append(pltpu.VMEM((rows * n_pieces, columns), pieces[0].dtype))
    fixed.append(pltpu.SemaphoreType.DMA((n_args + n_outs + n_pieces,)))

    def body(start_ref, *refs):
        arg_refs, refs = refs[:n_args], refs[n_args:]
        piece_refs, refs = refs[:n_pieces], refs[n_pieces:]
        out_refs, refs = refs[:n_outs], refs[n_outs:]
        local, rest = refs[: len(fixed)], refs[len(fixed) :]
        sems = local[-1]
        lazies = [
            Lazy([pltpu.make_async_copy(ref, local[i], sems.at[i])], local[i]) for i, ref in enumerate(arg_refs)
        ]
        kept = [
            Kept(local[n_args + i], pltpu.make_async_copy(local[n_args + i], ref, sems.at[n_args + i]))
            for i, ref in enumerate(out_refs)
        ]
        weights = []
        if pieces:
            target, first = local[-2], n_args + n_outs
            copies = [
                pltpu.make_async_copy(ref, target.at[pl.ds(i * rows, rows)], sems.at[first + i])
                for i, ref in enumerate(piece_refs)
            ]
            weights = [Lazy(copies, target)]
        kernel(start_ref, *lazies, *weights, *kept, *rest)
        for lazy in lazies + weights:
            lazy.finish()
        for out in kept:
            out.flush()
        for out in kept:
            out.copy.wait()

    return pl.pallas_call(
        body,
        in_specs=[whole(pltpu.SMEM)] + [whole(pl.ANY)] * (n_args + n_pieces),
        out_specs=tuple(whole(pl.ANY) for _ in outs),
        out_shape=tuple(outs),
        scratch_shapes=fixed + list(scratch),
        compiler_params=params(44 * 1024 * 1024),
        cost_estimate=cost(microseconds),
        name=name,
    )(start, *[t if t.ndim == 3 and t.dtype == BF16 else far(t)[0] for t in args], *far(*pieces))


def dot(a, b, dims=((1,), (0,)), precision=None):
    return lax.dot_general(a, b, (dims, ((), ())), precision=precision, preferred_element_type=F32)


ROWS_BY_ROWS = ((1,), (1,))
COLS_BY_COLS = ((0,), (0,))


def spread_matrix(order):
    feature = lax.broadcasted_iota(jnp.int32, (order.shape[1], order.shape[1]), 0)
    return (feature == order).astype(F32).astype(BF16)


def gather_matrix(order_col):
    feature = lax.broadcasted_iota(jnp.int32, (order_col.shape[0], order_col.shape[0]), 1)
    return (feature == order_col).astype(F32).astype(BF16)


def reorder(values, places):
    return dot(values, places).astype(BF16)


def restore(values, back):
    if values.dtype == BF16:
        return dot(values, back).astype(BF16)
    high = values.astype(BF16)
    low = (values - high.astype(F32)).astype(BF16)
    rows = values.shape[0]
    both = dot(jnp.concatenate([high, low], 0), back)
    return both[:rows] + both[rows:]


def rope_tables(length):
    position = np.arange(length).astype(np.float32)
    inverse = (10000.0 ** (-np.arange(HD // 2).astype(np.float32) * 2.0 / HD)).astype(np.float32)
    angles = (position[:, None] * inverse[None, :]).astype(np.float32)
    cosine, sine = np.cos(angles), np.sin(angles)
    return (
        np.concatenate([cosine] * 4, 1).astype(np.float32),
        np.concatenate([-sine, sine, -sine, sine], 1).astype(np.float32),
    )


def swap_halves(values):
    lane = lax.broadcasted_iota(jnp.int32, values.shape, 1)
    low = lane % HD < HD // 2
    return jnp.where(low, pltpu.roll(values, 128 - HD // 2, 1), pltpu.roll(values, HD // 2, 1))


def span_mask(length, start):
    query = lax.broadcasted_iota(jnp.int32, (length, length), 0)
    key = lax.broadcasted_iota(jnp.int32, (length, length), 1)
    in_query = (query >= start) & (query < start + SPAN)
    in_key = (key >= start) & (key < start + SPAN)
    return (key <= query) | (in_query & in_key)


def head_masks(length):
    lane = lax.broadcasted_iota(jnp.int32, (length, 2 * HD), 1)
    return (lane < HD, lane >= HD)


def row_mean(values):
    return jnp.mean(values, -1, keepdims=True)


def row_sum(values):
    return jnp.sum(values, -1, keepdims=True)


def slot_matrix(target_row):
    slot = lax.broadcasted_iota(jnp.int32, (SLOTS, target_row.shape[1]), 0)
    return slot == target_row


def pick_matrix(target_col):
    slot = lax.broadcasted_iota(jnp.int32, (target_col.shape[0], SLOTS), 1)
    return slot == target_col


def gate_pair(logits, first, second):
    lane = lax.broadcasted_iota(jnp.int32, logits.shape, 1)
    one = row_sum(jnp.where(lane == first, logits, 0.0))
    two = row_sum(jnp.where(lane == second, logits, 0.0))
    return soft_pair(one, two)


def soft_pair(one, two):
    top = jnp.maximum(one, two)
    one, two = jnp.exp(one - top), jnp.exp(two - top)
    total = one + two
    return one / total, two / total


def blend_pairs(logits):
    base = ZW - 2 * NC
    return [
        soft_pair(logits[:, base + 2 * c : base + 2 * c + 1], logits[:, base + 2 * c + 1 : base + 2 * c + 2])
        for c in range(NC)
    ]


def chosen_weight(gates, routes, expert):
    return sum(jnp.where(route == expert, gate, 0.0) for gate, route in zip(gates, routes))


def mix_weights(gates, routes, blends):
    of_u = chosen_weight(gates, routes, E + 1)
    of_const = []
    for c in range(NC):
        weight = chosen_weight(gates, routes, E + 2 + c)
        of_u = of_u + weight * blends[c][0]
        of_const.append(weight * blends[c][1])
    return of_u, of_const


def prep_kernel(routes_row, routes_col, order_row, order_col, cot, target_row, target_col, cot_low):
    tokens = order_row.shape[1]
    earlier = jnp.where(order_row[...] < order_col[...], 1.0, 0.0).astype(BF16)
    later = jnp.where(order_col[...] < order_row[...], 1.0, 0.0).astype(BF16)
    lane = lax.broadcasted_iota(jnp.int32, (tokens, 128), 1)
    sub = lax.broadcasted_iota(jnp.int32, (16, tokens), 0)
    for layer in range(LAYERS):
        cols = [routes_col[:, 2 * layer + k : 2 * layer + k + 1] for k in range(2)]
        rows = [routes_row[2 * layer + k : 2 * layer + k + 1, :] for k in range(2)]
        wanted = jnp.where((lane == cols[0]) | (lane == cols[1]), 1.0, 0.0).astype(BF16)
        counts = dot(earlier, wanted)
        wanted_t = jnp.where((sub == rows[0]) | (sub == rows[1]), 1.0, 0.0).astype(BF16)
        counts_t = dot(wanted_t, later)
        for k in range(2):
            rank = row_sum(jnp.where(lane == cols[k], counts, 0.0)).astype(jnp.int32)
            kept = (cols[k] < E) & (rank < CAP)
            target_col[:, 2 * layer + k : 2 * layer + k + 1] = jnp.where(kept, cols[k] * CAP + rank, -1)
            rank_t = jnp.sum(jnp.where(sub == rows[k], counts_t, 0.0), 0, keepdims=True).astype(jnp.int32)
            kept_t = (rows[k] < E) & (rank_t < CAP)
            target_row[2 * layer + k : 2 * layer + k + 1, :] = jnp.where(kept_t, rows[k] * CAP + rank_t, -1)
    width = cot.shape[1]
    rows = cot[...].astype(BF16)
    marks = jnp.zeros((tokens, 128), F32)
    for k in range(2):
        last = 2 * (LAYERS - 1) + k
        target = target_col[:, last : last + 1]
        high = (target + 16) // 16 * 16 - 16
        marks = jnp.where(lane == 2 * k, high.astype(F32), marks)
        marks = jnp.where(lane == 2 * k + 1, (target - high).astype(F32), marks)
    for holder in range(cot_low.shape[0]):
        cot_low[holder, :, :width] = rows
        cot_low[holder, :, width:] = marks.astype(BF16)


def marked_slots(marks):
    taken = None
    for k in range(2):
        target = (marks[:, 2 * k : 2 * k + 1] + marks[:, 2 * k + 1 : 2 * k + 2]).astype(jnp.int32)
        mine = pick_matrix(target)
        taken = mine if taken is None else taken | mine
    return taken.astype(F32).astype(BF16)


def spread_kernel(place, *refs):
    sources, out = refs
    width = out.shape[3]
    for level in range(sources.shape[0]):
        source = sources.at[level]
        taken = marked_slots(source[:, width:].astype(F32))
        rows = dot(taken, source[:, :width], COLS_BY_COLS)
        for expert in range(E):
            out[jnp.bitwise_xor(expert, place[0]), level] = rows[expert * CAP : (expert + 1) * CAP].astype(BF16)


def combine_kernel(shares, *refs):
    sources, out = refs
    for level in range(sources.shape[0]):
        rows = shares[:, level].astype(F32).reshape(SLOTS, shares.shape[3]).astype(BF16)
        out[level] = dot(marked_slots(sources[level].astype(F32)), rows).astype(BF16)


def attend(x, attn_gain, weights, places, cosine, signed_sine, start, q, k, v, stat, o, packed, attended):
    tokens, width = x.shape
    scale = HD**-0.5
    normed = x * lax.rsqrt(row_mean(x * x) + EPSILON) * attn_gain
    packed[...] = dot(reorder(normed.astype(BF16), places), weights[:, : 3 * width])
    allowed = span_mask(tokens, start)
    masks = head_masks(tokens)
    lane = lax.broadcasted_iota(jnp.int32, (tokens, 128), 1)
    kept = jnp.zeros((tokens, 128), F32)
    for pair in range(H // 2):
        at = slice(128 * pair, 128 * pair + 128)
        turned = []
        for part in range(2):
            raw = packed[:, part * width + 128 * pair : part * width + 128 * pair + 128]
            turned.append((raw * cosine + swap_halves(raw) * signed_sine).astype(BF16))
        queries, keys = turned
        values = packed[:, 2 * width + 128 * pair : 2 * width + 128 * pair + 128].astype(BF16)
        q[:, at], k[:, at], v[:, at] = queries, keys, values
        total = jnp.zeros((tokens, 128), F32)
        for side in range(2):
            mine = masks[side]
            scores = dot(jnp.where(mine, queries, 0), keys, ROWS_BY_ROWS) * scale
            scores = jnp.where(allowed, scores, NEGATIVE)
            top = jnp.max(scores, -1, keepdims=True)
            probs = jnp.exp(scores - top)
            inverse = 1.0 / row_sum(probs)
            kept = jnp.where(lane == 2 * pair + side, top, kept)
            kept = jnp.where(lane == 64 + 2 * pair + side, inverse, kept)
            total = total + dot((probs * inverse).astype(BF16), jnp.where(mine, values, 0))
        attended[:, at] = total.astype(BF16)
    stat[...] = kept
    o[...] = attended[...]
    for out in (q, k, v, stat, o):
        out.flush()
    return x + dot(reorder(attended[...], places), weights[:, 3 * width : 4 * width])


def mix_in(y, moe_gain, mix_rows, target_row, z_extra):
    u = y * lax.rsqrt(row_mean(y * y) + EPSILON) * moe_gain
    logits = dot(u, mix_rows, ROWS_BY_ROWS, TOP)
    if z_extra is not None:
        logits = logits + z_extra
    spread = slot_matrix(target_row[0:1]) | slot_matrix(target_row[1:2])
    return u, logits, dot(spread.astype(F32).astype(BF16), u.astype(BF16)).astype(BF16)


def forward_first(
    start, x, target_row, order, cosine, signed_sine, mix_rows, weights, q, k, v, stat, o, y, z, slots, gains, packed, attended
):
    width = x.shape[1]
    places = spread_matrix(order[...])
    gain_rows = dot(weights[:, 4 * width :], places, ((0,), (1,)))[0:8, :]
    gains[...] = gain_rows
    gains.flush()
    middle = attend(
        x[...], gain_rows[0:1], weights, places, cosine[...], signed_sine[...], start[0], q, k, v, stat, o, packed, attended
    )
    y[...] = middle
    y.flush()
    u, logits, rows = mix_in(middle, gain_rows[1:2], mix_rows[...], target_row[0:2, :], None)
    z[...] = logits
    for holder in range(slots.shape[0]):
        slots[holder] = rows


def in_two(column, lane):
    high = column.astype(BF16).astype(F32)
    return jnp.where(lane == 0, high, jnp.where(lane == 1, column - high, 0.0)).astype(BF16)


def gather_shares(returned, target_col, layer):
    tokens = target_col.shape[0]
    both = jnp.concatenate(
        [pick_matrix(target_col[:, 2 * layer + k : 2 * layer + k + 1]).astype(F32) for k in range(2)], 0
    ).astype(BF16)
    holders = len(returned) if isinstance(returned, list) else returned.shape[0]
    total = sum(dot(both, returned[holder]) for holder in range(holders))
    return [total[:tokens], total[tokens:]]


def gather_sum(returned, target_col, layer):
    picked = [pick_matrix(target_col[:, 2 * layer + k : 2 * layer + k + 1]) for k in range(2)]
    picked = (picked[0] | picked[1]).astype(F32).astype(BF16)
    return sum(dot(picked, returned[holder]) for holder in range(returned.shape[0]))


def mixed_stream(y, u, logits, routes, const_value, picks):
    gates = gate_pair(logits, *routes)
    of_u, of_const = mix_weights(gates, routes, blend_pairs(logits))
    stream = y + of_u * u
    for c in range(NC):
        stream = stream + of_const[c] * const_value[c : c + 1, :]
    return stream if picks is None else stream + gates[0] * picks[0] + gates[1] * picks[1]


def forward_second(
    start, returned, y0, z0, gains, const_value0, routes_col, target_col, order, cosine, signed_sine, mix_rows, carry,
    target_row, weights,
    picks0, x1, q, k, v, stat, o, y, z, slots, gate_slots, packed, attended,
):
    y_first, logits_first = y0[...], z0[...]
    u_first = y_first * lax.rsqrt(row_mean(y_first * y_first) + EPSILON) * gains[1:2, :]
    routes = [routes_col[:, k : k + 1] for k in range(2)]
    picks = gather_shares(returned, target_col, 0)
    picks0[0], picks0[1] = picks
    picks0.flush()
    stream = mixed_stream(y_first, u_first, logits_first, routes, const_value0[...], picks)
    x1[...] = stream
    x1.flush()
    places = spread_matrix(order[...])
    middle = attend(
        stream, gains[2:3, :], weights, places, cosine[...], signed_sine[...], start[0], q, k, v, stat, o, packed, attended
    )
    y[...] = middle
    y.flush()
    z_extra = dot(logits_first, carry[...], precision=TOP)
    u, logits, rows = mix_in(middle, gains[3:4, :], mix_rows[...], target_row[2:4, :], z_extra)
    z[...] = logits
    for holder in range(slots.shape[0]):
        slots[holder] = rows
    slots.flush()
    gates = gate_pair(logits, routes_col[:, 2:3], routes_col[:, 3:4])
    lane = lax.broadcasted_iota(jnp.int32, (x1.shape[0], 128), 1)
    of_slots = 0.0
    for r in range(2):
        spread = slot_matrix(target_row[2 + r : 3 + r, :]).astype(F32).astype(BF16)
        of_slots = of_slots + dot(spread, in_two(gates[r], lane))
    for holder in range(gate_slots.shape[0]):
        gate_slots[holder] = of_slots.astype(BF16)


def final_kernel(y, z, gains, const_value, routes_col, parts, out):
    middle, logits = y[...], z[...]
    u = middle * lax.rsqrt(row_mean(middle * middle) + EPSILON) * gains[3:4, :]
    routes = [routes_col[:, 2 + k : 3 + k] for k in range(2)]
    stream = middle + sum(parts[level].astype(F32) for level in range(parts.shape[0]))
    out[...] = mixed_stream(stream, u, logits, routes, const_value[...], None)


def experts_forward(rows, gate_w, up_w, down_w, gate_pre, up_pre, part):
    a = dot(rows[...], gate_w[...])
    b = dot(rows[...], up_w[...])
    gate_pre[...] = a
    up_pre[...] = b
    hidden = (a / (1.0 + jnp.exp(-a)) * b).astype(BF16)
    part[...] = dot(hidden, down_w[...]).astype(BF16)


def expert_back(a, b, df, gate_w, up_w, down_w, hidden, da, db):
    dh = dot(df, down_w[...], ROWS_BY_ROWS)
    sig = 1.0 / (1.0 + jnp.exp(-a))
    act = a * sig
    hidden_low = (act * b).astype(BF16)
    hidden[...] = hidden_low
    da_low = (dh * b * sig * (1.0 + a * (1.0 - sig))).astype(BF16)
    db_low = (dh * act).astype(BF16)
    da[...] = da_low
    db[...] = db_low
    return hidden_low, dot(da_low, gate_w[...], ROWS_BY_ROWS) + dot(db_low, up_w[...], ROWS_BY_ROWS)


def experts_backward(df, gate_pre, up_pre, gate_w, up_w, down_w, hidden, da, db, du):
    rows = expert_back(gate_pre[...], up_pre[...], df[...], gate_w, up_w, down_w, hidden, da, db)[1]
    du[...] = rows.astype(BF16)


def in_order(pieces, place):
    for bit in (1, 2, 4):
        flip = jnp.bitwise_and(place, bit) != 0
        pieces = [jnp.where(flip, pieces[i ^ bit], pieces[i]) for i in range(E)]
    return pieces


def experts_both(place, rows, *refs):
    pieces, (gate_w, up_w, down_w, hidden, da, db, du, cot) = refs[:E], refs[E:]
    width = rows.shape[1]
    pieces = in_order([piece[...].reshape(CAP, width).astype(F32) for piece in pieces], place[0])
    cot[...] = jnp.concatenate(pieces, 0).astype(BF16)
    a = dot(rows[...], gate_w[...])
    b = dot(rows[...], up_w[...])
    hidden_low, du_rows = expert_back(a, b, cot[...], gate_w, up_w, down_w, hidden, da, db)
    share = dot(hidden_low, down_w[...]).astype(BF16)
    inner = row_sum(share.astype(F32) * cot[...].astype(F32))
    for to in range(E):
        mine = slice(to * CAP, (to + 1) * CAP)
        du[to] = narrow(du_rows[mine], inner[mine]).astype(BF16)


def narrow(rows, column):
    parts = [rows[:, i : i + 128] for i in range(0, rows.shape[1], 128)]
    lane = lax.broadcasted_iota(jnp.int32, (8, 128), 1)
    last = jnp.zeros((8, 128), F32)
    for i in range(CAP // 8):
        value = column[8 * i : 8 * i + 8]
        high = value.astype(BF16).astype(F32)
        last = jnp.where(lane == i, high, jnp.where(lane == 8 + i, value - high, last))
    return jnp.concatenate(parts + [last], 0)


def widen(block):
    return jnp.concatenate([block[i : i + CAP] for i in range(0, block.shape[0] - 8, CAP)], 1)


def expert_grads(rows, hidden, da, db, df, dgate, dup, ddown):
    @pl.when(pl.program_id(0) == 0)
    def _():
        dgate[...] = jnp.zeros_like(dgate)
        dup[...] = jnp.zeros_like(dup)
        ddown[...] = jnp.zeros_like(ddown)

    dgate[0, 0] += dot(rows, da[...], COLS_BY_COLS)
    dup[0, 0] += dot(rows, db[...], COLS_BY_COLS)
    ddown[0, 0] += dot(hidden, df[...], COLS_BY_COLS)


def expert_grads_second(rows, hidden, da, db, df, gates, down_w, dgate, dup, ddown, shares):
    gate = row_sum(gates[...].astype(F32))
    low = hidden[...]
    share = dot(low, down_w[...]) * gate
    for place in range(E):
        shares[place, 0] = share[place * CAP : (place + 1) * CAP].astype(BF16)
    scaled = (rows[...].astype(F32) * gate).astype(BF16)
    expert_grads(scaled, (low.astype(F32) * gate).astype(BF16), da, db, df, dgate, dup, ddown)


def expert_grads_first(rows, hidden, da, db, df, *refs):
    expert_grads(rows[...], hidden[...], da, db, df, *refs[3:])


def mixture_back(layer, grad, dgates, dlogits_extra, y, z, moe_gain, routes_col, const_value):
    middle, logits = y[...], z[...]
    u = middle * lax.rsqrt(row_mean(middle * middle) + EPSILON) * moe_gain
    routes = [routes_col[:, 2 * layer + r : 2 * layer + r + 1] for r in range(2)]
    gates = gate_pair(logits, *routes)
    blends = blend_pairs(logits)
    by_u = row_sum(grad * u)
    by_const = [row_sum(grad * const_value[c : c + 1, :]) for c in range(NC)]
    dgates = list(dgates)
    for r in range(2):
        dgates[r] = dgates[r] + jnp.where(routes[r] == E + 1, by_u, 0.0)
        for c in range(NC):
            value = blends[c][0] * by_u + blends[c][1] * by_const[c]
            dgates[r] = dgates[r] + jnp.where(routes[r] == E + 2 + c, value, 0.0)
    mean = gates[0] * dgates[0] + gates[1] * dgates[1]
    lane = lax.broadcasted_iota(jnp.int32, logits.shape, 1)
    dlogits = jnp.zeros_like(logits)
    for r in range(2):
        dlogits = jnp.where(lane == routes[r], gates[r] * (dgates[r] - mean), dlogits)
    base = ZW - 2 * NC
    for c in range(NC):
        weight = chosen_weight(gates, routes, E + 2 + c)
        first, second = weight * by_u, weight * by_const[c]
        mean = blends[c][0] * first + blends[c][1] * second
        dlogits = jnp.where(lane == base + 2 * c, blends[c][0] * (first - mean), dlogits)
        dlogits = jnp.where(lane == base + 2 * c + 1, blends[c][1] * (second - mean), dlogits)
    return dlogits if dlogits_extra is None else dlogits + dlogits_extra


def mixture_grads(layer, grad, dlogits, y, z, moe_gain, routes_col, small, at):
    middle, logits = y[...], z[...]
    u = middle * lax.rsqrt(row_mean(middle * middle) + EPSILON) * moe_gain
    routes = [routes_col[:, 2 * layer + r : 2 * layer + r + 1] for r in range(2)]
    _, of_const = mix_weights(gate_pair(logits, *routes), routes, blend_pairs(logits))
    for c in range(NC):
        small[at + ZW + c : at + ZW + c + 1, :] = jnp.sum(of_const[c] * grad, 0, keepdims=True)
    small[at : at + ZW, :] = dot(dlogits, u, COLS_BY_COLS, TOP)


def backward_layer(
    layer, start, grad, dlogits, dexpert, y, x, z, q, k, v, stat, routes_col, mix_rows, attn_gain, moe_gain, weights, back,
    cosine, signed_sine,
    dx_out, normed_out, dpacked, dy_out, dgains,
):
    tokens, width = x.shape
    scale = HD**-0.5
    middle, logits = y[...], z[...]
    inv_y = lax.rsqrt(row_mean(middle * middle) + EPSILON)
    unit = middle * inv_y
    routes = [routes_col[:, 2 * layer + r : 2 * layer + r + 1] for r in range(2)]
    of_u, _ = mix_weights(gate_pair(logits, *routes), routes, blend_pairs(logits))
    du = of_u * grad + dexpert + dot(dlogits, mix_rows[...], precision=TOP)
    dunit = du * moe_gain
    dmiddle = grad + inv_y * dunit - unit * (inv_y * row_mean(dunit * unit))
    dgains[...] = jnp.zeros_like(dgains)
    dgains[1:2, :] = jnp.sum(du * unit, 0, keepdims=True)
    dy_low = dmiddle.astype(BF16)
    dy_out[...] = dy_low
    dy_out.flush()
    dattended = restore(dot(dy_low, weights[:, 3 * width : 4 * width], ROWS_BY_ROWS).astype(BF16), back)
    allowed = span_mask(tokens, start)
    masks = head_masks(tokens)
    for pair in range(H // 2):
        at = slice(128 * pair, 128 * pair + 128)
        queries, keys, values, dattn = q[:, at], k[:, at], v[:, at], dattended[:, at]
        dq = jnp.zeros((tokens, 128), F32)
        dk = jnp.zeros((tokens, 128), F32)
        dv = jnp.zeros((tokens, 128), F32)
        for side in range(2):
            mine = masks[side]
            head = 2 * pair + side
            my_queries = jnp.where(mine, queries, 0)
            my_dattn = jnp.where(mine, dattn, 0)
            scores = dot(my_queries, keys, ROWS_BY_ROWS) * scale
            scores = jnp.where(allowed, scores, NEGATIVE)
            probs = jnp.exp(scores - stat[:, head : head + 1]) * stat[:, 64 + head : 65 + head]
            dprobs = dot(my_dattn, values, ROWS_BY_ROWS)
            dscores = (probs * (dprobs - row_sum(probs * dprobs))).astype(BF16)
            dv = dv + dot(probs.astype(BF16), my_dattn, COLS_BY_COLS)
            dq = dq + dot(dscores, jnp.where(mine, keys, 0))
            dk = dk + dot(dscores, my_queries, COLS_BY_COLS)
        dq, dk = dq * scale, dk * scale
        dpacked[:, at] = (dq * cosine - swap_halves(dq) * signed_sine).astype(BF16)
        dpacked[:, width + 128 * pair : width + 128 * pair + 128] = (
            dk * cosine - swap_halves(dk) * signed_sine
        ).astype(BF16)
        dpacked[:, 2 * width + 128 * pair : 2 * width + 128 * pair + 128] = dv.astype(BF16)
    dpacked.flush()
    dnormed = restore(dot(dpacked[...], weights[:, : 3 * width], ROWS_BY_ROWS), back)
    stream = x[...]
    inv_x = lax.rsqrt(row_mean(stream * stream) + EPSILON)
    unit = stream * inv_x
    normed_out[...] = (unit * attn_gain).astype(BF16)
    normed_out.flush()
    dgains[0:1, :] = jnp.sum(dnormed * unit, 0, keepdims=True)
    dunit = dnormed * attn_gain
    dx = dmiddle + inv_x * dunit - unit * (inv_x * row_mean(dunit * unit))
    dx_out[...] = dx
    dx_out.flush()
    return dx


def backward_second(
    start, dout, y, z, gains, routes_col, target_col, const_value, shares, mix_rows, carry, z0, order_col, stat, q, k, v,
    cosine, signed_sine, x, target_row, weights,
    dx_out, normed_out, dpacked, dy_out, dgains, dlogits_out, dz0, slots,
):
    grad = dout[...]
    blocks = [[shares[holder + e].astype(F32) for e in range(E)] for holder in range(0, shares.shape[0], E)]
    rows = [jnp.concatenate([widen(block) for block in held], 0).astype(BF16) for held in blocks]
    totals = gather_shares(rows, target_col, 1)
    gates = gate_pair(z[...], routes_col[:, 2:3], routes_col[:, 3:4])
    dexpert = gates[0] * totals[0] + gates[1] * totals[1]
    sums = [sum(held[e][-8:] for held in blocks) for e in range(E)]
    column = jnp.concatenate([t[:, i : i + 1] + t[:, 8 + i : 9 + i] for t in sums for i in range(CAP // 8)], 0)
    column = in_two(column, lax.broadcasted_iota(jnp.int32, (SLOTS, 128), 1))
    dgates = [row_sum(t) for t in gather_shares([column], target_col, 1)]
    dlogits = mixture_back(1, grad, dgates, None, y, z, gains[3:4, :], routes_col, const_value)
    dlogits_out[...] = dlogits
    dz0[...] = dot(dlogits, carry[...], ROWS_BY_ROWS, TOP)
    dlogits_out.flush()
    dz0.flush()
    dx = backward_layer(
        1, start[0], grad, dlogits, dexpert, y, x, z, q, k, v, stat, routes_col, mix_rows, gains[2:3, :], gains[3:4, :],
        weights, gather_matrix(order_col[...]), cosine[...], signed_sine[...],
        dx_out, normed_out, dpacked, dy_out, dgains,
    )
    gates = gate_pair(z0[...], routes_col[:, 0:1], routes_col[:, 1:2])
    rows = 0.0
    for r in range(2):
        spread = slot_matrix(target_row[r : r + 1, :]).astype(F32).astype(BF16)
        rows = rows + dot(spread, (gates[r] * dx).astype(BF16))
    rows = rows.astype(BF16)
    for holder in range(slots.shape[0]):
        slots[holder] = rows


def mixture_first(
    start, dout, y, z, gains, routes_col, const_value, picks, dz0, cotangent, y1, z1, dlogits1, dlogits_out, small
):
    small[...] = jnp.zeros_like(small)
    grad = dout[...]
    dgates = [row_sum(grad * picks[r]) for r in range(2)]
    dlogits = mixture_back(0, grad, dgates, dz0[...], y, z, gains[1:2, :], routes_col, const_value)
    dlogits_out[...] = dlogits
    mixture_grads(0, grad, dlogits, y, z, gains[1:2, :], routes_col, small, 0)
    mixture_grads(1, cotangent[...], dlogits1[...], y1, z1, gains[3:4, :], routes_col, small, 24)
    small[48 : 48 + ZW, 0:ZW] = dot(z[...], dlogits1[...], COLS_BY_COLS, TOP)


def backward_first(
    start, dout, y, z, gains, routes_col, target_col, dlogits, mix_rows, shares, order_col, order, stat, q, k, v, cosine,
    signed_sine, x, o, weights,
    dx_out, *rest,
):
    grads, (normed, dpacked, dy, dgains) = rest[:8], rest[8:]
    backward_layer(
        0, start[0], dout[...], dlogits[...], gather_sum(shares, target_col, 0), y, x, z, q, k, v, stat, routes_col, mix_rows,
        gains[0:1, :], gains[1:2, :], weights, gather_matrix(order_col[...]), cosine[...], signed_sine[...],
        dx_out, Local(normed), Local(dpacked), Local(dy), dgains,
    )
    packet(normed, dpacked, o, dy, order, dgains, None, grads)


class Local:
    def __init__(self, local):
        self.local = local

    def __getitem__(self, index):
        return self.local[index]

    def __setitem__(self, index, value):
        self.local[index] = value

    def flush(self):
        pass


def projection_grads(start, normed, dpacked, o, dy, order, dgains, extra, *outs):
    packet(normed, dpacked, o, dy, order, dgains, extra, outs)


def packet(normed, dpacked, o, dy, order, dgains, extra, outs):
    width = normed.shape[1]
    places = spread_matrix(order[...])
    rows = width // len(outs)

    def store(first, part):
        low = part.astype(BF16)
        for i, out in enumerate(outs):
            out[:, first : first + part.shape[1]] = low[i * rows : (i + 1) * rows]

    sums = [dgains[...]] + ([] if extra is None else [extra[...]])
    sums.append(jnp.zeros((128 - sum(t.shape[0] for t in sums), width), F32))
    store(4 * width, dot(places, jnp.concatenate(sums, 0).astype(BF16), ((0,), (1,))))
    store(3 * width, dot(reorder(o[...], places), dy[...], COLS_BY_COLS))
    features = reorder(normed[...], places)
    for part in range(3):
        columns = slice(part * width, (part + 1) * width)
        store(part * width, dot(features, dpacked[:, columns], COLS_BY_COLS))


def rotated(shift, devices):
    return [(i, (i + shift) % devices) for i in range(devices)]


def flipped(bits, devices):
    return [(i, i ^ bits) for i in range(devices)]


def feature_order(width):
    devices = lax.axis_size("ep")
    levels = devices // 8
    rows = width // devices
    me = lax.axis_index("ep")
    place = jnp.arange(width, dtype=jnp.int32)
    inside, block = place % rows, place // rows
    level = (block % levels + me // 8) % levels
    chip = ((block // levels) % 4) ^ ((me // 2) % 4)
    core = (block // (4 * levels)) ^ (me % 2)
    return (((level * 4 + chip) * 2 + core) * rows + inside).reshape(1, width)


def plane_parts(block):
    devices = lax.axis_size("ep")
    return [block] + [lax.ppermute(block, "ep", rotated(-8 * d, devices)) for d in range(1, devices // 8)]


def gather_planes(block):
    return jnp.concatenate(plane_parts(block), 0)


def gather_plane(column, chips):
    return [lax.ppermute(column, "ep", flipped(2 * d, lax.axis_size("ep"))) for d in chips]


def gather_chip(near):
    return near + [lax.ppermute(piece, "ep", flipped(1, lax.axis_size("ep"))) for piece in near]


def sum_chips(pieces):
    devices = lax.axis_size("ep")
    totals = [None] * 4
    for d in (1, 2, 3, 0):
        far = lax.ppermute(pieces[4 + d], "ep", flipped(1, devices))
        totals[d] = pieces[d].astype(F32) + far.astype(F32)
    return totals[0], [total.astype(BF16) for total in totals[1:]]


def sum_plane(low, chips):
    return [lax.ppermute(part, "ep", flipped(2 * d, lax.axis_size("ep"))) for part, d in zip(low, chips)]


def sum_planes(total, chips, beside=None):
    devices = lax.axis_size("ep")
    total = total + sum(part.astype(F32) for part in chips)
    levels = devices // 8
    rows = total.shape[0] // levels
    low = total.astype(BF16)
    if beside is not None:
        low, beside = lax.optimization_barrier((low, beside))
    planes = [
        lax.ppermute(low[d * rows : (d + 1) * rows], "ep", rotated(8 * d, devices)) for d in range(1, levels)
    ]
    total = total[:rows] + sum(part.astype(F32) for part in planes)
    return total if beside is None else (total, beside)


def exchange(slots):
    return lax.all_to_all(slots, "ep", split_axis=0, concat_axis=0, tiled=True)


def by_blocks(rows_per_step, width):
    return pl.BlockSpec((rows_per_step, width), lambda i: (i, 0))


def shards(
    x_in,
    cotangent,
    attn_gain,
    w_qkv,
    w_out,
    moe_gain,
    w_router,
    w_carry,
    const_gate,
    const_value,
    exp_gate,
    exp_up,
    exp_down,
    routes,
    drop_order,
    image_start,
):
    devices = lax.axis_size("ep")
    holders = devices // E
    tokens, width = x_in.shape
    inner = exp_gate.shape[-1]
    total_rows = devices * CAP
    block = SLOTS
    steps = total_rows // block
    cosine, signed_sine = (jnp.asarray(t) for t in rope_tables(tokens))

    def beside(layer, extra):
        return jnp.concatenate([w_qkv[layer], w_out[layer]] + extra, 1)

    gain_columns = jnp.stack([attn_gain[0], moe_gain[0], attn_gain[1], moe_gain[1]], 1)
    gain_columns = jnp.pad(gain_columns, ((0, 0), (0, 124)))
    order = feature_order(width)
    order_col = order.reshape(width, 1)
    mix_rows = [
        jnp.concatenate([w_router[layer].T, const_gate[layer].reshape(2 * NC, width)], 0) for layer in range(LAYERS)
    ]
    carry = jnp.pad(w_carry, ((0, ZW - w_carry.shape[0]), (0, ZW - w_carry.shape[1])))

    routes_row = routes.transpose(0, 2, 1).reshape(2 * LAYERS, tokens)
    routes_col = routes.transpose(1, 0, 2).reshape(tokens, 2 * LAYERS)

    slots_shape = shaped((holders, SLOTS, width), BF16)
    flat = shaped((tokens, width), F32)
    flat_low = shaped((tokens, width), BF16)
    logits_shape = shaped((tokens, ZW), F32)
    stat_shape = shaped((tokens, 128), F32)
    scratch = [pltpu.VMEM((tokens, 3 * width), F32), pltpu.VMEM((tokens, width), BF16)]

    target_row, target_col, cot_low = pl.pallas_call(
        prep_kernel,
        out_shape=(
            shaped((2 * LAYERS, tokens), jnp.int32), shaped((tokens, 2 * LAYERS), jnp.int32),
            shaped((holders, tokens, width + 128), BF16),
        ),
        compiler_params=params(),
        cost_estimate=cost(3),
        name="prep",
    )(routes_row, routes_col, drop_order, drop_order.reshape(tokens, 1), cotangent)

    def send(slots):
        return exchange(slots.reshape(devices, CAP, slots.shape[-1]))

    def across_planes(rows):
        groups = [list(range(i, devices, E)) for i in range(E)]
        return lax.all_to_all(rows, "ep", split_axis=0, concat_axis=0, tiled=True, axis_index_groups=groups)

    def in_plane(rows):
        groups = [list(range(E * i, E * i + E)) for i in range(holders)]
        back = lax.all_to_all(
            rows.reshape(E, holders * CAP, width), "ep", split_axis=0, concat_axis=0, tiled=True, axis_index_groups=groups
        )
        return back.reshape(rows.shape)

    column0, cot_low, later = lax.optimization_barrier(
        (gather_planes(beside(0, [gain_columns])), cot_low, beside(1, [jnp.zeros_like(gain_columns)]))
    )
    near0 = [column0] + gather_plane(column0, (1, 2, 3))
    cot_column = across_planes(cot_low)
    pieces0, cot_column = lax.optimization_barrier((gather_chip(near0), cot_column))
    column1 = plane_parts(later)
    q, k, v, stat, o, y, z, slots, gains = staged(
        forward_first, "forward_first", 10,
        (flat_low, flat_low, flat_low, stat_shape, flat_low, flat, logits_shape, slots_shape, shaped((8, width), F32)),
        image_start, (x_in, target_row, order, cosine, signed_sine, mix_rows[0]), pieces0, scratch,
    )
    y0, z0, attention0 = y, z, (stat, q, k, v)
    attended0 = o
    column1, slots = lax.optimization_barrier((column1, slots))
    column1 = jnp.concatenate(column1, 0)
    near1 = gather_plane(column1, (1, 2))

    def weight_specs(layer):
        return [
            pl.BlockSpec((None, None, width, inner), lambda i: (layer, 0, 0, 0)),
            pl.BlockSpec((None, None, width, inner), lambda i: (layer, 0, 0, 0)),
            pl.BlockSpec((None, None, inner, width), lambda i: (layer, 0, 0, 0)),
        ]

    rows0, near1, column1 = lax.optimization_barrier((send(slots).reshape(total_rows, width), near1, column1))
    pieces1 = gather_chip([column1] + near1 + gather_plane(column1, (3,)))
    gate_pre, up_pre, part = pl.pallas_call(
        experts_forward,
        grid=(steps,),
        in_specs=[by_blocks(block, width)] + weight_specs(0),
        out_specs=(by_blocks(block, inner), by_blocks(block, inner), by_blocks(block, width)),
        out_shape=(
            shaped((total_rows, inner), F32), shaped((total_rows, inner), F32), shaped((total_rows, width), BF16)
        ),
        compiler_params=params(24 * 1024 * 1024),
        cost_estimate=cost(7),
        name="experts_forward",
    )(rows0, *far(exp_gate, exp_up, exp_down))

    marks, part = lax.optimization_barrier((cot_column, part))
    place = (lax.axis_index("ep") % E).astype(jnp.int32)
    cot_slots = pl.pallas_call(
        spread_kernel,
        in_specs=[whole(pltpu.SMEM), whole()],
        out_shape=shaped((E, holders, CAP, width), BF16),
        compiler_params=params(),
        cost_estimate=cost(4),
        name="spread",
    )(place.reshape(1), marks)
    returned, cot_slots = lax.optimization_barrier((send(part).reshape(holders, SLOTS, width), cot_slots))
    picks0, x1, q, k, v, stat, o, y1, z1, slots, gate_slots = staged(
        forward_second, "forward_second", 11,
        (
            shaped((2, tokens, width), F32), flat, flat_low, flat_low, flat_low, stat_shape, flat_low, flat, logits_shape,
            slots_shape, shaped((holders, SLOTS, 128), BF16),
        ),
        image_start,
        (
            returned, y0, z0, gains, const_value[0], routes_col, target_col, order, cosine, signed_sine, mix_rows[1], carry,
            target_row,
        ),
        pieces1, scratch,
    )
    attention1, attended1 = (stat, q, k, v), o

    cot_back = [lax.ppermute(cot_slots[d], "ep", flipped(d, devices)) for d in range(1, E)]
    rows1, cot_back = lax.optimization_barrier((send(slots).reshape(total_rows, width), cot_back))
    low_inner = shaped((total_rows, inner), BF16)
    low_rows = shaped((total_rows, width), BF16)
    narrow_rows = CAP * width // 128 + 8
    hidden1, da1, db1, du1, cot_rows = pl.pallas_call(
        experts_both,
        grid=(steps,),
        in_specs=[whole(pltpu.SMEM), by_blocks(block, width), pl.BlockSpec((1, 1, CAP, width), lambda i: (0, i, 0, 0))]
        + [pl.BlockSpec((1, CAP, width), lambda i: (i, 0, 0))] * (E - 1)
        + weight_specs(1),
        out_specs=(
            by_blocks(block, inner), by_blocks(block, inner), by_blocks(block, inner),
            pl.BlockSpec((E, narrow_rows, 128), lambda i: (i, 0, 0)), by_blocks(block, width),
        ),
        out_shape=(low_inner, low_inner, low_inner, shaped((devices, narrow_rows, 128), BF16), low_rows),
        compiler_params=params(24 * 1024 * 1024),
        cost_estimate=cost(11),
        name="experts_both",
    )(place.reshape(1), rows1, *far(cot_slots, *cot_back, exp_gate, exp_up, exp_down))

    shares1 = exchange(du1)
    gate_slots, shares1 = lax.optimization_barrier((gate_slots, shares1))
    gate_rows = send(gate_slots)
    packed_low = shaped((tokens, 3 * width), BF16)
    gains_shape = shaped((8, width), F32)
    dx1, normed1, dpacked1, dy1, dgains1, dlogits1, dz0, df_slots = staged(
        backward_second, "backward_second", 16,
        (flat, flat_low, packed_low, flat_low, gains_shape, logits_shape, logits_shape, slots_shape),
        image_start,
        (
            cotangent, y1, z1, gains, routes_col, target_col, const_value[1], shares1, mix_rows[1], carry, z0, order_col,
            *attention1, cosine, signed_sine, x1, target_row,
        ),
        pieces1,
    )
    piece = shaped((width // 8, 4 * width + 128), BF16)
    dlogits0, small = staged(
        mixture_first, "mixture_first", 0.5, (logits_shape, shaped((64, width), F32)),
        image_start, (dx1, y0, z0, gains, routes_col, const_value[0], picks0, dz0, cotangent, y1, z1, dlogits1),
    )
    grads1 = staged(
        projection_grads, "projection_grads", 0.5, (piece,) * 8,
        image_start, (normed1, dpacked1, attended1, dy1, order, dgains1, small),
    )
    total1, low1 = sum_chips(grads1)
    chips1 = sum_plane(low1[:2], (1, 2))

    df_slots, gate_rows = lax.optimization_barrier((df_slots, gate_rows))
    df0 = send(df_slots).reshape(total_rows, width)
    df0, chips1, low1 = lax.optimization_barrier((df0, chips1, low1))
    chips1 += sum_plane(low1[2:], (3,))
    hidden0, da0, db0, du0 = pl.pallas_call(
        experts_backward,
        grid=(steps,),
        in_specs=[by_blocks(block, width), by_blocks(block, inner), by_blocks(block, inner)] + weight_specs(0),
        out_specs=(
            by_blocks(block, inner), by_blocks(block, inner), by_blocks(block, inner), by_blocks(block, width)
        ),
        out_shape=(low_inner, low_inner, low_inner, low_rows),
        compiler_params=params(24 * 1024 * 1024),
        cost_estimate=cost(9),
        name="experts_backward",
    )(df0, *far(gate_pre, up_pre, exp_gate, exp_up, exp_down))
    shares0 = send(du0).reshape(holders, SLOTS, width)

    grad_shapes = (
        shaped((LAYERS, 1, width, inner), F32), shaped((LAYERS, 1, width, inner), F32),
        shaped((LAYERS, 1, inner, width), F32),
    )
    operands = (rows1, hidden1, da1, db1, cot_rows, gate_rows.reshape(total_rows, 128))
    *expert_parts, gated = pl.pallas_call(
        expert_grads_second,
        grid_spec=pl.GridSpec(
            grid=(steps,),
            in_specs=[by_blocks(block, t.shape[1]) for t in operands] + weight_specs(1)[2:],
            out_specs=(
                pl.BlockSpec((1, 1, width, inner), lambda i: (1, 0, 0, 0)),
                pl.BlockSpec((1, 1, width, inner), lambda i: (1, 0, 0, 0)),
                pl.BlockSpec((1, 1, inner, width), lambda i: (1, 0, 0, 0)),
                pl.BlockSpec((E, 1, CAP, width), lambda i: (0, i, 0, 0)),
            ),
        ),
        out_shape=grad_shapes + (shaped((E, holders, CAP, width), BF16),),
        compiler_params=params(),
        cost_estimate=cost(9),
        name="expert_grads_second",
    )(*operands, exp_down)
    chips1, expert_parts = lax.optimization_barrier((chips1, expert_parts))
    reduced1, shares0 = sum_planes(total1, chips1, shares0)
    gated, shares0 = lax.optimization_barrier((gated, shares0))
    gated = in_plane(gated)
    grad_x, *grads0 = staged(
        backward_first, "backward_first", 1, (flat,) + (piece,) * 8,
        image_start,
        (
            dx1, y0, z0, gains, routes_col, target_col, dlogits0, mix_rows[0], shares0, order_col, order, *attention0, cosine,
            signed_sine, x_in, attended0,
        ),
        pieces0,
        [
            pltpu.VMEM((tokens, width), BF16), pltpu.VMEM((tokens, 3 * width), BF16), pltpu.VMEM((tokens, width), BF16),
            pltpu.VMEM((8, width), F32),
        ],
    )
    grads0, gated = lax.optimization_barrier((grads0, gated))
    (total0, low0), gated, mine, hidden0 = lax.optimization_barrier(
        (sum_chips(grads0), gated, reduced1[:, 4 * width :], hidden0)
    )
    chips0 = sum_plane(low0, (1, 2, 3))
    parts = pl.pallas_call(
        combine_kernel,
        grid=(1,),
        in_specs=[
            pl.BlockSpec((E, holders, CAP, width), lambda i: (0, 0, 0, 0)),
            pl.BlockSpec((holders, tokens, 128), lambda i: (0, 0, width // 128)),
        ],
        out_specs=pl.BlockSpec((holders, tokens, width), lambda i: (0, 0, 0)),
        out_shape=shaped((holders, tokens, width), BF16),
        compiler_params=params(),
        cost_estimate=cost(5),
        name="combine",
    )(gated, cot_column)
    parts, hidden0 = lax.optimization_barrier((parts, hidden0))
    operands = (rows0, hidden0, da0, db0, df0)
    expert_parts = pl.pallas_call(
        expert_grads_first,
        grid=(steps,),
        in_specs=[by_blocks(block, t.shape[1]) for t in operands] + [whole(pl.ANY)] * 3,
        out_specs=(
            pl.BlockSpec((1, 1, width, inner), lambda i: (0, 0, 0, 0)),
            pl.BlockSpec((1, 1, width, inner), lambda i: (0, 0, 0, 0)),
            pl.BlockSpec((1, 1, inner, width), lambda i: (0, 0, 0, 0)),
        ),
        out_shape=grad_shapes,
        input_output_aliases={5: 0, 6: 1, 7: 2},
        compiler_params=params(),
        cost_estimate=cost(9),
        name="expert_grads_first",
    )(*operands, *expert_parts)
    parts = across_planes(parts)
    mine = jnp.broadcast_to(mine[None], (devices,) + mine.shape)
    mine, parts, chips0 = lax.optimization_barrier((mine, parts, chips0))
    reduced0 = sum_planes(total0, chips0)
    small = exchange(mine).reshape(width, 128)[:, 8:72]
    hidden_out = pl.pallas_call(
        final_kernel,
        out_shape=flat,
        compiler_params=params(),
        cost_estimate=cost(4),
        name="final",
    )(y1, z1, gains, const_value[1], routes_col, parts)

    routers = w_router.shape[-1]
    across = small.T
    both = jnp.stack([across[0:24], across[24:48]])
    reduced = jnp.stack([reduced0, reduced1])
    return (
        hidden_out,
        grad_x,
        reduced[:, :, 4 * width],
        reduced[:, :, : 3 * width],
        reduced[:, :, 3 * width : 4 * width],
        reduced[:, :, 4 * width + 1],
        jnp.stack([small[:, :routers], small[:, 24 : 24 + routers]]),
        across[48 : 48 + routers, :routers],
        both[:, routers:ZW].reshape(LAYERS, NC, 2, width),
        both[:, ZW : ZW + NC],
        *expert_parts,
    )


def solution(mesh):
    in_specs = (
        P("ep", None),
        P("ep", None),
        P(None, "ep"),
        P(None, "ep", None),
        P(None, "ep", None),
        P(None, "ep"),
        P(),
        P(),
        P(),
        P(),
        P(None, "ep", None, None),
        P(None, "ep", None, None),
        P(None, "ep", None, None),
        P(None, "ep", None),
        P("ep", None),
        P("ep"),
    )
    out_specs = (
        P("ep", None),
        P("ep", None),
        P(None, "ep"),
        P(None, "ep", None),
        P(None, "ep", None),
        P(None, "ep"),
        P(),
        P(),
        P(),
        P(),
        P(None, "ep", None, None),
        P(None, "ep", None, None),
        P(None, "ep", None, None),
    )
    return jax.shard_map(shards, mesh=mesh, in_specs=in_specs, out_specs=out_specs, check_vma=False)
```

```python
from functools import partial

import jax
import jax.numpy as jnp
import numpy as np
from jax import lax
from jax.experimental import pallas as pl
from jax.experimental.pallas import tpu as pltpu
from jax.sharding import PartitionSpec as P

H = 12
HD = 64
E = 8
NC = 2
LAYERS = 2
SPAN = 128
CAP = 40
SLOTS = E * CAP
ZW = 16

EPSILON = 1e-06
NEGATIVE = -1e30
F32 = jnp.float32
BF16 = jnp.bfloat16
TOP = lax.Precision.HIGHEST
VMEM_LIMIT = 61 * 1024 * 1024


def whole(space=pltpu.VMEM):
    return pl.BlockSpec(memory_space=space)


def shaped(shape, dtype):
    return pltpu.HBM(shape, dtype)


def params(limit=VMEM_LIMIT):
    return pltpu.CompilerParams(vmem_limit_bytes=limit)


def far(*arrays):
    return [pltpu.with_memory_space_constraint(t, pltpu.HBM) for t in arrays]


def cost(microseconds):
    return pl.CostEstimate(
        flops=int(microseconds * 1e9), bytes_accessed=int(microseconds * 3e6), transcendentals=0
    )


class Lazy:
    def __init__(self, copies, local):
        self.copies, self.local = copies, local
        self.shape, self.dtype = local.shape, local.dtype
        for copy in copies:
            copy.start()

    def finish(self):
        for copy in self.copies:
            copy.wait()
        self.copies = []

    def __getitem__(self, index):
        self.finish()
        return self.local[index]


class Kept:
    def __init__(self, local, copy):
        self.local, self.copy, self.sent = local, copy, False
        self.shape, self.dtype = local.shape, local.dtype

    def __getitem__(self, index):
        return self.local[index]

    def __setitem__(self, index, value):
        self.local[index] = value

    def flush(self):
        if not self.sent:
            self.copy.start()
        self.sent = True


def staged(kernel, name, microseconds, outs, start, args, pieces=(), scratch=()):
    n_args, n_outs, n_pieces = len(args), len(outs), len(pieces)
    fixed = [pltpu.VMEM(t.shape, t.dtype) for t in args] + [pltpu.VMEM(t.shape, t.dtype) for t in outs]
    if pieces:
        rows, columns = pieces[0].shape
        fixed.append(pltpu.VMEM((rows * n_pieces, columns), pieces[0].dtype))
    fixed.append(pltpu.SemaphoreType.DMA((n_args + n_outs + n_pieces,)))

    def body(start_ref, *refs):
        arg_refs, refs = refs[:n_args], refs[n_args:]
        piece_refs, refs = refs[:n_pieces], refs[n_pieces:]
        out_refs, refs = refs[:n_outs], refs[n_outs:]
        local, rest = refs[: len(fixed)], refs[len(fixed) :]
        sems = local[-1]
        lazies = [
            Lazy([pltpu.make_async_copy(ref, local[i], sems.at[i])], local[i]) for i, ref in enumerate(arg_refs)
        ]
        kept = [
            Kept(local[n_args + i], pltpu.make_async_copy(local[n_args + i], ref, sems.at[n_args + i]))
            for i, ref in enumerate(out_refs)
        ]
        weights = []
        if pieces:
            target, first = local[-2], n_args + n_outs
            copies = [
                pltpu.make_async_copy(ref, target.at[pl.ds(i * rows, rows)], sems.at[first + i])
                for i, ref in enumerate(piece_refs)
            ]
            weights = [Lazy(copies, target)]
        kernel(start_ref, *lazies, *weights, *kept, *rest)
        for lazy in lazies + weights:
            lazy.finish()
        for out in kept:
            out.flush()
        for out in kept:
            out.copy.wait()

    return pl.pallas_call(
        body,
        in_specs=[whole(pltpu.SMEM)] + [whole(pl.ANY)] * (n_args + n_pieces),
        out_specs=tuple(whole(pl.ANY) for _ in outs),
        out_shape=tuple(outs),
        scratch_shapes=fixed + list(scratch),
        compiler_params=params(44 * 1024 * 1024),
        cost_estimate=cost(microseconds),
        name=name,
    )(start, *[t if t.ndim == 3 and t.dtype == BF16 else far(t)[0] for t in args], *far(*pieces))


def dot(a, b, dims=((1,), (0,)), precision=None):
    return lax.dot_general(a, b, (dims, ((), ())), precision=precision, preferred_element_type=F32)


ROWS_BY_ROWS = ((1,), (1,))
COLS_BY_COLS = ((0,), (0,))


def spread_matrix(order):
    feature = lax.broadcasted_iota(jnp.int32, (order.shape[1], order.shape[1]), 0)
    return (feature == order).astype(F32).astype(BF16)


def gather_matrix(order_col):
    feature = lax.broadcasted_iota(jnp.int32, (order_col.shape[0], order_col.shape[0]), 1)
    return (feature == order_col).astype(F32).astype(BF16)


def reorder(values, places):
    return dot(values, places).astype(BF16)


def restore(values, back):
    if values.dtype == BF16:
        return dot(values, back).astype(BF16)
    high = values.astype(BF16)
    low = (values - high.astype(F32)).astype(BF16)
    rows = values.shape[0]
    both = dot(jnp.concatenate([high, low], 0), back)
    return both[:rows] + both[rows:]


def rope_tables(length):
    position = np.arange(length).astype(np.float32)
    inverse = (10000.0 ** (-np.arange(HD // 2).astype(np.float32) * 2.0 / HD)).astype(np.float32)
    angles = (position[:, None] * inverse[None, :]).astype(np.float32)
    cosine, sine = np.cos(angles), np.sin(angles)
    return (
        np.concatenate([cosine] * 4, 1).astype(np.float32),
        np.concatenate([-sine, sine, -sine, sine], 1).astype(np.float32),
    )


def swap_halves(values):
    lane = lax.broadcasted_iota(jnp.int32, values.shape, 1)
    low = lane % HD < HD // 2
    return jnp.where(low, pltpu.roll(values, 128 - HD // 2, 1), pltpu.roll(values, HD // 2, 1))


def span_mask(length, start):
    query = lax.broadcasted_iota(jnp.int32, (length, length), 0)
    key = lax.broadcasted_iota(jnp.int32, (length, length), 1)
    in_query = (query >= start) & (query < start + SPAN)
    in_key = (key >= start) & (key < start + SPAN)
    return (key <= query) | (in_query & in_key)


def head_masks(length):
    lane = lax.broadcasted_iota(jnp.int32, (length, 2 * HD), 1)
    return (lane < HD, lane >= HD)


def row_mean(values):
    return jnp.mean(values, -1, keepdims=True)


def row_sum(values):
    return jnp.sum(values, -1, keepdims=True)


def slot_matrix(target_row):
    slot = lax.broadcasted_iota(jnp.int32, (SLOTS, target_row.shape[1]), 0)
    return slot == target_row


def pick_matrix(target_col):
    slot = lax.broadcasted_iota(jnp.int32, (target_col.shape[0], SLOTS), 1)
    return slot == target_col


def gate_pair(logits, first, second):
    lane = lax.broadcasted_iota(jnp.int32, logits.shape, 1)
    one = row_sum(jnp.where(lane == first, logits, 0.0))
    two = row_sum(jnp.where(lane == second, logits, 0.0))
    return soft_pair(one, two)


def soft_pair(one, two):
    top = jnp.maximum(one, two)
    one, two = jnp.exp(one - top), jnp.exp(two - top)
    total = one + two
    return one / total, two / total


def blend_pairs(logits):
    base = ZW - 2 * NC
    return [
        soft_pair(logits[:, base + 2 * c : base + 2 * c + 1], logits[:, base + 2 * c + 1 : base + 2 * c + 2])
        for c in range(NC)
    ]


def chosen_weight(gates, routes, expert):
    return sum(jnp.where(route == expert, gate, 0.0) for gate, route in zip(gates, routes))


def mix_weights(gates, routes, blends):
    of_u = chosen_weight(gates, routes, E + 1)
    of_const = []
    for c in range(NC):
        weight = chosen_weight(gates, routes, E + 2 + c)
        of_u = of_u + weight * blends[c][0]
        of_const.append(weight * blends[c][1])
    return of_u, of_const


def prep_kernel(routes_col, order, cot, target_row, target_col, cot_low):
    tokens = order.shape[1]
    order_row = order[...].astype(F32)
    order_col = jnp.transpose(jnp.broadcast_to(order_row, (128, tokens)))[:, 0:1]
    routes_row = jnp.concatenate([routes_col[...].astype(F32), jnp.zeros((tokens, 128 - 2 * LAYERS), F32)], 1)
    routes_row = jnp.transpose(routes_row)[0:8].astype(jnp.int32)
    earlier = jnp.where(order_row < order_col, 1.0, 0.0).astype(BF16)
    later = jnp.where(order_col < order_row, 1.0, 0.0).astype(BF16)
    lane = lax.broadcasted_iota(jnp.int32, (tokens, 128), 1)
    sub = lax.broadcasted_iota(jnp.int32, (16, tokens), 0)
    for layer in range(LAYERS):
        cols = [routes_col[:, 2 * layer + k : 2 * layer + k + 1] for k in range(2)]
        rows = [routes_row[2 * layer + k : 2 * layer + k + 1, :] for k in range(2)]
        wanted = jnp.where((lane == cols[0]) | (lane == cols[1]), 1.0, 0.0).astype(BF16)
        counts = dot(earlier, wanted)
        wanted_t = jnp.where((sub == rows[0]) | (sub == rows[1]), 1.0, 0.0).astype(BF16)
        counts_t = dot(wanted_t, later)
        for k in range(2):
            rank = row_sum(jnp.where(lane == cols[k], counts, 0.0)).astype(jnp.int32)
            kept = (cols[k] < E) & (rank < CAP)
            target_col[:, 2 * layer + k : 2 * layer + k + 1] = jnp.where(kept, cols[k] * CAP + rank, -1)
            rank_t = jnp.sum(jnp.where(sub == rows[k], counts_t, 0.0), 0, keepdims=True).astype(jnp.int32)
            kept_t = (rows[k] < E) & (rank_t < CAP)
            target_row[2 * layer + k : 2 * layer + k + 1, :] = jnp.where(kept_t, rows[k] * CAP + rank_t, -1)
    width = cot.shape[1]
    rows = cot[...].astype(BF16)
    marks = jnp.zeros((tokens, 128), F32)
    for k in range(2):
        last = 2 * (LAYERS - 1) + k
        target = target_col[:, last : last + 1]
        high = (target + 16) // 16 * 16 - 16
        marks = jnp.where(lane == 2 * k, high.astype(F32), marks)
        marks = jnp.where(lane == 2 * k + 1, (target - high).astype(F32), marks)
    for holder in range(cot_low.shape[0]):
        cot_low[holder, :, :width] = rows
        cot_low[holder, :, width:] = marks.astype(BF16)


def marked_slots(marks):
    taken = None
    for k in range(2):
        target = (marks[:, 2 * k : 2 * k + 1] + marks[:, 2 * k + 1 : 2 * k + 2]).astype(jnp.int32)
        mine = pick_matrix(target)
        taken = mine if taken is None else taken | mine
    return taken.astype(F32).astype(BF16)


def spread_kernel(place, *refs):
    sources, out = refs
    width = out.shape[3]
    for level in range(sources.shape[0]):
        source = sources.at[level]
        taken = marked_slots(source[:, width:].astype(F32))
        rows = dot(taken, source[:, :width], COLS_BY_COLS)
        for expert in range(E):
            out[jnp.bitwise_xor(expert, place[0]), level] = rows[expert * CAP : (expert + 1) * CAP].astype(BF16)


def combine_kernel(shares, *refs):
    sources, out = refs
    for level in range(sources.shape[0]):
        rows = shares[:, level].astype(F32).reshape(SLOTS, shares.shape[3]).astype(BF16)
        out[level] = dot(marked_slots(sources[level].astype(F32)), rows).astype(BF16)


def attend(x, attn_gain, weights, places, cosine, signed_sine, start, q, k, v, stat, o, packed, attended):
    tokens, width = x.shape
    scale = HD**-0.5
    normed = x * lax.rsqrt(row_mean(x * x) + EPSILON) * attn_gain
    packed[...] = dot(reorder(normed.astype(BF16), places), weights[:, : 3 * width])
    allowed = span_mask(tokens, start)
    masks = head_masks(tokens)
    lane = lax.broadcasted_iota(jnp.int32, (tokens, 128), 1)
    kept = jnp.zeros((tokens, 128), F32)
    for pair in range(H // 2):
        at = slice(128 * pair, 128 * pair + 128)
        turned = []
        for part in range(2):
            raw = packed[:, part * width + 128 * pair : part * width + 128 * pair + 128]
            turned.append((raw * cosine + swap_halves(raw) * signed_sine).astype(BF16))
        queries, keys = turned
        values = packed[:, 2 * width + 128 * pair : 2 * width + 128 * pair + 128].astype(BF16)
        q[:, at], k[:, at], v[:, at] = queries, keys, values
        total = jnp.zeros((tokens, 128), F32)
        for side in range(2):
            mine = masks[side]
            scores = dot(jnp.where(mine, queries, 0), keys, ROWS_BY_ROWS) * scale
            scores = jnp.where(allowed, scores, NEGATIVE)
            top = jnp.max(scores, -1, keepdims=True)
            probs = jnp.exp(scores - top)
            inverse = 1.0 / row_sum(probs)
            kept = jnp.where(lane == 2 * pair + side, top, kept)
            kept = jnp.where(lane == 64 + 2 * pair + side, inverse, kept)
            total = total + dot((probs * inverse).astype(BF16), jnp.where(mine, values, 0))
        attended[:, at] = total.astype(BF16)
    stat[...] = kept
    o[...] = attended[...]
    for out in (q, k, v, stat, o):
        out.flush()
    return x + dot(reorder(attended[...], places), weights[:, 3 * width : 4 * width])


def mix_in(y, moe_gain, mix_rows, target_row, z_extra):
    u = y * lax.rsqrt(row_mean(y * y) + EPSILON) * moe_gain
    logits = dot(u, mix_rows, ROWS_BY_ROWS, TOP)
    if z_extra is not None:
        logits = logits + z_extra
    spread = slot_matrix(target_row[0:1]) | slot_matrix(target_row[1:2])
    return u, logits, dot(spread.astype(F32).astype(BF16), u.astype(BF16)).astype(BF16)


def forward_first(
    start, x, target_row, order, cosine, signed_sine, mix_rows, weights, q, k, v, stat, o, y, z, slots, gains, packed, attended
):
    width = x.shape[1]
    places = spread_matrix(order[...])
    gain_rows = dot(weights[:, 4 * width :], places, ((0,), (1,)))[0:8, :]
    gains[...] = gain_rows
    gains.flush()
    middle = attend(
        x[...], gain_rows[0:1], weights, places, cosine[...], signed_sine[...], start[0], q, k, v, stat, o, packed, attended
    )
    y[...] = middle
    y.flush()
    u, logits, rows = mix_in(middle, gain_rows[1:2], mix_rows[...], target_row[0:2, :], None)
    z[...] = logits
    for holder in range(slots.shape[0]):
        slots[holder] = rows


def in_two(column, lane):
    high = column.astype(BF16).astype(F32)
    return jnp.where(lane == 0, high, jnp.where(lane == 1, column - high, 0.0)).astype(BF16)


def gather_shares(returned, target_col, layer):
    tokens = target_col.shape[0]
    both = jnp.concatenate(
        [pick_matrix(target_col[:, 2 * layer + k : 2 * layer + k + 1]).astype(F32) for k in range(2)], 0
    ).astype(BF16)
    holders = len(returned) if isinstance(returned, list) else returned.shape[0]
    total = sum(dot(both, returned[holder]) for holder in range(holders))
    return [total[:tokens], total[tokens:]]


def gather_sum(returned, target_col, layer):
    picked = [pick_matrix(target_col[:, 2 * layer + k : 2 * layer + k + 1]) for k in range(2)]
    picked = (picked[0] | picked[1]).astype(F32).astype(BF16)
    return sum(dot(picked, returned[holder]) for holder in range(returned.shape[0]))


def mixed_stream(y, u, logits, routes, const_value, picks):
    gates = gate_pair(logits, *routes)
    of_u, of_const = mix_weights(gates, routes, blend_pairs(logits))
    stream = y + of_u * u
    for c in range(NC):
        stream = stream + of_const[c] * const_value[c : c + 1, :]
    return stream if picks is None else stream + gates[0] * picks[0] + gates[1] * picks[1]


def forward_second(
    start, returned, y0, z0, gains, const_value0, routes_col, target_col, order, cosine, signed_sine, mix_rows, carry,
    target_row, weights,
    picks0, x1, q, k, v, stat, o, y, z, slots, gate_slots, packed, attended,
):
    y_first, logits_first = y0[...], z0[...]
    u_first = y_first * lax.rsqrt(row_mean(y_first * y_first) + EPSILON) * gains[1:2, :]
    routes = [routes_col[:, k : k + 1] for k in range(2)]
    picks = gather_shares(returned, target_col, 0)
    picks0[0], picks0[1] = picks
    picks0.flush()
    stream = mixed_stream(y_first, u_first, logits_first, routes, const_value0[...], picks)
    x1[...] = stream
    x1.flush()
    places = spread_matrix(order[...])
    middle = attend(
        stream, gains[2:3, :], weights, places, cosine[...], signed_sine[...], start[0], q, k, v, stat, o, packed, attended
    )
    y[...] = middle
    y.flush()
    z_extra = dot(logits_first, carry[...], precision=TOP)
    u, logits, rows = mix_in(middle, gains[3:4, :], mix_rows[...], target_row[2:4, :], z_extra)
    z[...] = logits
    for holder in range(slots.shape[0]):
        slots[holder] = rows
    slots.flush()
    gates = gate_pair(logits, routes_col[:, 2:3], routes_col[:, 3:4])
    lane = lax.broadcasted_iota(jnp.int32, (x1.shape[0], 128), 1)
    of_slots = 0.0
    for r in range(2):
        spread = slot_matrix(target_row[2 + r : 3 + r, :]).astype(F32).astype(BF16)
        of_slots = of_slots + dot(spread, in_two(gates[r], lane))
    for holder in range(gate_slots.shape[0]):
        gate_slots[holder] = of_slots.astype(BF16)


def final_kernel(y, z, gains, const_value, routes_col, parts, out):
    middle, logits = y[...], z[...]
    u = middle * lax.rsqrt(row_mean(middle * middle) + EPSILON) * gains[3:4, :]
    routes = [routes_col[:, 2 + k : 3 + k] for k in range(2)]
    stream = middle + sum(parts[level].astype(F32) for level in range(parts.shape[0]))
    out[...] = mixed_stream(stream, u, logits, routes, const_value[...], None)


def experts_forward(rows, gate_w, up_w, down_w, gate_pre, up_pre, part):
    a = dot(rows[...], gate_w[...])
    b = dot(rows[...], up_w[...])
    gate_pre[...] = a
    up_pre[...] = b
    hidden = (a / (1.0 + jnp.exp(-a)) * b).astype(BF16)
    part[...] = dot(hidden, down_w[...]).astype(BF16)


def expert_back(a, b, df, gate_w, up_w, down_w, hidden, da, db):
    dh = dot(df, down_w[...], ROWS_BY_ROWS)
    sig = 1.0 / (1.0 + jnp.exp(-a))
    act = a * sig
    hidden_low = (act * b).astype(BF16)
    hidden[...] = hidden_low
    da_low = (dh * b * sig * (1.0 + a * (1.0 - sig))).astype(BF16)
    db_low = (dh * act).astype(BF16)
    da[...] = da_low
    db[...] = db_low
    return hidden_low, dot(da_low, gate_w[...], ROWS_BY_ROWS) + dot(db_low, up_w[...], ROWS_BY_ROWS)


def experts_backward(df, gate_pre, up_pre, gate_w, up_w, down_w, hidden, da, db, du):
    rows = expert_back(gate_pre[...], up_pre[...], df[...], gate_w, up_w, down_w, hidden, da, db)[1]
    du[...] = rows.astype(BF16)


def in_order(pieces, place):
    for bit in (1, 2, 4):
        flip = jnp.bitwise_and(place, bit) != 0
        pieces = [jnp.where(flip, pieces[i ^ bit], pieces[i]) for i in range(E)]
    return pieces


def experts_both(place, rows, *refs):
    pieces, (gate_w, up_w, down_w, hidden, da, db, du, cot) = refs[:E], refs[E:]
    width = rows.shape[1]
    pieces = in_order([piece[...].reshape(CAP, width).astype(F32) for piece in pieces], place[0])
    cot[...] = jnp.concatenate(pieces, 0).astype(BF16)
    a = dot(rows[...], gate_w[...])
    b = dot(rows[...], up_w[...])
    hidden_low, du_rows = expert_back(a, b, cot[...], gate_w, up_w, down_w, hidden, da, db)
    share = dot(hidden_low, down_w[...]).astype(BF16)
    inner = row_sum(share.astype(F32) * cot[...].astype(F32))
    for to in range(E):
        mine = slice(to * CAP, (to + 1) * CAP)
        du[to] = narrow(du_rows[mine], inner[mine]).astype(BF16)


def narrow(rows, column):
    parts = [rows[:, i : i + 128] for i in range(0, rows.shape[1], 128)]
    lane = lax.broadcasted_iota(jnp.int32, (8, 128), 1)
    last = jnp.zeros((8, 128), F32)
    for i in range(CAP // 8):
        value = column[8 * i : 8 * i + 8]
        high = value.astype(BF16).astype(F32)
        last = jnp.where(lane == i, high, jnp.where(lane == 8 + i, value - high, last))
    return jnp.concatenate(parts + [last], 0)


def widen(block):
    return jnp.concatenate([block[i : i + CAP] for i in range(0, block.shape[0] - 8, CAP)], 1)


def expert_grads(rows, hidden, da, db, df, dgate, dup, ddown):
    @pl.when(pl.program_id(0) == 0)
    def _():
        dgate[...] = jnp.zeros_like(dgate)
        dup[...] = jnp.zeros_like(dup)
        ddown[...] = jnp.zeros_like(ddown)

    dgate[0, 0] += dot(rows, da[...], COLS_BY_COLS)
    dup[0, 0] += dot(rows, db[...], COLS_BY_COLS)
    ddown[0, 0] += dot(hidden, df[...], COLS_BY_COLS)


def expert_grads_second(rows, hidden, da, db, df, gates, down_w, dgate, dup, ddown, shares):
    gate = row_sum(gates[...].astype(F32))
    low = hidden[...]
    share = dot(low, down_w[...]) * gate
    for place in range(E):
        shares[place, 0] = share[place * CAP : (place + 1) * CAP].astype(BF16)
    scaled = (rows[...].astype(F32) * gate).astype(BF16)
    expert_grads(scaled, (low.astype(F32) * gate).astype(BF16), da, db, df, dgate, dup, ddown)


def expert_grads_first(rows, hidden, da, db, df, *refs):
    expert_grads(rows[...], hidden[...], da, db, df, *refs[3:])


def mixture_back(layer, grad, dgates, dlogits_extra, y, z, moe_gain, routes_col, const_value):
    middle, logits = y[...], z[...]
    u = middle * lax.rsqrt(row_mean(middle * middle) + EPSILON) * moe_gain
    routes = [routes_col[:, 2 * layer + r : 2 * layer + r + 1] for r in range(2)]
    gates = gate_pair(logits, *routes)
    blends = blend_pairs(logits)
    by_u = row_sum(grad * u)
    by_const = [row_sum(grad * const_value[c : c + 1, :]) for c in range(NC)]
    dgates = list(dgates)
    for r in range(2):
        dgates[r] = dgates[r] + jnp.where(routes[r] == E + 1, by_u, 0.0)
        for c in range(NC):
            value = blends[c][0] * by_u + blends[c][1] * by_const[c]
            dgates[r] = dgates[r] + jnp.where(routes[r] == E + 2 + c, value, 0.0)
    mean = gates[0] * dgates[0] + gates[1] * dgates[1]
    lane = lax.broadcasted_iota(jnp.int32, logits.shape, 1)
    dlogits = jnp.zeros_like(logits)
    for r in range(2):
        dlogits = jnp.where(lane == routes[r], gates[r] * (dgates[r] - mean), dlogits)
    base = ZW - 2 * NC
    for c in range(NC):
        weight = chosen_weight(gates, routes, E + 2 + c)
        first, second = weight * by_u, weight * by_const[c]
        mean = blends[c][0] * first + blends[c][1] * second
        dlogits = jnp.where(lane == base + 2 * c, blends[c][0] * (first - mean), dlogits)
        dlogits = jnp.where(lane == base + 2 * c + 1, blends[c][1] * (second - mean), dlogits)
    return dlogits if dlogits_extra is None else dlogits + dlogits_extra


def mixture_grads(layer, grad, dlogits, y, z, moe_gain, routes_col, small, at):
    middle, logits = y[...], z[...]
    u = middle * lax.rsqrt(row_mean(middle * middle) + EPSILON) * moe_gain
    routes = [routes_col[:, 2 * layer + r : 2 * layer + r + 1] for r in range(2)]
    _, of_const = mix_weights(gate_pair(logits, *routes), routes, blend_pairs(logits))
    for c in range(NC):
        small[at + ZW + c : at + ZW + c + 1, :] = jnp.sum(of_const[c] * grad, 0, keepdims=True)
    small[at : at + ZW, :] = dot(dlogits, u, COLS_BY_COLS, TOP)


def backward_layer(
    layer, start, grad, dlogits, dexpert, y, x, z, q, k, v, stat, routes_col, mix_rows, attn_gain, moe_gain, weights, back,
    cosine, signed_sine,
    dx_out, normed_out, dpacked, dy_out, dgains,
):
    tokens, width = x.shape
    scale = HD**-0.5
    middle, logits = y[...], z[...]
    inv_y = lax.rsqrt(row_mean(middle * middle) + EPSILON)
    unit = middle * inv_y
    routes = [routes_col[:, 2 * layer + r : 2 * layer + r + 1] for r in range(2)]
    of_u, _ = mix_weights(gate_pair(logits, *routes), routes, blend_pairs(logits))
    du = of_u * grad + dexpert + dot(dlogits, mix_rows[...], precision=TOP)
    dunit = du * moe_gain
    dmiddle = grad + inv_y * dunit - unit * (inv_y * row_mean(dunit * unit))
    dgains[...] = jnp.zeros_like(dgains)
    dgains[1:2, :] = jnp.sum(du * unit, 0, keepdims=True)
    dy_low = dmiddle.astype(BF16)
    dy_out[...] = dy_low
    dy_out.flush()
    dattended = restore(dot(dy_low, weights[:, 3 * width : 4 * width], ROWS_BY_ROWS).astype(BF16), back)
    allowed = span_mask(tokens, start)
    masks = head_masks(tokens)
    for pair in range(H // 2):
        at = slice(128 * pair, 128 * pair + 128)
        queries, keys, values, dattn = q[:, at], k[:, at], v[:, at], dattended[:, at]
        dq = jnp.zeros((tokens, 128), F32)
        dk = jnp.zeros((tokens, 128), F32)
        dv = jnp.zeros((tokens, 128), F32)
        for side in range(2):
            mine = masks[side]
            head = 2 * pair + side
            my_queries = jnp.where(mine, queries, 0)
            my_dattn = jnp.where(mine, dattn, 0)
            scores = dot(my_queries, keys, ROWS_BY_ROWS) * scale
            scores = jnp.where(allowed, scores, NEGATIVE)
            probs = jnp.exp(scores - stat[:, head : head + 1]) * stat[:, 64 + head : 65 + head]
            dprobs = dot(my_dattn, values, ROWS_BY_ROWS)
            dscores = (probs * (dprobs - row_sum(probs * dprobs))).astype(BF16)
            dv = dv + dot(probs.astype(BF16), my_dattn, COLS_BY_COLS)
            dq = dq + dot(dscores, jnp.where(mine, keys, 0))
            dk = dk + dot(dscores, my_queries, COLS_BY_COLS)
        dq, dk = dq * scale, dk * scale
        dpacked[:, at] = (dq * cosine - swap_halves(dq) * signed_sine).astype(BF16)
        dpacked[:, width + 128 * pair : width + 128 * pair + 128] = (
            dk * cosine - swap_halves(dk) * signed_sine
        ).astype(BF16)
        dpacked[:, 2 * width + 128 * pair : 2 * width + 128 * pair + 128] = dv.astype(BF16)
    dpacked.flush()
    dnormed = restore(dot(dpacked[...], weights[:, : 3 * width], ROWS_BY_ROWS), back)
    stream = x[...]
    inv_x = lax.rsqrt(row_mean(stream * stream) + EPSILON)
    unit = stream * inv_x
    normed_out[...] = (unit * attn_gain).astype(BF16)
    normed_out.flush()
    dgains[0:1, :] = jnp.sum(dnormed * unit, 0, keepdims=True)
    dunit = dnormed * attn_gain
    dx = dmiddle + inv_x * dunit - unit * (inv_x * row_mean(dunit * unit))
    dx_out[...] = dx
    dx_out.flush()
    return dx


def backward_second(
    start, dout, y, z, gains, routes_col, target_col, const_value, shares, mix_rows, carry, z0, order_col, stat, q, k, v,
    cosine, signed_sine, x, target_row, weights,
    dx_out, normed_out, dpacked, dy_out, dgains, dlogits_out, dz0, slots,
):
    grad = dout[...]
    blocks = [[shares[holder + e].astype(F32) for e in range(E)] for holder in range(0, shares.shape[0], E)]
    rows = [jnp.concatenate([widen(block) for block in held], 0).astype(BF16) for held in blocks]
    totals = gather_shares(rows, target_col, 1)
    gates = gate_pair(z[...], routes_col[:, 2:3], routes_col[:, 3:4])
    dexpert = gates[0] * totals[0] + gates[1] * totals[1]
    sums = [sum(held[e][-8:] for held in blocks) for e in range(E)]
    column = jnp.concatenate([t[:, i : i + 1] + t[:, 8 + i : 9 + i] for t in sums for i in range(CAP // 8)], 0)
    column = in_two(column, lax.broadcasted_iota(jnp.int32, (SLOTS, 128), 1))
    dgates = [row_sum(t) for t in gather_shares([column], target_col, 1)]
    dlogits = mixture_back(1, grad, dgates, None, y, z, gains[3:4, :], routes_col, const_value)
    dlogits_out[...] = dlogits
    dz0[...] = dot(dlogits, carry[...], ROWS_BY_ROWS, TOP)
    dlogits_out.flush()
    dz0.flush()
    dx = backward_layer(
        1, start[0], grad, dlogits, dexpert, y, x, z, q, k, v, stat, routes_col, mix_rows, gains[2:3, :], gains[3:4, :],
        weights, gather_matrix(order_col[...]), cosine[...], signed_sine[...],
        dx_out, normed_out, dpacked, dy_out, dgains,
    )
    gates = gate_pair(z0[...], routes_col[:, 0:1], routes_col[:, 1:2])
    rows = 0.0
    for r in range(2):
        spread = slot_matrix(target_row[r : r + 1, :]).astype(F32).astype(BF16)
        rows = rows + dot(spread, (gates[r] * dx).astype(BF16))
    rows = rows.astype(BF16)
    for holder in range(slots.shape[0]):
        slots[holder] = rows


def mixture_first(
    start, dout, y, z, gains, routes_col, const_value, picks, dz0, cotangent, y1, z1, dlogits1, dlogits_out, small
):
    small[...] = jnp.zeros_like(small)
    grad = dout[...]
    dgates = [row_sum(grad * picks[r]) for r in range(2)]
    dlogits = mixture_back(0, grad, dgates, dz0[...], y, z, gains[1:2, :], routes_col, const_value)
    dlogits_out[...] = dlogits
    mixture_grads(0, grad, dlogits, y, z, gains[1:2, :], routes_col, small, 0)
    mixture_grads(1, cotangent[...], dlogits1[...], y1, z1, gains[3:4, :], routes_col, small, 24)
    small[48 : 48 + ZW, 0:ZW] = dot(z[...], dlogits1[...], COLS_BY_COLS, TOP)


def backward_first(
    start, dout, y, z, gains, routes_col, target_col, dlogits, mix_rows, shares, order_col, order, stat, q, k, v, cosine,
    signed_sine, x, o, weights,
    dx_out, *rest,
):
    grads, (normed, dpacked, dy, dgains) = rest[:8], rest[8:]
    backward_layer(
        0, start[0], dout[...], dlogits[...], gather_sum(shares, target_col, 0), y, x, z, q, k, v, stat, routes_col, mix_rows,
        gains[0:1, :], gains[1:2, :], weights, gather_matrix(order_col[...]), cosine[...], signed_sine[...],
        dx_out, Local(normed), Local(dpacked), Local(dy), dgains,
    )
    packet(normed, dpacked, o, dy, order, dgains, None, grads)


class Local:
    def __init__(self, local):
        self.local = local

    def __getitem__(self, index):
        return self.local[index]

    def __setitem__(self, index, value):
        self.local[index] = value

    def flush(self):
        pass


def projection_grads(start, normed, dpacked, o, dy, order, dgains, extra, *outs):
    packet(normed, dpacked, o, dy, order, dgains, extra, outs)


def packet(normed, dpacked, o, dy, order, dgains, extra, outs):
    width = normed.shape[1]
    places = spread_matrix(order[...])
    rows = width // len(outs)

    def store(first, part):
        low = part.astype(BF16)
        for i, out in enumerate(outs):
            out[:, first : first + part.shape[1]] = low[i * rows : (i + 1) * rows]

    sums = [dgains[...]] + ([] if extra is None else [extra[...]])
    sums.append(jnp.zeros((128 - sum(t.shape[0] for t in sums), width), F32))
    store(4 * width, dot(places, jnp.concatenate(sums, 0).astype(BF16), ((0,), (1,))))
    store(3 * width, dot(reorder(o[...], places), dy[...], COLS_BY_COLS))
    features = reorder(normed[...], places)
    for part in range(3):
        columns = slice(part * width, (part + 1) * width)
        store(part * width, dot(features, dpacked[:, columns], COLS_BY_COLS))


def rotated(shift, devices):
    return [(i, (i + shift) % devices) for i in range(devices)]


def flipped(bits, devices):
    return [(i, i ^ bits) for i in range(devices)]


def feature_order(width):
    devices = lax.axis_size("ep")
    levels = devices // 8
    rows = width // devices
    me = lax.axis_index("ep")
    place = jnp.arange(width, dtype=jnp.int32)
    inside, block = place % rows, place // rows
    level = (block % levels + me // 8) % levels
    chip = ((block // levels) % 4) ^ ((me // 2) % 4)
    core = (block // (4 * levels)) ^ (me % 2)
    return (((level * 4 + chip) * 2 + core) * rows + inside).reshape(1, width)


def plane_parts(block):
    devices = lax.axis_size("ep")
    return [block] + [lax.ppermute(block, "ep", rotated(-8 * d, devices)) for d in range(1, devices // 8)]


def gather_planes(block):
    return jnp.concatenate(plane_parts(block), 0)


def gather_plane(column, chips):
    return [lax.ppermute(column, "ep", flipped(2 * d, lax.axis_size("ep"))) for d in chips]


def gather_chip(near):
    return near + [lax.ppermute(piece, "ep", flipped(1, lax.axis_size("ep"))) for piece in near]


def sum_chips(pieces):
    devices = lax.axis_size("ep")
    totals = [None] * 4
    for d in (1, 2, 3, 0):
        far = lax.ppermute(pieces[4 + d], "ep", flipped(1, devices))
        totals[d] = pieces[d].astype(F32) + far.astype(F32)
    return totals[0], [total.astype(BF16) for total in totals[1:]]


def sum_plane(low, chips):
    return [lax.ppermute(part, "ep", flipped(2 * d, lax.axis_size("ep"))) for part, d in zip(low, chips)]


def sum_planes(total, chips, beside=None):
    devices = lax.axis_size("ep")
    total = total + sum(part.astype(F32) for part in chips)
    levels = devices // 8
    rows = total.shape[0] // levels
    low = total.astype(BF16)
    if beside is not None:
        low, beside = lax.optimization_barrier((low, beside))
    planes = [
        lax.ppermute(low[d * rows : (d + 1) * rows], "ep", rotated(8 * d, devices)) for d in range(1, levels)
    ]
    total = total[:rows] + sum(part.astype(F32) for part in planes)
    return total if beside is None else (total, beside)


def exchange(slots):
    return lax.all_to_all(slots, "ep", split_axis=0, concat_axis=0, tiled=True)


def by_blocks(rows_per_step, width):
    return pl.BlockSpec((rows_per_step, width), lambda i: (i, 0))


def shards(
    x_in,
    cotangent,
    attn_gain,
    w_qkv,
    w_out,
    moe_gain,
    w_router,
    w_carry,
    const_gate,
    const_value,
    exp_gate,
    exp_up,
    exp_down,
    routes,
    drop_order,
    image_start,
):
    devices = lax.axis_size("ep")
    holders = devices // E
    tokens, width = x_in.shape
    inner = exp_gate.shape[-1]
    total_rows = devices * CAP
    block = SLOTS
    steps = total_rows // block
    large = 2 * block
    large_steps = total_rows // large
    cosine, signed_sine = (jnp.asarray(t) for t in rope_tables(tokens))

    def beside(layer, extra):
        return jnp.concatenate([w_qkv[layer], w_out[layer]] + extra, 1)

    gain_columns = jnp.stack([attn_gain[0], moe_gain[0], attn_gain[1], moe_gain[1]], 1)
    gain_columns = jnp.pad(gain_columns, ((0, 0), (0, 124)))
    order = feature_order(width)
    order_col = order.reshape(width, 1)
    mix_rows = [
        jnp.concatenate([w_router[layer].T, const_gate[layer].reshape(2 * NC, width)], 0) for layer in range(LAYERS)
    ]
    carry = jnp.pad(w_carry, ((0, ZW - w_carry.shape[0]), (0, ZW - w_carry.shape[1])))

    routes_col = routes.transpose(1, 0, 2).reshape(tokens, 2 * LAYERS)

    slots_shape = shaped((holders, SLOTS, width), BF16)
    flat = shaped((tokens, width), F32)
    flat_low = shaped((tokens, width), BF16)
    logits_shape = shaped((tokens, ZW), F32)
    stat_shape = shaped((tokens, 128), F32)
    scratch = [pltpu.VMEM((tokens, 3 * width), F32), pltpu.VMEM((tokens, width), BF16)]

    target_row, target_col, cot_low = pl.pallas_call(
        prep_kernel,
        out_shape=(
            shaped((2 * LAYERS, tokens), jnp.int32), shaped((tokens, 2 * LAYERS), jnp.int32),
            shaped((holders, tokens, width + 128), BF16),
        ),
        compiler_params=params(),
        cost_estimate=cost(3),
        name="prep",
    )(routes_col, drop_order, cotangent)

    def send(slots):
        return exchange(slots.reshape(devices, CAP, slots.shape[-1]))

    def across_planes(rows):
        groups = [list(range(i, devices, E)) for i in range(E)]
        return lax.all_to_all(rows, "ep", split_axis=0, concat_axis=0, tiled=True, axis_index_groups=groups)

    def in_plane(rows):
        groups = [list(range(E * i, E * i + E)) for i in range(holders)]
        back = lax.all_to_all(
            rows.reshape(E, holders * CAP, width), "ep", split_axis=0, concat_axis=0, tiled=True, axis_index_groups=groups
        )
        return back.reshape(rows.shape)

    column0, cot_low, later = lax.optimization_barrier(
        (gather_planes(beside(0, [gain_columns])), cot_low, beside(1, [jnp.zeros_like(gain_columns)]))
    )
    near0 = [column0] + gather_plane(column0, (1, 2, 3))
    cot_column = across_planes(cot_low)
    pieces0, cot_column = lax.optimization_barrier((gather_chip(near0), cot_column))
    column1 = plane_parts(later)
    q, k, v, stat, o, y, z, slots, gains = staged(
        forward_first, "forward_first", 10,
        (flat_low, flat_low, flat_low, stat_shape, flat_low, flat, logits_shape, slots_shape, shaped((8, width), F32)),
        image_start, (x_in, target_row, order, cosine, signed_sine, mix_rows[0]), pieces0, scratch,
    )
    y0, z0, attention0 = y, z, (stat, q, k, v)
    attended0 = o
    column1, slots = lax.optimization_barrier((column1, slots))
    column1 = jnp.concatenate(column1, 0)
    near1 = gather_plane(column1, (1, 2))

    def weight_specs(layer):
        return [
            pl.BlockSpec((None, None, width, inner), lambda i: (layer, 0, 0, 0)),
            pl.BlockSpec((None, None, width, inner), lambda i: (layer, 0, 0, 0)),
            pl.BlockSpec((None, None, inner, width), lambda i: (layer, 0, 0, 0)),
        ]

    rows0, near1, column1 = lax.optimization_barrier((send(slots).reshape(total_rows, width), near1, column1))
    pieces1 = gather_chip([column1] + near1 + gather_plane(column1, (3,)))
    gate_pre, up_pre, part = pl.pallas_call(
        experts_forward,
        grid=(large_steps,),
        in_specs=[by_blocks(large, width)] + weight_specs(0),
        out_specs=(by_blocks(large, inner), by_blocks(large, inner), by_blocks(large, width)),
        out_shape=(
            shaped((total_rows, inner), F32), shaped((total_rows, inner), F32), shaped((total_rows, width), BF16)
        ),
        compiler_params=params(24 * 1024 * 1024),
        cost_estimate=cost(7),
        name="experts_forward",
    )(rows0, *far(exp_gate, exp_up, exp_down))

    marks, part = lax.optimization_barrier((cot_column, part))
    place = (lax.axis_index("ep") % E).astype(jnp.int32)
    cot_slots = pl.pallas_call(
        spread_kernel,
        in_specs=[whole(pltpu.SMEM), whole()],
        out_shape=shaped((E, holders, CAP, width), BF16),
        compiler_params=params(),
        cost_estimate=cost(4),
        name="spread",
    )(place.reshape(1), marks)
    returned, cot_slots = lax.optimization_barrier((send(part).reshape(holders, SLOTS, width), cot_slots))
    picks0, x1, q, k, v, stat, o, y1, z1, slots, gate_slots = staged(
        forward_second, "forward_second", 11,
        (
            shaped((2, tokens, width), F32), flat, flat_low, flat_low, flat_low, stat_shape, flat_low, flat, logits_shape,
            slots_shape, shaped((holders, SLOTS, 128), BF16),
        ),
        image_start,
        (
            returned, y0, z0, gains, const_value[0], routes_col, target_col, order, cosine, signed_sine, mix_rows[1], carry,
            target_row,
        ),
        pieces1, scratch,
    )
    attention1, attended1 = (stat, q, k, v), o

    cot_back = [lax.ppermute(cot_slots[d], "ep", flipped(d, devices)) for d in range(1, E)]
    rows1, cot_back = lax.optimization_barrier((send(slots).reshape(total_rows, width), cot_back))
    low_inner = shaped((total_rows, inner), BF16)
    low_rows = shaped((total_rows, width), BF16)
    narrow_rows = CAP * width // 128 + 8
    hidden1, da1, db1, du1, cot_rows = pl.pallas_call(
        experts_both,
        grid=(steps,),
        in_specs=[whole(pltpu.SMEM), by_blocks(block, width), pl.BlockSpec((1, 1, CAP, width), lambda i: (0, i, 0, 0))]
        + [pl.BlockSpec((1, CAP, width), lambda i: (i, 0, 0))] * (E - 1)
        + weight_specs(1),
        out_specs=(
            by_blocks(block, inner), by_blocks(block, inner), by_blocks(block, inner),
            pl.BlockSpec((E, narrow_rows, 128), lambda i: (i, 0, 0)), by_blocks(block, width),
        ),
        out_shape=(low_inner, low_inner, low_inner, shaped((devices, narrow_rows, 128), BF16), low_rows),
        compiler_params=params(24 * 1024 * 1024),
        cost_estimate=cost(11),
        name="experts_both",
    )(place.reshape(1), rows1, *far(cot_slots, *cot_back, exp_gate, exp_up, exp_down))

    shares1 = exchange(du1)
    gate_slots, shares1 = lax.optimization_barrier((gate_slots, shares1))
    gate_rows = send(gate_slots)
    packed_low = shaped((tokens, 3 * width), BF16)
    gains_shape = shaped((8, width), F32)
    dx1, normed1, dpacked1, dy1, dgains1, dlogits1, dz0, df_slots = staged(
        backward_second, "backward_second", 16,
        (flat, flat_low, packed_low, flat_low, gains_shape, logits_shape, logits_shape, slots_shape),
        image_start,
        (
            cotangent, y1, z1, gains, routes_col, target_col, const_value[1], shares1, mix_rows[1], carry, z0, order_col,
            *attention1, cosine, signed_sine, x1, target_row,
        ),
        pieces1,
    )
    piece = shaped((width // 8, 4 * width + 128), BF16)
    dlogits0, small = staged(
        mixture_first, "mixture_first", 0.5, (logits_shape, shaped((64, width), F32)),
        image_start, (dx1, y0, z0, gains, routes_col, const_value[0], picks0, dz0, cotangent, y1, z1, dlogits1),
    )
    grads1 = staged(
        projection_grads, "projection_grads", 0.5, (piece,) * 8,
        image_start, (normed1, dpacked1, attended1, dy1, order, dgains1, small),
    )
    total1, low1 = sum_chips(grads1)
    chips1 = sum_plane(low1[:2], (1, 2))

    df_slots, gate_rows = lax.optimization_barrier((df_slots, gate_rows))
    df0 = send(df_slots).reshape(total_rows, width)
    df0, chips1, low1 = lax.optimization_barrier((df0, chips1, low1))
    chips1 += sum_plane(low1[2:], (3,))
    hidden0, da0, db0, du0 = pl.pallas_call(
        experts_backward,
        grid=(steps,),
        in_specs=[by_blocks(block, width), by_blocks(block, inner), by_blocks(block, inner)] + weight_specs(0),
        out_specs=(
            by_blocks(block, inner), by_blocks(block, inner), by_blocks(block, inner), by_blocks(block, width)
        ),
        out_shape=(low_inner, low_inner, low_inner, low_rows),
        compiler_params=params(24 * 1024 * 1024),
        cost_estimate=cost(9),
        name="experts_backward",
    )(df0, *far(gate_pre, up_pre, exp_gate, exp_up, exp_down))
    shares0 = send(du0).reshape(holders, SLOTS, width)

    grad_shapes = (
        shaped((LAYERS, 1, width, inner), F32), shaped((LAYERS, 1, width, inner), F32),
        shaped((LAYERS, 1, inner, width), F32),
    )
    operands = (rows1, hidden1, da1, db1, cot_rows, gate_rows.reshape(total_rows, 128))
    *expert_parts, gated = pl.pallas_call(
        expert_grads_second,
        grid_spec=pl.GridSpec(
            grid=(steps,),
            in_specs=[by_blocks(block, t.shape[1]) for t in operands] + weight_specs(1)[2:],
            out_specs=(
                pl.BlockSpec((1, 1, width, inner), lambda i: (1, 0, 0, 0)),
                pl.BlockSpec((1, 1, width, inner), lambda i: (1, 0, 0, 0)),
                pl.BlockSpec((1, 1, inner, width), lambda i: (1, 0, 0, 0)),
                pl.BlockSpec((E, 1, CAP, width), lambda i: (0, i, 0, 0)),
            ),
        ),
        out_shape=grad_shapes + (shaped((E, holders, CAP, width), BF16),),
        compiler_params=params(),
        cost_estimate=cost(9),
        name="expert_grads_second",
    )(*operands, exp_down)
    chips1, expert_parts = lax.optimization_barrier((chips1, expert_parts))
    reduced1, shares0 = sum_planes(total1, chips1, shares0)
    gated, shares0 = lax.optimization_barrier((gated, shares0))
    gated = in_plane(gated)
    grad_x, *grads0 = staged(
        backward_first, "backward_first", 1, (flat,) + (piece,) * 8,
        image_start,
        (
            dx1, y0, z0, gains, routes_col, target_col, dlogits0, mix_rows[0], shares0, order_col, order, *attention0, cosine,
            signed_sine, x_in, attended0,
        ),
        pieces0,
        [
            pltpu.VMEM((tokens, width), BF16), pltpu.VMEM((tokens, 3 * width), BF16), pltpu.VMEM((tokens, width), BF16),
            pltpu.VMEM((8, width), F32),
        ],
    )
    grads0, gated = lax.optimization_barrier((grads0, gated))
    (total0, low0), gated, mine, hidden0 = lax.optimization_barrier(
        (sum_chips(grads0), gated, reduced1[:, 4 * width :], hidden0)
    )
    chips0 = sum_plane(low0, (1, 2, 3))
    parts = pl.pallas_call(
        combine_kernel,
        grid=(1,),
        in_specs=[
            pl.BlockSpec((E, holders, CAP, width), lambda i: (0, 0, 0, 0)),
            pl.BlockSpec((holders, tokens, 128), lambda i: (0, 0, width // 128)),
        ],
        out_specs=pl.BlockSpec((holders, tokens, width), lambda i: (0, 0, 0)),
        out_shape=shaped((holders, tokens, width), BF16),
        compiler_params=params(),
        cost_estimate=cost(5),
        name="combine",
    )(gated, cot_column)
    parts, hidden0 = lax.optimization_barrier((parts, hidden0))
    operands = (rows0, hidden0, da0, db0, df0)
    expert_parts = pl.pallas_call(
        expert_grads_first,
        grid=(large_steps,),
        in_specs=[by_blocks(large, t.shape[1]) for t in operands] + [whole(pl.ANY)] * 3,
        out_specs=(
            pl.BlockSpec((1, 1, width, inner), lambda i: (0, 0, 0, 0)),
            pl.BlockSpec((1, 1, width, inner), lambda i: (0, 0, 0, 0)),
            pl.BlockSpec((1, 1, inner, width), lambda i: (0, 0, 0, 0)),
        ),
        out_shape=grad_shapes,
        input_output_aliases={5: 0, 6: 1, 7: 2},
        compiler_params=params(),
        cost_estimate=cost(9),
        name="expert_grads_first",
    )(*operands, *expert_parts)
    parts = across_planes(parts)
    mine = jnp.broadcast_to(mine[None], (devices,) + mine.shape)
    mine, parts, chips0 = lax.optimization_barrier((mine, parts, chips0))
    reduced0 = sum_planes(total0, chips0)
    small = exchange(mine).reshape(width, 128)[:, 8:72]
    hidden_out = pl.pallas_call(
        final_kernel,
        out_shape=flat,
        compiler_params=params(),
        cost_estimate=cost(4),
        name="final",
    )(y1, z1, gains, const_value[1], routes_col, parts)

    routers = w_router.shape[-1]
    across = small.T
    both = jnp.stack([across[0:24], across[24:48]])
    reduced = jnp.stack([reduced0, reduced1])
    return (
        hidden_out,
        grad_x,
        reduced[:, :, 4 * width],
        reduced[:, :, : 3 * width],
        reduced[:, :, 3 * width : 4 * width],
        reduced[:, :, 4 * width + 1],
        jnp.stack([small[:, :routers], small[:, 24 : 24 + routers]]),
        across[48 : 48 + routers, :routers],
        both[:, routers:ZW].reshape(LAYERS, NC, 2, width),
        both[:, ZW : ZW + NC],
        *expert_parts,
    )


def solution(mesh):
    in_specs = (
        P("ep", None),
        P("ep", None),
        P(None, "ep"),
        P(None, "ep", None),
        P(None, "ep", None),
        P(None, "ep"),
        P(),
        P(),
        P(),
        P(),
        P(None, "ep", None, None),
        P(None, "ep", None, None),
        P(None, "ep", None, None),
        P(None, "ep", None),
        P("ep", None),
        P("ep"),
    )
    out_specs = (
        P("ep", None),
        P("ep", None),
        P(None, "ep"),
        P(None, "ep", None),
        P(None, "ep", None),
        P(None, "ep"),
        P(),
        P(),
        P(),
        P(),
        P(None, "ep", None, None),
        P(None, "ep", None, None),
        P(None, "ep", None, None),
    )
    return jax.shard_map(shards, mesh=mesh, in_specs=in_specs, out_specs=out_specs, check_vma=False)
```
